32 devices in a mesh: dp: 8 (over z, x), tensor: 4 (over y, core).
Axes of the slice: x: 2, y: 2, z: 4, core: 2. Of those that a mesh axis runs over, the one named last changes fastest.
Arguments:
- text_states: bfloat16 [2, 1024, 4096], P(None, 'dp'), may hold values from -16 to 16, as said below
- image_states: bfloat16 [2, 32, 4096], P(None, 'dp'), may hold values from -81 to 81
- out_grad: bfloat16 [2, 1024, 4096], P(None, 'dp'), may hold values from -6 to 6
- text_lengths: int32 [2], replicated, may hold values from 256 to 1024
- query_weight: bfloat16 [4096, 4096], P('dp', 'tensor'), as said below
- key_weight: bfloat16 [4096, 4096], P('dp', 'tensor'), as said below
- value_weight: bfloat16 [4096, 4096], P('dp', 'tensor'), may hold values from -0.09375 to 0.09375
- out_weight: bfloat16 [4096, 4096], P('tensor', 'dp'), may hold values from -0.09375 to 0.09375
Outputs:
- text_grad: bfloat16 [2, 1024, 4096], P(None, 'dp', 'tensor')
- image_grad: bfloat16 [2, 32, 4096], P(None, 'dp', 'tensor')
- out_weight_grad: bfloat16 [4096, 4096], P('tensor', 'dp')
The draws below stay inside these ranges and needn't reach their ends.
Inputs may be any that keep to these rules, and one draw needn't show every extreme that they name: `text_states`: text states are normal rows with row scales; rows at multiples of 256 have entries within 3. `query_weight`: entries within 8 / sqrt(4096) in magnitude. `key_weight`: entries within 8 / sqrt(4096) in magnitude.
All inputs are finite; a program needn't handle non-finite values.
Results may differ from the reference program's by a relative error of at most 0.019.
The reference program's roundings to bfloat16 on the way count: a program that leaves them out, or rounds other values in their place, can miss the bound.
Values may be sent and summed in bfloat16 or wider, within the bound.
No kernel may reach another device: no remote copies, remote signals or barrier semaphores. Data moves between devices by JAX's collectives and lax.ppermute only.
A program may use at most 128 MiB of HBM per device.

```python
import jax
import jax.numpy as jnp
from jax import lax

D = 4096
HEADS = 32
HEAD_DIM = 128
SAMPLES = 2
TOK_DEV = 128
TEXT = 1024
IMAGE = 32
N_DP = 8
N_TENSOR = 4


def text_base(key):
    key = jax.random.fold_in(key, 901)
    key_values, key_scales = jax.random.split(key)
    values = jnp.clip(jax.random.normal(key_values, (SAMPLES, TEXT, D), jnp.float32), -6.0, 6.0)
    anchor = jnp.arange(TEXT) % (TEXT // 4) == 0
    values = jnp.where(anchor[None, :, None], jnp.clip(values, -3.0, 3.0), values)
    row_scale = jnp.exp(jax.random.uniform(key_scales, (SAMPLES, TEXT), jnp.float32, jnp.log(0.4), jnp.log(2.5)))
    row_scale = jnp.where(anchor[None, :], 1.0, row_scale)
    return values * row_scale[..., None]


def weight_base(key):
    key = jax.random.fold_in(key, 902)
    values = jnp.clip(jax.random.normal(key, (D, D), jnp.float32), -6.0, 6.0)
    return values * D ** (-0.5)


def draw_text_states(key, part):
    return text_base(key).astype(jnp.bfloat16)


def draw_query_weight(key, part):
    return weight_base(key).astype(jnp.bfloat16)


def draw_key_weight(key, part):
    key = jax.random.fold_in(key, 7)
    fresh = jnp.clip(jax.random.normal(key, (D, D), jnp.float32), -6.0, 6.0) * D ** (-0.5)
    result = fresh
    return result.astype(jnp.bfloat16)


def draw_image_states(key, part):
    key = jax.random.fold_in(key, 5)
    key_rest = jax.random.fold_in(key, 0)
    result = jnp.clip(jax.random.normal(key_rest, (SAMPLES, IMAGE, D), jnp.float32), -6.0, 6.0)
    return result.astype(jnp.bfloat16)


def strengthened(values, key, source, target, blocks, factor):
    owner, partner = [(jnp.arange(values.shape[axis_at]) // (values.shape[axis_at] // blocks)).reshape([-1 if axis == axis_at else 1 for axis in range(values.ndim)]) for axis_at in (source, target)]
    chosen = jax.random.permutation(key, blocks)[partner]
    strong = (owner == chosen) | (owner == (partner + blocks // 2) % blocks)
    return jnp.where(strong, factor * values, values)


def steps_of(rng, extent, pieces, least, largest):
    def one(axis_at, blocks):
        draws = jax.random.uniform(jax.random.fold_in(jax.random.fold_in(rng, 6), axis_at), (blocks,), jnp.float32, least / len(pieces), largest / len(pieces))
        return jnp.repeat(jnp.exp(draws), extent[axis_at] // blocks).reshape((-1,) + (1,) * (len(extent) - axis_at - 1))

    loudness = one(*pieces[0])
    for cut in pieces[1:]:
        loudness = loudness * one(*cut)
    return loudness


def scatter_about(own_key, extent, width, most, shards=(), kind=jnp.bfloat16):
    gain = steps_of(own_key, extent, shards, -0.22, 0.18) if shards else 1.0
    drawn = jax.random.normal(own_key, extent, jnp.float32) * width * gain
    return jnp.minimum(jnp.maximum(drawn, -most), most).astype(kind)


def noise_with(stream_key, extent, scale, limit, pieces, heavy, kind=jnp.bfloat16):
    values = scale * jax.random.normal(stream_key, extent, jnp.float32)
    if pieces:
        values = values * steps_of(stream_key, extent, pieces, -0.22, 0.18)
    return jnp.clip(strengthened(values, jax.random.fold_in(stream_key, 3), *heavy), -limit, limit).astype(kind)


def setup_inputs(seed: int = 0) -> dict:
    key_of = jax.random.split(jax.random.key(seed), 9)
    return {
        "text_states": draw_text_states(jax.random.fold_in(key_of[8], 71), 0),
        "image_states": draw_image_states(jax.random.fold_in(key_of[8], 71), 0),
        "out_grad": noise_with(key_of[2], (SAMPLES, TEXT, D), 1.0, 6.0, ((1, 8),), (1, 2, 8, 2.0)),
        "text_lengths": jax.random.randint(key_of[3], (SAMPLES,), TEXT // 4, TEXT + 1).astype(jnp.int32),
        "query_weight": draw_query_weight(jax.random.fold_in(key_of[8], 71), 0),
        "key_weight": draw_key_weight(jax.random.fold_in(key_of[8], 71), 0),
        "value_weight": scatter_about(key_of[6], (D, D), D ** -0.5, 0.09375, ((0, 8), (1, 4))),
        "out_weight": scatter_about(key_of[7], (D, D), D ** -0.5, 0.09375, ((0, 4), (1, 8))),
    }


def softmax_rows(scores):
    peak = jnp.max(scores, axis=-1, keepdims=True)
    expo = jnp.exp(scores - peak)
    return expo / jnp.sum(expo, axis=-1, keepdims=True)


def reference(text_states, image_states, out_grad, text_lengths, query_weight, key_weight, value_weight, out_weight):
    score_scale = HEAD_DIM ** -0.5
    group_cols = D // N_TENSOR

    def groups(weight):
        return weight.reshape(D, N_TENSOR, group_cols).transpose(1, 0, 2)

    wq_groups = groups(query_weight)
    wk_groups = groups(key_weight)
    wv_groups = groups(value_weight)

    def one_sample(carry, items):
        states, image_rows, grad_rows, length = items
        live_rows = jnp.arange(TEXT, dtype=jnp.int32) < length
        live = jnp.where(live_rows[:, None], grad_rows, jnp.zeros_like(grad_rows))
        queries = jnp.dot(states, query_weight, preferred_element_type=jnp.float32).astype(jnp.bfloat16)
        keys_all = jnp.dot(image_rows, key_weight, preferred_element_type=jnp.float32).astype(jnp.bfloat16)
        values_all = jnp.dot(image_rows, value_weight, preferred_element_type=jnp.float32).astype(jnp.bfloat16)
        query_heads = queries.reshape(TEXT, HEADS, HEAD_DIM).astype(jnp.float32)
        key_heads = keys_all.reshape(IMAGE, HEADS, HEAD_DIM).astype(jnp.float32)
        value_heads = values_all.reshape(IMAGE, HEADS, HEAD_DIM).astype(jnp.float32)
        scores = jnp.einsum('thd,jhd->htj', query_heads, key_heads) * score_scale
        soft_prob = softmax_rows(scores)
        prob_low = soft_prob.astype(jnp.bfloat16).astype(jnp.float32)
        attended = jnp.einsum('htj,jhd->thd', prob_low, value_heads).astype(jnp.bfloat16).reshape(TEXT, D)
        attended_grad = jnp.dot(live, out_weight.T, preferred_element_type=jnp.float32).astype(jnp.bfloat16)
        grad_heads = attended_grad.reshape(TEXT, HEADS, HEAD_DIM).astype(jnp.float32)
        value_grad = jnp.einsum('htj,thd->jhd', prob_low, grad_heads).astype(jnp.bfloat16)
        prob_grad = jnp.einsum('thd,jhd->htj', grad_heads, value_heads)
        row_delta = jnp.sum(soft_prob * prob_grad, axis=-1, keepdims=True)
        score_grad = (soft_prob * (prob_grad - row_delta) * score_scale).astype(jnp.bfloat16).astype(jnp.float32)
        query_grad = jnp.einsum('htj,jhd->thd', score_grad, key_heads).astype(jnp.bfloat16)
        key_grad = jnp.einsum('htj,thd->jhd', score_grad, query_heads).astype(jnp.bfloat16)
        query_groups = query_grad.reshape(TEXT, N_TENSOR, group_cols).transpose(1, 0, 2)
        key_groups = key_grad.reshape(IMAGE, N_TENSOR, group_cols).transpose(1, 0, 2)
        value_groups = value_grad.reshape(IMAGE, N_TENSOR, group_cols).transpose(1, 0, 2)

        def group_term(sums, parts):
            q_part, k_part, v_part, wq_part, wk_part, wv_part = parts
            text_term = jnp.dot(q_part, wq_part.T, preferred_element_type=jnp.float32).astype(jnp.bfloat16)
            image_term = jnp.dot(k_part, wk_part.T, preferred_element_type=jnp.float32)
            image_term = (image_term + jnp.dot(v_part, wv_part.T, preferred_element_type=jnp.float32)).astype(jnp.bfloat16)
            return (sums[0] + text_term.astype(jnp.float32), sums[1] + image_term.astype(jnp.float32)), None

        zero_text = jnp.zeros((TEXT, D), jnp.float32)
        zero_image = jnp.zeros((IMAGE, D), jnp.float32)
        (text_sum, image_sum), _ = lax.scan(group_term, (zero_text, zero_image), (query_groups, key_groups, value_groups, wq_groups, wk_groups, wv_groups))
        return carry, (text_sum.astype(jnp.bfloat16), image_sum.astype(jnp.bfloat16), attended, live)

    _, results = lax.scan(one_sample, jnp.zeros((), jnp.float32), (text_states, image_states, out_grad, text_lengths))
    text_grad, image_grad, attended_all, live_all = results

    def blocks(array):
        return array.reshape(SAMPLES, N_DP, TOK_DEV, D).transpose(1, 0, 2, 3).reshape(N_DP, SAMPLES * TOK_DEV, D)

    def block_term(total, parts):
        attended_block, live_block = parts
        term = jnp.dot(attended_block.T, live_block, preferred_element_type=jnp.float32).astype(jnp.bfloat16)
        return total + term.astype(jnp.float32), None

    total, _ = lax.scan(block_term, jnp.zeros((D, D), jnp.float32), (blocks(attended_all), blocks(live_all)))
    return text_grad, image_grad, total.astype(jnp.bfloat16)
```

```python
import jax
import jax.numpy as jnp
from jax import lax
from jax.sharding import PartitionSpec as P

HEAD_DIM = 128
F32 = jnp.float32
BF16 = jnp.bfloat16
BACK = (((1,), (1,)), ((), ()))


def softmax_rows(scores):
    peak = jnp.max(scores, axis=-1, keepdims=True)
    expo = jnp.exp(scores - peak)
    return expo / jnp.sum(expo, axis=-1, keepdims=True)


def low(values):
    return lax.reduce_precision(values, 8, 7)


def shards(
    text_states,
    image_states,
    out_grad,
    text_lengths,
    query_weight,
    key_weight,
    value_weight,
    out_weight,
):
    score_scale = HEAD_DIM ** (-0.5)
    samples, tok_rows, width = text_states.shape
    image_own = image_states.shape[1]
    n_dp = lax.axis_size("dp")
    n_tensor = lax.axis_size("tensor")
    rows = samples * tok_rows
    image_rows = samples * image_own
    local_cols = query_weight.shape[1]
    own_width = query_weight.shape[0]
    head_count = local_cols // HEAD_DIM
    image_count = n_dp * image_own

    wq_full = lax.all_gather(query_weight, "dp", axis=0, tiled=True)
    wo_full = lax.all_gather(out_weight, "dp", axis=1, tiled=True)

    first_row = lax.axis_index("dp") * tok_rows
    positions = first_row + lax.iota(jnp.int32, tok_rows)
    live_rows = positions[None, :] < text_lengths[:, None]
    grad_live = jnp.where(live_rows[..., None], out_grad, jnp.zeros_like(out_grad))
    text_flat = text_states.reshape(rows, width)
    live_flat = grad_live.reshape(rows, width)

    image_flat = image_states.reshape(image_rows, width)
    image_cols = lax.all_to_all(image_flat, "dp", split_axis=1, concat_axis=0, tiled=True)
    part_kv = jnp.concatenate(
        [
            jnp.dot(image_cols, key_weight, preferred_element_type=F32),
            jnp.dot(image_cols, value_weight, preferred_element_type=F32),
        ],
        axis=1,
    )
    part_kv = part_kv.reshape(n_dp, image_rows, 2 * local_cols)
    kv_own = jnp.sum(lax.all_to_all(part_kv, "dp", split_axis=0, concat_axis=0), axis=0)
    kv_all = lax.all_gather(kv_own.astype(BF16), "dp", axis=0)
    kv_all = kv_all.reshape(n_dp, samples, image_own, 2, head_count, HEAD_DIM)
    kv_all = kv_all.transpose(3, 1, 0, 2, 4, 5).reshape(
        2, samples, image_count, head_count, HEAD_DIM
    )
    key_heads, value_heads = kv_all[0], kv_all[1]

    queries = jnp.dot(text_flat, wq_full, preferred_element_type=F32).astype(BF16)
    query_heads = queries.reshape(samples, tok_rows, head_count, HEAD_DIM)
    scores = (
        jnp.einsum("sthd,sjhd->shtj", query_heads, key_heads, preferred_element_type=F32)
        * score_scale
    )
    soft_prob = softmax_rows(scores)
    prob_low = soft_prob.astype(BF16)
    attended = jnp.einsum("shtj,sjhd->sthd", prob_low, value_heads, preferred_element_type=F32)
    attended = attended.astype(BF16).reshape(rows, local_cols)

    live_cols = lax.all_to_all(live_flat, "dp", split_axis=1, concat_axis=0, tiled=True)
    live_cols = live_cols.reshape(n_dp, rows, own_width)
    attended_all = lax.all_gather(attended, "dp", axis=0)
    partial = lax.dot_general(
        attended_all, live_cols, (((1,), (1,)), ((0,), (0,))), preferred_element_type=F32
    )
    weight_grad = jnp.sum(low(partial), axis=0).astype(BF16)

    attended_grad = lax.dot_general(live_flat, wo_full, BACK, preferred_element_type=F32)
    grad_heads = attended_grad.astype(BF16).reshape(samples, tok_rows, head_count, HEAD_DIM)
    value_part = jnp.einsum("shtj,sthd->sjhd", prob_low, grad_heads, preferred_element_type=F32)
    prob_grad = jnp.einsum(
        "sthd,sjhd->shtj", grad_heads, value_heads, preferred_element_type=F32
    )
    row_delta = jnp.sum(soft_prob * prob_grad, axis=-1, keepdims=True)
    score_grad = (soft_prob * (prob_grad - row_delta) * score_scale).astype(BF16)
    query_grad = jnp.einsum(
        "shtj,sjhd->sthd", score_grad, key_heads, preferred_element_type=F32
    ).astype(BF16)
    key_part = jnp.einsum("shtj,sthd->sjhd", score_grad, query_heads, preferred_element_type=F32)

    query_grad = query_grad.reshape(rows, local_cols)
    text_term = lax.dot_general(query_grad, wq_full, BACK, preferred_element_type=F32)
    text_term = text_term.astype(BF16)
    text_parts = lax.all_to_all(
        text_term.reshape(rows, n_tensor, width // n_tensor), "tensor", split_axis=1, concat_axis=0
    )
    text_grad = jnp.sum(text_parts.astype(F32), axis=0).astype(BF16)
    text_grad = text_grad.reshape(samples, tok_rows, width // n_tensor)

    kv_part = jnp.stack([key_part, value_part], axis=2)
    kv_part = kv_part.reshape(samples, n_dp, image_own, 2 * local_cols).transpose(1, 0, 2, 3)
    kv_part = kv_part.reshape(n_dp, image_rows, 2 * local_cols)
    kv_grad = jnp.sum(lax.all_to_all(kv_part, "dp", split_axis=0, concat_axis=0), axis=0)
    kv_grad_all = lax.all_gather(kv_grad.astype(BF16), "dp", axis=0, tiled=True)
    key_low, value_low = kv_grad_all[:, :local_cols], kv_grad_all[:, local_cols:]
    image_term = lax.dot_general(key_low, key_weight, BACK, preferred_element_type=F32)
    image_term = image_term + lax.dot_general(
        value_low, value_weight, BACK, preferred_element_type=F32
    )
    image_term = lax.all_to_all(
        image_term.astype(BF16), "dp", split_axis=0, concat_axis=1, tiled=True
    )
    image_parts = lax.all_to_all(
        image_term.reshape(image_rows, n_tensor, width // n_tensor),
        "tensor",
        split_axis=1,
        concat_axis=0,
    )
    image_grad = jnp.sum(image_parts.astype(F32), axis=0).astype(BF16)
    image_grad = image_grad.reshape(samples, image_own, width // n_tensor)
    return text_grad, image_grad, weight_grad


def solution(mesh):
    return jax.shard_map(
        shards,
        mesh=mesh,
        in_specs=(
            P(None, "dp", None),
            P(None, "dp", None),
            P(None, "dp", None),
            P(),
            P("dp", "tensor"),
            P("dp", "tensor"),
            P("dp", "tensor"),
            P("tensor", "dp"),
        ),
        out_specs=(P(None, "dp", "tensor"), P(None, "dp", "tensor"), P("tensor", "dp")),
        check_vma=False,
    )
```

```python
import jax
import jax.numpy as jnp
from jax import lax
from jax.sharding import PartitionSpec as P

HEAD_DIM = 128
F32 = jnp.float32
BF16 = jnp.bfloat16
BACK = (((1,), (1,)), ((), ()))


def softmax_rows(scores):
    peak = jnp.max(scores, axis=-1, keepdims=True)
    expo = jnp.exp(scores - peak)
    return expo / jnp.sum(expo, axis=-1, keepdims=True)


def low(values):
    return lax.reduce_precision(values, 8, 7)


def after(values, *others):
    return lax.optimization_barrier((values, *others))[0]


class Line:
    def __init__(self):
        self.n_dp = lax.axis_size("dp")
        self.n_z = self.n_dp // 2
        self.place = lax.axis_index("dp")
        self.z = self.place // 2
        self.x = self.place % 2

    def move(self, block, moves):
        pairs = [(2 * a + e, 2 * b + e) for a, b in moves for e in range(2)]
        return lax.ppermute(block, "dp", pairs)

    def swap(self, block, planes=None):
        planes = range(self.n_z) if planes is None else planes
        pairs = [(2 * a + e, 2 * a + 1 - e) for a in planes for e in range(2)]
        return lax.ppermute(block, "dp", pairs)

    def along(self, block):
        n = self.n_z
        if n != 4:
            shifted = [self.move(block, [((a + m) % n, a) for a in range(n)]) for m in range(1, n)]
            return [(block, None)] + [(values, None) for values in shifted]
        above = self.move(block, [(1, 0), (2, 1), (3, 2)])
        below = self.move(block, [(0, 1), (1, 2), (2, 3)])
        across = self.move(block, [(0, 2), (1, 3), (2, 0), (3, 1)])
        edge = self.move(across, [(1, 0), (2, 3)])
        return [
            (block, None),
            (above, (0, 1, 2)),
            (across, None),
            (below, (1, 2, 3)),
            (edge, (0, 3)),
        ]

    def pick(self, raw):
        if self.n_z != 4:
            return raw
        own, above, across, below, edge = raw
        return [
            own,
            jnp.where(self.z == 3, edge, above),
            across,
            jnp.where(self.z == 0, edge, below),
        ]

    def rolled(self, values, axis):
        doubled = jnp.concatenate([values, values], axis=axis)
        return lax.dynamic_slice_in_dim(doubled, self.z, self.n_z, axis)

    def unrolled(self, values, axis):
        doubled = jnp.concatenate([values, values], axis=axis)
        start = lax.rem(self.n_z - self.z, self.n_z)
        return lax.dynamic_slice_in_dim(doubled, start, self.n_z, axis)

    def own_first(self, values, axis):
        return jnp.where(self.x == 0, values, jnp.flip(values, axis))


def shards(
    text_states,
    image_states,
    out_grad,
    text_lengths,
    query_weight,
    key_weight,
    value_weight,
    out_weight,
):
    score_scale = HEAD_DIM ** (-0.5)
    samples, tok_rows, width = text_states.shape
    image_own = image_states.shape[1]
    line = Line()
    n_dp, n_z = line.n_dp, line.n_z
    n_tensor = lax.axis_size("tensor")
    core = lax.axis_index("tensor") % 2
    rows = samples * tok_rows
    image_rows = samples * image_own
    local_cols = query_weight.shape[1]
    own_width = query_weight.shape[0]
    head_count = local_cols // HEAD_DIM
    image_count = n_dp * image_own
    half_cols = local_cols // 2

    def core_swap(block):
        return lax.ppermute(block, "tensor", [(t, t ^ 1) for t in range(n_tensor)])

    first_row = lax.axis_index("dp") * tok_rows
    positions = first_row + lax.iota(jnp.int32, tok_rows)
    live_rows = positions[None, :] < text_lengths[:, None]
    grad_live = jnp.where(live_rows[..., None], out_grad, jnp.zeros_like(out_grad))
    text_flat = text_states.reshape(rows, width)
    live_flat = grad_live.reshape(rows, width)

    wq_raw = line.along(query_weight)
    wq_other = [line.swap(values, planes) for values, planes in wq_raw]
    wq_slots = list(zip(line.pick([values for values, _ in wq_raw]), line.pick(wq_other)))

    wo_keep = lax.dynamic_slice_in_dim(out_weight, line.x * half_cols, half_cols, 0)
    wo_send = lax.dynamic_slice_in_dim(out_weight, (1 - line.x) * half_cols, half_cols, 0)
    wo_pair = jnp.concatenate([wo_keep, line.swap(wo_send)], axis=1)
    wo_pair = after(wo_pair, wq_raw[2][0])
    wo_raw = line.along(wo_pair)
    wo_slots = line.pick([values for values, _ in wo_raw])

    live_half = lax.dynamic_slice_in_dim(live_flat, core * (width // 2), width // 2, 1)
    half_here = line.swap(live_half)
    half_there = core_swap(half_here)
    live_other = jnp.where(
        core == 0,
        jnp.concatenate([half_here, half_there], axis=1),
        jnp.concatenate([half_there, half_here], axis=1),
    )

    image_flat = image_states.reshape(image_rows, width)
    image_cols = lax.all_to_all(image_flat, "dp", split_axis=1, concat_axis=0, tiled=True)
    part_kv = jnp.concatenate(
        [
            jnp.dot(image_cols, key_weight, preferred_element_type=F32),
            jnp.dot(image_cols, value_weight, preferred_element_type=F32),
        ],
        axis=1,
    )
    part_kv = part_kv.reshape(n_dp, image_rows, 2 * local_cols)
    kv_own = jnp.sum(lax.all_to_all(part_kv, "dp", split_axis=0, concat_axis=0), axis=0)

    def everywhere(values):
        copies = jnp.broadcast_to(values[None], (n_dp, *values.shape))
        return lax.all_to_all(copies, "dp", split_axis=0, concat_axis=0)

    kv_all = everywhere(kv_own.astype(BF16))
    kv_all = kv_all.reshape(n_dp, samples, image_own, 2, head_count, HEAD_DIM)
    kv_all = kv_all.transpose(3, 1, 0, 2, 4, 5).reshape(
        2, samples, image_count, head_count, HEAD_DIM
    )
    key_heads, value_heads = kv_all[0], kv_all[1]

    def relative(values):
        cut = values.reshape(values.shape[0], n_z, 2, own_width)
        return line.own_first(line.rolled(cut, 1), 2)

    text_rel = relative(text_flat)
    queries = 0.0
    for m in range(n_z):
        for e in range(2):
            queries += jnp.dot(text_rel[:, m, e], wq_slots[m][e], preferred_element_type=F32)
    queries = queries.astype(BF16)
    query_heads = queries.reshape(samples, tok_rows, head_count, HEAD_DIM)
    scores = (
        jnp.einsum("sthd,sjhd->shtj", query_heads, key_heads, preferred_element_type=F32)
        * score_scale
    )
    soft_prob = softmax_rows(scores)
    prob_low = soft_prob.astype(BF16)
    attended = jnp.einsum("shtj,sjhd->sthd", prob_low, value_heads, preferred_element_type=F32)
    attended = attended.astype(BF16).reshape(rows, local_cols)

    half_rows = rows // 2
    own_half = lax.dynamic_slice_in_dim(live_flat, core * half_rows, half_rows, 0)
    own_half = after(own_half, wo_raw[2][0])
    cols_here = lax.all_to_all(
        own_half.reshape(half_rows, n_dp, own_width), "dp", split_axis=1, concat_axis=0
    )
    cols_here = cols_here.reshape(n_dp, half_rows, own_width)
    live_cols = jnp.concatenate([cols_here, core_swap(cols_here)], axis=1)
    live_cols = live_cols.reshape(n_z, 2, rows, own_width)
    live_cols = line.own_first(line.rolled(live_cols, 0), 1).reshape(n_dp, rows, own_width)
    attended_rel = attended.reshape(2, half_rows, local_cols)
    attended_rel = jnp.where(core == 0, attended_rel, jnp.flip(attended_rel, 0))
    att_raw = line.along(attended_rel.reshape(rows, local_cols))
    att_other = [line.swap(values, planes) for values, planes in att_raw]
    att_slots = zip(line.pick([values for values, _ in att_raw]), line.pick(att_other))
    attended_all = jnp.stack([values for pair in att_slots for values in pair])
    partial = lax.dot_general(
        attended_all, live_cols, (((1,), (1,)), ((0,), (0,))), preferred_element_type=F32
    )
    weight_grad = jnp.sum(low(partial), axis=0).astype(BF16)

    live_rel = relative(jnp.concatenate([live_flat, live_other], axis=0))
    half_grad = 0.0
    for m in range(n_z):
        half_grad += lax.dot_general(
            live_rel[:, m].reshape(2 * rows, 2 * own_width),
            wo_slots[m],
            BACK,
            preferred_element_type=F32,
        )
    half_grad = half_grad.astype(BF16)
    grad_keep, grad_send = half_grad[:rows], half_grad[rows:]
    grad_come = line.swap(grad_send)
    attended_grad = jnp.where(
        line.x == 0,
        jnp.concatenate([grad_keep, grad_come], axis=1),
        jnp.concatenate([grad_come, grad_keep], axis=1),
    )
    grad_heads = attended_grad.reshape(samples, tok_rows, head_count, HEAD_DIM)
    value_part = jnp.einsum("shtj,sthd->sjhd", prob_low, grad_heads, preferred_element_type=F32)
    prob_grad = jnp.einsum(
        "sthd,sjhd->shtj", grad_heads, value_heads, preferred_element_type=F32
    )
    row_delta = jnp.sum(soft_prob * prob_grad, axis=-1, keepdims=True)
    score_grad = (soft_prob * (prob_grad - row_delta) * score_scale).astype(BF16)
    query_grad = jnp.einsum(
        "shtj,sjhd->sthd", score_grad, key_heads, preferred_element_type=F32
    ).astype(BF16)
    key_part = jnp.einsum("shtj,sthd->sjhd", score_grad, query_heads, preferred_element_type=F32)

    query_grad = query_grad.reshape(rows, local_cols)
    terms = [
        jnp.stack(
            [
                lax.dot_general(
                    query_grad, wq_slots[m][e], BACK, preferred_element_type=F32
                ).astype(BF16)
                for e in range(2)
            ],
            axis=1,
        )
        for m in range(n_z)
    ]
    text_term = line.unrolled(line.own_first(jnp.stack(terms, axis=1), 2), 1)
    text_parts = lax.all_to_all(
        text_term.reshape(rows, n_tensor, width // n_tensor), "tensor", split_axis=1, concat_axis=0
    )
    text_grad = jnp.sum(text_parts.astype(F32), axis=0).astype(BF16)
    text_grad = text_grad.reshape(samples, tok_rows, width // n_tensor)

    kv_part = jnp.stack([key_part, value_part], axis=2)
    kv_part = kv_part.reshape(samples, n_dp, image_own, 2 * local_cols).transpose(1, 0, 2, 3)
    kv_part = kv_part.reshape(n_dp, image_rows, 2 * local_cols)
    kv_grad = jnp.sum(lax.all_to_all(kv_part, "dp", split_axis=0, concat_axis=0), axis=0)
    kv_grad_all = everywhere(kv_grad.astype(BF16)).reshape(n_dp * image_rows, 2 * local_cols)
    key_low, value_low = kv_grad_all[:, :local_cols], kv_grad_all[:, local_cols:]
    image_term = lax.dot_general(key_low, key_weight, BACK, preferred_element_type=F32)
    image_term = image_term + lax.dot_general(
        value_low, value_weight, BACK, preferred_element_type=F32
    )
    image_term = lax.all_to_all(
        image_term.astype(BF16), "dp", split_axis=0, concat_axis=1, tiled=True
    )
    image_parts = lax.all_to_all(
        image_term.reshape(image_rows, n_tensor, width // n_tensor),
        "tensor",
        split_axis=1,
        concat_axis=0,
    )
    image_grad = jnp.sum(image_parts.astype(F32), axis=0).astype(BF16)
    image_grad = image_grad.reshape(samples, image_own, width // n_tensor)
    return text_grad, image_grad, weight_grad


def solution(mesh):
    return jax.shard_map(
        shards,
        mesh=mesh,
        in_specs=(
            P(None, "dp", None),
            P(None, "dp", None),
            P(None, "dp", None),
            P(),
            P("dp", "tensor"),
            P("dp", "tensor"),
            P("dp", "tensor"),
            P("tensor", "dp"),
        ),
        out_specs=(P(None, "dp", "tensor"), P(None, "dp", "tensor"), P("tensor", "dp")),
        check_vma=False,
    )
```

```python
import functools

import jax
import jax.numpy as jnp
from jax import lax
from jax.experimental import pallas as pl
from jax.experimental.pallas import tpu as pltpu
from jax.sharding import PartitionSpec as P

HEAD_DIM = 128
F32 = jnp.float32
BF16 = jnp.bfloat16
BACK = (((1,), (1,)), ((), ()))
FIRST = (((0,), (0,)), ((), ()))
VMEM_LIMIT = 48 * 1024 * 1024


def after(values, *others):
    return lax.optimization_barrier((values, *others))[0]


def matmul(a, b, dims=None):
    if dims is None:
        return jnp.dot(a, b, preferred_element_type=F32)
    return lax.dot_general(a, b, dims, preferred_element_type=F32)


class Line:
    def __init__(self):
        self.n_dp = lax.axis_size("dp")
        self.n_z = self.n_dp // 2

    def move(self, block, moves):
        pairs = [(2 * a + e, 2 * b + e) for a, b in moves for e in range(2)]
        return lax.ppermute(block, "dp", pairs)

    def swap(self, block, planes=None):
        planes = range(self.n_z) if planes is None else planes
        pairs = [(2 * a + e, 2 * a + 1 - e) for a in planes for e in range(2)]
        return lax.ppermute(block, "dp", pairs)

    def along(self, block):
        n = self.n_z
        if n != 4:
            return [self.move(block, [((a + m) % n, a) for a in range(n)]) for m in range(1, n)]
        above = self.move(block, [(1, 0), (2, 1), (3, 2)])
        below = self.move(block, [(0, 1), (1, 2), (2, 3)])
        across = self.move(block, [(0, 2), (1, 3), (2, 0), (3, 1)])
        return [above, across, below]

    def relay(self, moved):
        return [self.move(moved[1], [(1, 0), (2, 3)])] if self.n_z == 4 else []

    def swap_moved(self, moved):
        if self.n_z != 4:
            return [self.swap(block) for block in moved]
        planes = ((0, 1, 2), None, (1, 2, 3))
        return [self.swap(block, at) for block, at in zip(moved, planes)]

    def swap_relayed(self, relayed):
        return [self.swap(block, (0, 3)) for block in relayed]

    def slots(self, z):
        if self.n_z != 4:
            return [(m, None) for m in range(self.n_z)]
        return [
            (0, None),
            (1, z < 3),
            (2, None),
            (3, z > 0),
            (jnp.where(z == 3, 1, 3), (z == 3) | (z == 0)),
        ]


def each_block(line, place, body):
    z, x = place[0], place[1]
    for i, (m, came) in enumerate(line.slots(z)):
        plane = lax.rem(z + m, line.n_z)
        for e in range(2):
            index = 2 * plane + (x if e == 0 else 1 - x)
            if came is None:
                body(i, e, index)
            else:
                pl.when(came)(functools.partial(body, i, e, index))


def columns(index, size):
    return pl.ds(pl.multiple_of(index * size, size), size)


def probabilities(query, key, image_own):
    scores = matmul(key, query, BACK) * HEAD_DIM ** (-0.5)
    image = lax.broadcasted_iota(jnp.int32, scores.shape, 0)
    token = lax.broadcasted_iota(jnp.int32, scores.shape, 1)
    image_sample = lax.rem(lax.div(image, image_own), 2)
    same = image_sample == lax.div(token, scores.shape[1] // 2)
    scores = jnp.where(same, scores, -1e30)
    peak = jnp.max(scores, axis=0, keepdims=True)
    expo = jnp.where(same, jnp.exp(scores - peak), 0.0)
    return expo / jnp.sum(expo, axis=0, keepdims=True)


def forward_kernel(line, image_own, place, text, kv, *refs):
    n = (len(refs) - 3) // 2
    weights, (query_out, attended_out, total) = (refs[:n], refs[n : 2 * n]), refs[2 * n :]
    own_width = weights[0][0].shape[0]
    rows, cols = total.shape
    total[...] = jnp.zeros_like(total)

    def add(i, e, index):
        total[...] += matmul(text[:, columns(index, own_width)], weights[e][i][...])

    each_block(line, place, add)
    query_out[...] = total[...].astype(BF16)
    part = rows // 4
    quarter = place[2]
    for h in range(cols // HEAD_DIM):
        at = slice(h * HEAD_DIM, (h + 1) * HEAD_DIM)
        value = kv[:, cols + h * HEAD_DIM : cols + (h + 1) * HEAD_DIM]
        prob = probabilities(query_out[:, at], kv[:, at], image_own)
        attended = matmul(prob.astype(BF16), value, FIRST).astype(BF16)
        for r in range(4):
            low_bit = (quarter + r) % 2
            high_bit = (quarter // 2 + r // 2) % 2
            start = pl.multiple_of((2 * low_bit + high_bit) * part, part)
            attended_out[pl.ds(start, part), at] = attended[r * part : (r + 1) * part]


def grad_kernel(line, place, live, here, there, *refs):
    weights, (keep_out, send_out, keep, send) = refs[:-4], refs[-4:]
    own_width = weights[0].shape[1] // 2
    half = line.n_dp // 2
    core = place[2] % 2
    keep[...] = jnp.zeros_like(keep)
    send[...] = jnp.zeros_like(send)

    def add(i, e, index):
        weight = weights[i][:, e * own_width : (e + 1) * own_width]
        keep[...] += matmul(live[:, columns(index, own_width)], weight, BACK)
        inner = columns(lax.rem(index, half), own_width)
        other = jnp.where(lax.div(index, half) == core, here[:, inner], there[:, inner])
        send[...] += matmul(other, weight, BACK)

    each_block(line, place, add)
    keep_out[...] = keep[...].astype(BF16)
    send_out[...] = send[...].astype(BF16)


def backward_kernel(image_own, place, query, kv, keep, come, query_grad, kv_grad):
    cols = query.shape[1]
    half = cols // 2
    x = place[1]
    for h in range(cols // HEAD_DIM):
        at = slice(h * HEAD_DIM, (h + 1) * HEAD_DIM)
        value_at = slice(cols + h * HEAD_DIM, cols + (h + 1) * HEAD_DIM)
        side = h * HEAD_DIM // half
        inner = slice(h * HEAD_DIM - side * half, (h + 1) * HEAD_DIM - side * half)
        grad = jnp.where(x == side, keep[:, inner], come[:, inner])
        prob = probabilities(query[:, at], kv[:, at], image_own)
        kv_grad[:, value_at] = matmul(prob.astype(BF16), grad)
        prob_grad = matmul(kv[:, value_at], grad, BACK)
        delta = jnp.sum(prob * prob_grad, axis=0, keepdims=True)
        score_grad = (prob * (prob_grad - delta) * HEAD_DIM ** (-0.5)).astype(BF16)
        kv_grad[:, at] = matmul(score_grad, query[:, at])
        query_grad[:, at] = matmul(score_grad, kv[:, at], FIRST).astype(BF16)


def term_kernel(line, place, query_grad, *refs):
    n = (len(refs) - 1) // 2
    weights, out = (refs[:n], refs[n : 2 * n]), refs[-1]

    def write(i, e, index):
        out[index] = matmul(query_grad[...], weights[e][i][...], BACK).astype(BF16)

    each_block(line, place, write)


def weight_grad_kernel(line, place, *refs):
    live, refs = refs[:4], refs[4:]
    n = (len(refs) - 2) // 2
    attended, (out, total) = (refs[:n], refs[n : 2 * n]), refs[2 * n :]
    total[...] = jnp.zeros_like(total)

    def add(i, e, index):
        block = jnp.concatenate([part[index] for part in live], axis=0)
        term = matmul(attended[e][i][...], block, FIRST)
        total[...] += term.astype(BF16).astype(F32)

    each_block(line, place, add)
    out[...] = total[...].astype(BF16)


def call(kernel, place, operands, outs, scratch=(), flops=0):
    moved = sum(a.size * a.dtype.itemsize for a in (*operands, *outs))
    single = len(outs) == 1
    return pl.pallas_call(
        kernel,
        out_shape=outs[0] if single else outs,
        in_specs=[pl.BlockSpec(memory_space=pltpu.SMEM)]
        + [pl.BlockSpec(memory_space=pltpu.VMEM)] * len(operands),
        out_specs=pl.BlockSpec(memory_space=pltpu.VMEM)
        if single
        else [pl.BlockSpec(memory_space=pltpu.VMEM)] * len(outs),
        scratch_shapes=list(scratch),
        compiler_params=pltpu.CompilerParams(vmem_limit_bytes=VMEM_LIMIT),
        cost_estimate=pl.CostEstimate(flops=flops, bytes_accessed=moved, transcendentals=0),
    )(place, *operands)


def shards(
    text_states,
    image_states,
    out_grad,
    text_lengths,
    query_weight,
    key_weight,
    value_weight,
    out_weight,
):
    samples, tok_rows, width = text_states.shape
    image_own = image_states.shape[1]
    line = Line()
    n_dp = line.n_dp
    n_tensor = lax.axis_size("tensor")
    dp_at, tensor_at = lax.axis_index("dp"), lax.axis_index("tensor")
    x, core = dp_at % 2, tensor_at % 2
    place = jnp.stack([dp_at // 2, x, tensor_at % 4]).astype(jnp.int32)
    rows = samples * tok_rows
    image_rows = samples * image_own
    images = n_dp * image_rows
    local_cols = query_weight.shape[1]
    own_width = query_weight.shape[0]
    half_cols = local_cols // 2
    shape = jax.ShapeDtypeStruct

    def tensor_swap(block, bit):
        return lax.ppermute(block, "tensor", [(t, t ^ bit) for t in range(n_tensor)])

    positions = dp_at * tok_rows + lax.iota(jnp.int32, tok_rows)
    live_rows = positions[None, :] < text_lengths[:, None]
    grad_live = jnp.where(live_rows[..., None], out_grad, jnp.zeros_like(out_grad))
    text_flat = text_states.reshape(rows, width)
    live_flat = grad_live.reshape(rows, width)
    image_flat = image_states.reshape(image_rows, width)

    wq_moved = line.along(query_weight)
    wq_swapped = line.swap(query_weight)
    wo_keep = lax.dynamic_slice_in_dim(out_weight, x * half_cols, half_cols, 0)
    wo_send = lax.dynamic_slice_in_dim(out_weight, (1 - x) * half_cols, half_cols, 0)
    wo_come = line.swap(wo_send)
    live_half = lax.dynamic_slice_in_dim(live_flat, core * (width // 2), width // 2, 1)
    live_here = line.swap(live_half)
    image_cols = lax.all_to_all(image_flat, "dp", split_axis=1, concat_axis=0, tiled=True)
    first = (*wq_moved, wq_swapped, wo_come, live_here, image_cols)

    wo_pair = after(jnp.concatenate([wo_keep, wo_come], axis=1), *first)
    wo_moved = line.along(wo_pair)
    wq_gated = lax.optimization_barrier((*wq_moved, *first))[: len(wq_moved)]
    wq_relayed = line.relay(wq_gated)
    wq_others = line.swap_moved(wq_gated)
    live_there = tensor_swap(after(live_here, *first), 1)

    image_cols = after(image_cols, *first)
    part_kv = jnp.concatenate(
        [matmul(image_cols, key_weight), matmul(image_cols, value_weight)], axis=1
    )
    part_kv = part_kv.reshape(n_dp, image_rows, 2 * local_cols)
    kv_own = jnp.sum(lax.all_to_all(part_kv, "dp", split_axis=0, concat_axis=0), axis=0)
    second = (*wo_moved, *wq_relayed, *wq_others, live_there, kv_own)

    def everywhere(values):
        copies = jnp.broadcast_to(values[None], (n_dp, *values.shape))
        return lax.all_to_all(copies, "dp", split_axis=0, concat_axis=0)

    gated = lax.optimization_barrier((*wo_moved, *wq_relayed, kv_own, *second))
    wo_gated, wq_last = gated[: len(wo_moved)], gated[len(wo_moved) :][: len(wq_relayed)]
    kv_gated = gated[len(wo_moved) + len(wq_relayed)]
    wo_relayed = line.relay(wo_gated)
    wq_last_other = line.swap_relayed(wq_last)
    kv_all = everywhere(kv_gated.astype(BF16)).reshape(images, 2 * local_cols)
    quarter_rows = rows // 4
    live_part = lax.dynamic_slice_in_dim(
        live_flat, (tensor_at % 4) * quarter_rows, quarter_rows, 0
    )
    live_part = after(live_part.reshape(quarter_rows, n_dp, own_width), *second)
    live_mine = lax.all_to_all(live_part, "dp", split_axis=1, concat_axis=0)
    live_mine = live_mine.reshape(n_dp, quarter_rows, own_width)
    live_y = tensor_swap(live_mine, 2)
    live_cols = [live_mine, live_y, tensor_swap(live_mine, 1), tensor_swap(live_y, 1)]

    wq_blocks = [query_weight, *wq_gated, *wq_last, wq_swapped, *wq_others, *wq_last_other]
    queries, attended = call(
        functools.partial(forward_kernel, line, image_own),
        place,
        (text_flat, kv_all, *wq_blocks),
        [shape((rows, local_cols), BF16)] * 2,
        [pltpu.VMEM((rows, local_cols), F32)],
        2 * rows * width * local_cols,
    )

    grad_keep, grad_send = call(
        functools.partial(grad_kernel, line),
        place,
        (live_flat, live_here, live_there, wo_pair, *wo_gated, *wo_relayed),
        [shape((rows, half_cols), BF16)] * 2,
        [pltpu.VMEM((rows, half_cols), F32)] * 2,
        2 * rows * width * local_cols,
    )
    grad_come = line.swap(grad_send)

    att_moved = line.along(attended)
    att_swapped = line.swap(attended)

    query_grad, kv_part = call(
        functools.partial(backward_kernel, image_own),
        place,
        (queries, kv_all, grad_keep, grad_come),
        [shape((rows, local_cols), BF16), shape((images, 2 * local_cols), F32)],
        (),
        10 * images * rows * local_cols,
    )

    att_ready = lax.optimization_barrier((*att_moved, att_swapped, query_grad))
    att_moved, att_swapped = att_ready[: len(att_moved)], att_ready[len(att_moved)]
    att_relayed = line.relay(att_moved)
    att_others = line.swap_moved(att_moved)
    att_last = line.swap_relayed(att_relayed)

    term = call(
        functools.partial(term_kernel, line),
        place,
        (att_ready[-1], *wq_blocks),
        [shape((n_dp, rows, own_width), BF16)],
        (),
        2 * rows * width * local_cols,
    )
    term = term.reshape(n_tensor, n_dp // n_tensor, rows, own_width)
    text_parts = lax.all_to_all(term, "tensor", split_axis=0, concat_axis=0)
    text_parts = text_parts.reshape(term.shape)
    text_grad = jnp.sum(text_parts.astype(F32), axis=0).astype(BF16)
    text_grad = text_grad.transpose(1, 0, 2).reshape(samples, tok_rows, width // n_tensor)

    kv_part = kv_part.reshape(n_dp, image_rows, 2 * local_cols)
    kv_grad = jnp.sum(lax.all_to_all(kv_part, "dp", split_axis=0, concat_axis=0), axis=0)
    kv_grad_all = everywhere(kv_grad.astype(BF16)).reshape(images, 2 * local_cols)
    image_term = matmul(kv_grad_all[:, :local_cols], key_weight, BACK)
    image_term = image_term + matmul(kv_grad_all[:, local_cols:], value_weight, BACK)
    image_term = lax.all_to_all(
        image_term.astype(BF16), "dp", split_axis=0, concat_axis=1, tiled=True
    )
    image_parts = lax.all_to_all(
        image_term.reshape(image_rows, n_tensor, width // n_tensor),
        "tensor",
        split_axis=1,
        concat_axis=0,
    )
    image_grad = jnp.sum(image_parts.astype(F32), axis=0).astype(BF16)
    image_grad = image_grad.reshape(samples, image_own, width // n_tensor)

    weight_grad = call(
        functools.partial(weight_grad_kernel, line),
        place,
        (*live_cols, attended, *att_moved, *att_relayed, att_swapped, *att_others, *att_last),
        [shape((local_cols, own_width), BF16)],
        [pltpu.VMEM((local_cols, own_width), F32)],
        2 * n_dp * rows * local_cols * own_width,
    )
    return text_grad, image_grad, weight_grad


def solution(mesh):
    return jax.shard_map(
        shards,
        mesh=mesh,
        in_specs=(
            P(None, "dp", None),
            P(None, "dp", None),
            P(None, "dp", None),
            P(),
            P("dp", "tensor"),
            P("dp", "tensor"),
            P("dp", "tensor"),
            P("tensor", "dp"),
        ),
        out_specs=(P(None, "dp", "tensor"), P(None, "dp", "tensor"), P("tensor", "dp")),
        check_vma=False,
    )
```

```python
import functools

import jax
import jax.numpy as jnp
from jax import lax
from jax.experimental import pallas as pl
from jax.experimental.pallas import tpu as pltpu
from jax.sharding import PartitionSpec as P

HEAD_DIM = 128
F32 = jnp.float32
BF16 = jnp.bfloat16
BACK = (((1,), (1,)), ((), ()))
FIRST = (((0,), (0,)), ((), ()))
VMEM_LIMIT = 48 * 1024 * 1024


def after(values, *others):
    return lax.optimization_barrier((values, *others))[0]


def matmul(a, b, dims=None):
    if dims is None:
        return jnp.dot(a, b, preferred_element_type=F32)
    return lax.dot_general(a, b, dims, preferred_element_type=F32)


class Line:
    def __init__(self):
        self.n_dp = lax.axis_size("dp")
        self.n_z = self.n_dp // 2

    def move(self, block, moves):
        pairs = [(2 * a + e, 2 * b + e) for a, b in moves for e in range(2)]
        return lax.ppermute(block, "dp", pairs)

    def swap(self, block, planes=None):
        planes = range(self.n_z) if planes is None else planes
        pairs = [(2 * a + e, 2 * a + 1 - e) for a in planes for e in range(2)]
        return lax.ppermute(block, "dp", pairs)

    def shift(self, block, distance):
        n = self.n_z
        return self.move(block, [((a + distance) % n, a) for a in range(n)])

    def near(self, block):
        above = self.move(block, [(1, 0), (2, 1), (3, 2)])
        below = self.move(block, [(0, 1), (1, 2), (2, 3)])
        return above, self.shift(block, 2), below

    def slots(self, z, relayed):
        if not relayed:
            return [(m, None) for m in range(self.n_z)]
        return [
            (0, None),
            (1, z < 3),
            (2, None),
            (3, z > 0),
            (jnp.where(z == 3, 1, 3), (z == 3) | (z == 0)),
        ]


def each_block(line, place, relayed, body):
    z, x = place[0], place[1]
    for i, (m, came) in enumerate(line.slots(z, relayed)):
        plane = lax.rem(z + m, line.n_z)
        for e in range(2):
            index = 2 * plane + (x if e == 0 else 1 - x)
            if came is None:
                body(i, e, index)
            else:
                pl.when(came)(functools.partial(body, i, e, index))


def columns(index, size):
    return pl.ds(pl.multiple_of(index * size, size), size)


def probabilities(query, key, image_own):
    scores = matmul(key, query, BACK) * HEAD_DIM ** (-0.5)
    image = lax.broadcasted_iota(jnp.int32, scores.shape, 0)
    token = lax.broadcasted_iota(jnp.int32, scores.shape, 1)
    image_sample = lax.rem(lax.div(image, image_own), 2)
    same = image_sample == lax.div(token, scores.shape[1] // 2)
    scores = jnp.where(same, scores, -1e30)
    peak = jnp.max(scores, axis=0, keepdims=True)
    expo = jnp.where(same, jnp.exp(scores - peak), 0.0)
    return expo / jnp.sum(expo, axis=0, keepdims=True)


def forward_kernel(line, relayed, image_own, place, text, kv, *refs):
    n = (len(refs) - 3) // 2
    weights, (query_out, attended_out, total) = (refs[:n], refs[n : 2 * n]), refs[2 * n :]
    own_width = weights[0][0].shape[0]
    rows, cols = total.shape
    total[...] = jnp.zeros_like(total)

    def add(i, e, index):
        total[...] += matmul(text[:, columns(index, own_width)], weights[e][i][...])

    each_block(line, place, relayed, add)
    query_out[...] = total[...].astype(BF16)
    part = rows // 4
    quarter = place[2]
    for h in range(cols // HEAD_DIM):
        at = slice(h * HEAD_DIM, (h + 1) * HEAD_DIM)
        value = kv[:, cols + h * HEAD_DIM : cols + (h + 1) * HEAD_DIM]
        prob = probabilities(query_out[:, at], kv[:, at], image_own)
        attended = matmul(prob.astype(BF16), value, FIRST).astype(BF16)
        for r in range(4):
            low_bit = (quarter + r) % 2
            high_bit = (quarter // 2 + r // 2) % 2
            start = pl.multiple_of((2 * low_bit + high_bit) * part, part)
            attended_out[pl.ds(start, part), at] = attended[r * part : (r + 1) * part]


def grad_kernel(line, place, live, here, there, *refs):
    weights, (keep_out, send_out, keep, send) = refs[:-4], refs[-4:]
    own_width = weights[0].shape[1] // 2
    half = line.n_dp // 2
    core = place[2] % 2
    keep[...] = jnp.zeros_like(keep)
    send[...] = jnp.zeros_like(send)

    def add(i, e, index):
        weight = weights[i][:, e * own_width : (e + 1) * own_width]
        keep[...] += matmul(live[:, columns(index, own_width)], weight, BACK)
        inner = columns(lax.rem(index, half), own_width)
        other = jnp.where(lax.div(index, half) == core, here[:, inner], there[:, inner])
        send[...] += matmul(other, weight, BACK)

    each_block(line, place, False, add)
    keep_out[...] = keep[...].astype(BF16)
    send_out[...] = send[...].astype(BF16)


def backward_kernel(image_own, place, query, kv, keep, come, query_grad, kv_grad):
    cols = query.shape[1]
    half = cols // 2
    x = place[1]
    for h in range(cols // HEAD_DIM):
        at = slice(h * HEAD_DIM, (h + 1) * HEAD_DIM)
        value_at = slice(cols + h * HEAD_DIM, cols + (h + 1) * HEAD_DIM)
        side = h * HEAD_DIM // half
        inner = slice(h * HEAD_DIM - side * half, (h + 1) * HEAD_DIM - side * half)
        grad = jnp.where(x == side, keep[:, inner], come[:, inner])
        prob = probabilities(query[:, at], kv[:, at], image_own)
        kv_grad[:, value_at] = matmul(prob.astype(BF16), grad)
        prob_grad = matmul(kv[:, value_at], grad, BACK)
        delta = jnp.sum(prob * prob_grad, axis=0, keepdims=True)
        score_grad = (prob * (prob_grad - delta) * HEAD_DIM ** (-0.5)).astype(BF16)
        kv_grad[:, at] = matmul(score_grad, query[:, at])
        query_grad[:, at] = matmul(score_grad, kv[:, at], FIRST).astype(BF16)


def term_kernel(line, relayed, place, query_grad, *refs):
    out = refs[-1]
    n = (len(refs) - 1) // 2
    weights = (refs[:n], refs[n : 2 * n])
    chunk = out.shape[1]

    def write(i, e, index):
        term = matmul(query_grad[...], weights[e][i][...], BACK)
        member = lax.bitwise_xor(lax.div(index, chunk), place[3])
        out[member, lax.rem(index, chunk)] = term.astype(BF16)

    each_block(line, place, relayed, write)


def weight_grad_kernel(line, place, *refs):
    live, refs = refs[:2], refs[2:]
    n = (len(refs) - 2) // 2
    attended, (out, total) = (refs[:n], refs[n : 2 * n]), refs[2 * n :]
    total[...] = jnp.zeros_like(total)

    def add(i, e, index):
        block = jnp.concatenate([part[i, index] for part in live for i in range(2)], axis=0)
        term = matmul(attended[e][i][...], block, FIRST)
        total[...] += term.astype(BF16).astype(F32)

    each_block(line, place, False, add)
    out[...] = total[...].astype(BF16)


def call(kernel, place, operands, outs, scratch=(), flops=0):
    moved = sum(a.size * a.dtype.itemsize for a in (*operands, *outs))
    single = len(outs) == 1
    return pl.pallas_call(
        kernel,
        out_shape=outs[0] if single else outs,
        in_specs=[pl.BlockSpec(memory_space=pltpu.SMEM)]
        + [pl.BlockSpec(memory_space=pltpu.VMEM)] * len(operands),
        out_specs=pl.BlockSpec(memory_space=pltpu.VMEM)
        if single
        else [pl.BlockSpec(memory_space=pltpu.VMEM)] * len(outs),
        scratch_shapes=list(scratch),
        compiler_params=pltpu.CompilerParams(vmem_limit_bytes=VMEM_LIMIT),
        cost_estimate=pl.CostEstimate(flops=flops, bytes_accessed=moved, transcendentals=0),
    )(place, *operands)


def shards(
    text_states,
    image_states,
    out_grad,
    text_lengths,
    query_weight,
    key_weight,
    value_weight,
    out_weight,
):
    samples, tok_rows, width = text_states.shape
    image_own = image_states.shape[1]
    line = Line()
    n_dp = line.n_dp
    n_tensor = lax.axis_size("tensor")
    dp_at, tensor_at = lax.axis_index("dp"), lax.axis_index("tensor")
    x, core = dp_at % 2, tensor_at % 2
    place = jnp.stack([dp_at // 2, x, tensor_at % 4, tensor_at]).astype(jnp.int32)
    rows = samples * tok_rows
    image_rows = samples * image_own
    images = n_dp * image_rows
    local_cols = query_weight.shape[1]
    own_width = query_weight.shape[0]
    half_cols = local_cols // 2
    shape = jax.ShapeDtypeStruct

    def tensor_swap(block, bit):
        return lax.ppermute(block, "tensor", [(t, t ^ bit) for t in range(n_tensor)])

    positions = dp_at * tok_rows + lax.iota(jnp.int32, tok_rows)
    live_rows = positions[None, :] < text_lengths[:, None]
    grad_live = jnp.where(live_rows[..., None], out_grad, jnp.zeros_like(out_grad))
    text_flat = text_states.reshape(rows, width)
    live_flat = grad_live.reshape(rows, width)
    image_flat = image_states.reshape(image_rows, width)

    gate = lax.optimization_barrier

    relayed = line.n_z == 4
    if relayed:
        wq_moved = list(line.near(query_weight))
    else:
        wq_moved = [line.shift(query_weight, m) for m in range(1, line.n_z)]
    wq_swapped = line.swap(query_weight)
    wo_keep = lax.dynamic_slice_in_dim(out_weight, x * half_cols, half_cols, 0)
    wo_send = lax.dynamic_slice_in_dim(out_weight, (1 - x) * half_cols, half_cols, 0)
    live_half = lax.dynamic_slice_in_dim(live_flat, core * (width // 2), width // 2, 1)
    wo_send, live_half, _ = gate((wo_send, live_half, wq_swapped))
    wo_come = line.swap(wo_send)
    live_here = line.swap(live_half)
    image_cols = lax.all_to_all(image_flat, "dp", split_axis=1, concat_axis=0, tiled=True)
    quarter_rows = rows // 4
    live_part = lax.dynamic_slice_in_dim(
        live_flat, (tensor_at % 4) * quarter_rows, quarter_rows, 0
    ).reshape(quarter_rows, n_dp, own_width)
    live_mine = lax.all_to_all(live_part, "dp", split_axis=1, concat_axis=0)
    live_mine = live_mine.reshape(n_dp, quarter_rows, own_width)
    wo_pair = jnp.concatenate([wo_keep, wo_come], axis=1)
    wo_pair, live_here, live_mine, image_cols, wq_swapped, *wq_moved = gate(
        (wo_pair, live_here, live_mine, image_cols, wq_swapped, *wq_moved)
    )

    if relayed:
        wq_moved.append(line.move(wq_moved[1], [(1, 0), (2, 3)]))
        planes = [(0, 1, 2), None, (1, 2, 3), (0, 3)]
    else:
        planes = [None] * len(wq_moved)
    wo_far = [line.shift(wo_pair, m) for m in range(2, line.n_z - 1)]
    wq_others = [line.swap(block, at) for block, at in zip(wq_moved[:2], planes)]
    live_y = tensor_swap(live_mine, 2)
    part_kv = jnp.concatenate(
        [matmul(image_cols, key_weight), matmul(image_cols, value_weight)], axis=1
    )
    part_kv = part_kv.reshape(n_dp, image_rows, 2 * local_cols)
    kv_own = jnp.sum(lax.all_to_all(part_kv, "dp", split_axis=0, concat_axis=0), axis=0)
    live_pair = jnp.stack([live_mine, live_y])
    n_moved, n_far = len(wq_moved), len(wo_far)
    second = gate((wo_pair, kv_own, live_here, live_pair, *wq_others, *wq_moved, *wo_far))
    wo_pair, kv_own, live_here, live_pair, *second = second
    wq_others, second = second[:2], second[2:]
    wq_moved, wo_far = second[:n_moved], second[n_moved:]

    def everywhere(values):
        copies = jnp.broadcast_to(values[None], (n_dp, *values.shape))
        return lax.all_to_all(copies, "dp", split_axis=0, concat_axis=0)

    wo_next = [line.shift(wo_pair, m) for m in (1, line.n_z - 1)]
    wq_others += [line.swap(block, at) for block, at in zip(wq_moved[2:], planes[2:])]
    live_there = tensor_swap(live_here, 1)
    kv_all = everywhere(kv_own.astype(BF16)).reshape(images, 2 * local_cols)
    wq_blocks = [query_weight, *wq_moved, wq_swapped, *wq_others]
    queries, attended = call(
        functools.partial(forward_kernel, line, relayed, image_own),
        place,
        (text_flat, kv_all, *wq_blocks),
        [shape((rows, local_cols), BF16)] * 2,
        [pltpu.VMEM((rows, local_cols), F32)],
        2 * rows * width * local_cols,
    )
    attended, live_pair, live_there, wo_pair, *wo_rest = gate(
        (attended, live_pair, live_there, wo_pair, *wo_next, *wo_far)
    )

    att_next = [line.shift(attended, m) for m in (1, line.n_z - 1)]
    att_swapped = line.swap(attended)
    grad_keep, grad_send = call(
        functools.partial(grad_kernel, line),
        place,
        (live_flat, live_here, live_there, wo_pair, wo_rest[0], *wo_rest[2:], wo_rest[1]),
        [shape((rows, half_cols), BF16)] * 2,
        [pltpu.VMEM((rows, half_cols), F32)] * 2,
        2 * rows * width * local_cols,
    )
    grad_come = line.swap(grad_send)
    live_core = tensor_swap(live_pair, 1)
    query_grad, kv_part = call(
        functools.partial(backward_kernel, image_own),
        place,
        (queries, kv_all, grad_keep, grad_come),
        [shape((rows, local_cols), BF16), shape((images, 2 * local_cols), F32)],
        (),
        10 * images * rows * local_cols,
    )
    chunk = n_dp // n_tensor
    term = call(
        functools.partial(term_kernel, line, relayed),
        place,
        (query_grad, *wq_blocks),
        [shape((n_tensor, chunk, rows, own_width), BF16)],
        (),
        2 * rows * width * local_cols,
    )
    kv_part = kv_part.reshape(n_dp, image_rows, 2 * local_cols)
    kv_part, term, attended, live_core, att_swapped, *att_next = gate(
        (kv_part, term, attended, live_core, att_swapped, *att_next)
    )

    text_parts = [term[0]]
    for k in range(n_tensor - 1, 1, -1):
        text_parts.append(tensor_swap(term[k], k))
    att_far = [line.shift(attended, m) for m in range(2, line.n_z - 1)]
    att_other_next = [line.swap(block) for block in att_next]
    kv_grad = jnp.sum(lax.all_to_all(kv_part, "dp", split_axis=0, concat_axis=0), axis=0)
    kv_grad, term_core, *third = gate(
        (kv_grad.astype(BF16), term[1], *att_other_next, *att_far)
    )
    att_other_next, att_far = third[:2], third[2:]

    text_parts.append(tensor_swap(term_core, 1))
    att_other_far = [line.swap(block) for block in att_far]
    kv_grad_all = everywhere(kv_grad).reshape(images, 2 * local_cols)
    image_term = matmul(kv_grad_all[:, :local_cols], key_weight, BACK)
    image_term = image_term + matmul(kv_grad_all[:, local_cols:], value_weight, BACK)
    image_term = lax.all_to_all(
        image_term.astype(BF16), "dp", split_axis=0, concat_axis=1, tiled=True
    )
    image_parts = lax.all_to_all(
        image_term.reshape(image_rows, n_tensor, width // n_tensor),
        "tensor",
        split_axis=1,
        concat_axis=0,
    )
    image_grad = jnp.sum(image_parts.astype(F32), axis=0).astype(BF16)
    image_grad = image_grad.reshape(samples, image_own, width // n_tensor)
    text_grad = functools.reduce(jnp.add, [part.astype(F32) for part in text_parts])
    text_grad = text_grad.astype(BF16).transpose(1, 0, 2)
    text_grad = text_grad.reshape(samples, tok_rows, width // n_tensor)

    att_blocks = [attended, att_next[0], *att_far, att_next[1]]
    att_others = [att_swapped, att_other_next[0], *att_other_far, att_other_next[1]]
    weight_grad = call(
        functools.partial(weight_grad_kernel, line),
        place,
        (live_pair, live_core, *att_blocks, *att_others),
        [shape((local_cols, own_width), BF16)],
        [pltpu.VMEM((local_cols, own_width), F32)],
        2 * n_dp * rows * local_cols * own_width,
    )
    return text_grad, image_grad, weight_grad


def solution(mesh):
    return jax.shard_map(
        shards,
        mesh=mesh,
        in_specs=(
            P(None, "dp", None),
            P(None, "dp", None),
            P(None, "dp", None),
            P(),
            P("dp", "tensor"),
            P("dp", "tensor"),
            P("dp", "tensor"),
            P("tensor", "dp"),
        ),
        out_specs=(P(None, "dp", "tensor"), P(None, "dp", "tensor"), P("tensor", "dp")),
        check_vma=False,
    )
```

```python
import functools

import jax
import jax.numpy as jnp
from jax import lax
from jax.experimental import pallas as pl
from jax.experimental.pallas import tpu as pltpu
from jax.sharding import PartitionSpec as P

HEAD_DIM = 128
F32 = jnp.float32
BF16 = jnp.bfloat16
BACK = (((1,), (1,)), ((), ()))
FIRST = (((0,), (0,)), ((), ()))
VMEM_LIMIT = 48 * 1024 * 1024


def after(values, *others):
    return lax.optimization_barrier((values, *others))[0]


def matmul(a, b, dims=None):
    if dims is None:
        return jnp.dot(a, b, preferred_element_type=F32)
    return lax.dot_general(a, b, dims, preferred_element_type=F32)


class Line:
    def __init__(self):
        self.n_dp = lax.axis_size("dp")
        self.n_z = self.n_dp // 2

    def move(self, block, moves):
        pairs = [(2 * a + e, 2 * b + e) for a, b in moves for e in range(2)]
        return lax.ppermute(block, "dp", pairs)

    def swap(self, block, planes=None):
        planes = range(self.n_z) if planes is None else planes
        pairs = [(2 * a + e, 2 * a + 1 - e) for a in planes for e in range(2)]
        return lax.ppermute(block, "dp", pairs)

    def shift(self, block, distance):
        n = self.n_z
        return self.move(block, [((a + distance) % n, a) for a in range(n)])

    def first(self, block):
        if self.n_z != 4:
            return [self.shift(block, m) for m in range(1, self.n_z)]
        above = self.move(block, [(1, 0), (2, 1), (3, 2)])
        below = self.move(block, [(0, 1), (1, 2), (2, 3)])
        return [above, below]

    def second(self, moved):
        if self.n_z != 4:
            return []
        return [self.move(moved[0], [(1, 0), (2, 1)]), self.move(moved[1], [(1, 2), (2, 3)])]

    def third(self, forwarded):
        if self.n_z != 4:
            return []
        across = jnp.where(lax.axis_index("dp") < 4, forwarded[0], forwarded[1])
        return [across, self.move(across, [(1, 0), (2, 3)])]

    def slots(self, z, relayed):
        if not relayed:
            return [(m, None) for m in range(self.n_z)]
        return [
            (0, None),
            (1, z < 3),
            (3, z > 0),
            (2, None),
            (jnp.where(z == 3, 1, 3), (z == 3) | (z == 0)),
        ]


def each_block(line, place, relayed, body):
    z, x = place[0], place[1]
    for i, (m, came) in enumerate(line.slots(z, relayed)):
        plane = lax.rem(z + m, line.n_z)
        for e in range(2):
            index = 2 * plane + (x if e == 0 else 1 - x)
            if came is None:
                body(i, e, index)
            else:
                pl.when(came)(functools.partial(body, i, e, index))


def columns(index, size):
    return pl.ds(pl.multiple_of(index * size, size), size)


def probabilities(query, key, image_own):
    scores = matmul(key, query, BACK) * HEAD_DIM ** (-0.5)
    image = lax.broadcasted_iota(jnp.int32, scores.shape, 0)
    token = lax.broadcasted_iota(jnp.int32, scores.shape, 1)
    image_sample = lax.rem(lax.div(image, image_own), 2)
    same = image_sample == lax.div(token, scores.shape[1] // 2)
    scores = jnp.where(same, scores, -1e30)
    peak = jnp.max(scores, axis=0, keepdims=True)
    expo = jnp.where(same, jnp.exp(scores - peak), 0.0)
    return expo / jnp.sum(expo, axis=0, keepdims=True)


def forward_kernel(line, relayed, image_own, place, text, kv, *refs):
    n = (len(refs) - 3) // 2
    weights, (query_out, attended_out, total) = (refs[:n], refs[n : 2 * n]), refs[2 * n :]
    own_width = weights[0][0].shape[0]
    rows, cols = total.shape
    total[...] = jnp.zeros_like(total)

    def add(i, e, index):
        total[...] += matmul(text[:, columns(index, own_width)], weights[e][i][...])

    each_block(line, place, relayed, add)
    query_out[...] = total[...].astype(BF16)
    part = rows // 4
    quarter = place[2]
    for h in range(cols // HEAD_DIM):
        at = slice(h * HEAD_DIM, (h + 1) * HEAD_DIM)
        value = kv[:, cols + h * HEAD_DIM : cols + (h + 1) * HEAD_DIM]
        prob = probabilities(query_out[:, at], kv[:, at], image_own)
        attended = matmul(prob.astype(BF16), value, FIRST).astype(BF16)
        for r in range(4):
            low_bit = (quarter + r) % 2
            high_bit = (quarter // 2 + r // 2) % 2
            start = pl.multiple_of((2 * low_bit + high_bit) * part, part)
            attended_out[pl.ds(start, part), at] = attended[r * part : (r + 1) * part]


def grad_kernel(line, place, live, here, there, *refs):
    weights, (keep_out, send_out, keep, send) = refs[:-4], refs[-4:]
    own_width = weights[0].shape[1] // 2
    half = line.n_dp // 2
    core = place[2] % 2
    keep[...] = jnp.zeros_like(keep)
    send[...] = jnp.zeros_like(send)

    def add(i, e, index):
        weight = weights[i][:, e * own_width : (e + 1) * own_width]
        keep[...] += matmul(live[:, columns(index, own_width)], weight, BACK)
        inner = columns(lax.rem(index, half), own_width)
        other = jnp.where(lax.div(index, half) == core, here[:, inner], there[:, inner])
        send[...] += matmul(other, weight, BACK)

    each_block(line, place, line.n_z == 4, add)
    keep_out[...] = keep[...].astype(BF16)
    send_out[...] = send[...].astype(BF16)


def backward_kernel(image_own, place, query, kv, keep, come, query_grad, kv_grad):
    cols = query.shape[1]
    half = cols // 2
    x = place[1]
    for h in range(cols // HEAD_DIM):
        at = slice(h * HEAD_DIM, (h + 1) * HEAD_DIM)
        value_at = slice(cols + h * HEAD_DIM, cols + (h + 1) * HEAD_DIM)
        side = h * HEAD_DIM // half
        inner = slice(h * HEAD_DIM - side * half, (h + 1) * HEAD_DIM - side * half)
        grad = jnp.where(x == side, keep[:, inner], come[:, inner])
        prob = probabilities(query[:, at], kv[:, at], image_own)
        kv_grad[:, value_at] = matmul(prob.astype(BF16), grad)
        prob_grad = matmul(kv[:, value_at], grad, BACK)
        delta = jnp.sum(prob * prob_grad, axis=0, keepdims=True)
        score_grad = (prob * (prob_grad - delta) * HEAD_DIM ** (-0.5)).astype(BF16)
        kv_grad[:, at] = matmul(score_grad, query[:, at])
        query_grad[:, at] = matmul(score_grad, kv[:, at], FIRST).astype(BF16)


def term_kernel(line, relayed, place, query_grad, *refs):
    out = refs[-1]
    n = (len(refs) - 1) // 2
    weights = (refs[:n], refs[n : 2 * n])
    chunk = out.shape[1]

    def write(i, e, index):
        term = matmul(query_grad[...], weights[e][i][...], BACK)
        member = lax.bitwise_xor(lax.div(index, chunk), place[3])
        out[member, lax.rem(index, chunk)] = term.astype(BF16)

    each_block(line, place, relayed, write)


def weight_grad_kernel(line, place, *refs):
    live, refs = refs[:2], refs[2:]
    n = (len(refs) - 2) // 2
    attended, (out, total) = (refs[:n], refs[n : 2 * n]), refs[2 * n :]
    total[...] = jnp.zeros_like(total)

    def add(i, e, index):
        block = jnp.concatenate([part[i, index] for part in live for i in range(2)], axis=0)
        term = matmul(attended[e][i][...], block, FIRST)
        total[...] += term.astype(BF16).astype(F32)

    each_block(line, place, False, add)
    out[...] = total[...].astype(BF16)


def call(kernel, place, operands, outs, scratch=(), flops=0):
    moved = sum(a.size * a.dtype.itemsize for a in (*operands, *outs))
    single = len(outs) == 1
    return pl.pallas_call(
        kernel,
        out_shape=outs[0] if single else outs,
        in_specs=[pl.BlockSpec(memory_space=pltpu.SMEM)]
        + [pl.BlockSpec(memory_space=pltpu.VMEM)] * len(operands),
        out_specs=pl.BlockSpec(memory_space=pltpu.VMEM)
        if single
        else [pl.BlockSpec(memory_space=pltpu.VMEM)] * len(outs),
        scratch_shapes=list(scratch),
        compiler_params=pltpu.CompilerParams(vmem_limit_bytes=VMEM_LIMIT),
        cost_estimate=pl.CostEstimate(flops=flops, bytes_accessed=moved, transcendentals=0),
    )(place, *operands)


def to_owner(line, terms):
    n_dp, n_tensor = line.n_dp, lax.axis_size("tensor")
    images, cols = terms.shape
    if line.n_z != n_tensor:
        terms = lax.all_to_all(terms, "dp", split_axis=0, concat_axis=1, tiled=True)
        terms = terms.reshape(images // n_dp, n_tensor, n_dp * cols // n_tensor)
        parts = lax.all_to_all(terms, "tensor", split_axis=1, concat_axis=0)
        return jnp.sum(parts.astype(F32), axis=0).astype(BF16)
    parts = lax.all_to_all(
        terms.reshape(n_tensor, images // n_tensor, cols), "tensor", split_axis=0, concat_axis=0
    )
    total = jnp.sum(parts.astype(F32), axis=0).astype(BF16)
    total = total.reshape(2, images // n_dp, cols)
    x = lax.axis_index("dp") % 2
    come = []
    for other in range(2):
        block = jnp.where(x == other, total[0], total[1])
        pairs = [
            ((2 * z + e) * n_tensor + t, (2 * t + (e ^ other)) * n_tensor + z)
            for z in range(line.n_z)
            for e in range(2)
            for t in range(n_tensor)
        ]
        come.append(lax.ppermute(block, ("dp", "tensor"), pairs))
    return jnp.where(
        x == 0, jnp.concatenate(come, axis=1), jnp.concatenate(come[::-1], axis=1)
    )


def shards(
    text_states,
    image_states,
    out_grad,
    text_lengths,
    query_weight,
    key_weight,
    value_weight,
    out_weight,
):
    samples, tok_rows, width = text_states.shape
    image_own = image_states.shape[1]
    line = Line()
    n_dp = line.n_dp
    n_tensor = lax.axis_size("tensor")
    dp_at, tensor_at = lax.axis_index("dp"), lax.axis_index("tensor")
    x, core = dp_at % 2, tensor_at % 2
    place = jnp.stack([dp_at // 2, x, tensor_at % 4, tensor_at]).astype(jnp.int32)
    rows = samples * tok_rows
    image_rows = samples * image_own
    images = n_dp * image_rows
    local_cols = query_weight.shape[1]
    own_width = query_weight.shape[0]
    half_cols = local_cols // 2
    shape = jax.ShapeDtypeStruct

    def tensor_swap(block, bit):
        return lax.ppermute(block, "tensor", [(t, t ^ bit) for t in range(n_tensor)])

    positions = dp_at * tok_rows + lax.iota(jnp.int32, tok_rows)
    live_rows = positions[None, :] < text_lengths[:, None]
    grad_live = jnp.where(live_rows[..., None], out_grad, jnp.zeros_like(out_grad))
    text_flat = text_states.reshape(rows, width)
    live_flat = grad_live.reshape(rows, width)
    image_flat = image_states.reshape(image_rows, width)

    gate = lax.optimization_barrier

    relayed = line.n_z == 4
    wq_moved = line.first(query_weight)
    wo_keep = lax.dynamic_slice_in_dim(out_weight, x * half_cols, half_cols, 0)
    wo_send = lax.dynamic_slice_in_dim(out_weight, (1 - x) * half_cols, half_cols, 0)
    wo_come = line.swap(wo_send)
    wq_swapped = line.swap(query_weight)
    live_half = lax.dynamic_slice_in_dim(live_flat, core * (width // 2), width // 2, 1)
    live_half, wo_come = gate((live_half, wo_come))
    live_here = line.swap(live_half)
    image_cols = lax.all_to_all(image_flat, "dp", split_axis=1, concat_axis=0, tiled=True)
    wo_pair = jnp.concatenate([wo_keep, wo_come], axis=1)
    wo_pair, image_cols, *wq_moved = gate((wo_pair, image_cols, *wq_moved))

    planes = [(0, 1, 2), (1, 2, 3)] if relayed else [None] * len(wq_moved)
    wq_two = line.second(wq_moved)
    wo_moved = line.first(wo_pair)
    above, live_here = gate((wq_moved[0], live_here))
    wq_others = [line.swap(above, planes[0])]
    part_kv = jnp.concatenate(
        [matmul(image_cols, key_weight), matmul(image_cols, value_weight)], axis=1
    )
    part_kv = part_kv.reshape(n_dp, image_rows, 2 * local_cols)
    kv_own = jnp.sum(lax.all_to_all(part_kv, "dp", split_axis=0, concat_axis=0), axis=0)
    kv_own, live_here, wq_swapped, wq_others[0], *moved = gate(
        (kv_own, live_here, wq_swapped, wq_others[0], *wq_moved, *wq_two, *wo_moved)
    )
    n_moved = len(wq_moved)
    wq_moved, wq_two, wo_moved = moved[:n_moved], moved[n_moved:-n_moved], moved[-n_moved:]

    def everywhere(values):
        copies = jnp.broadcast_to(values[None], (n_dp, *values.shape))
        return lax.all_to_all(copies, "dp", split_axis=0, concat_axis=0)

    wq_last = line.third(wq_two)
    wo_two = line.second(wo_moved)
    wq_others += [line.swap(block, at) for block, at in zip(wq_moved[1:], planes[1:])]
    wq_others += [line.swap(block) for block in wq_last[:1]]
    kv_all = everywhere(kv_own.astype(BF16)).reshape(images, 2 * local_cols)
    kv_all, live_here, wo_pair, live_flat, *moved = gate(
        (kv_all, live_here, wo_pair, live_flat, *wo_moved, *wo_two, *wq_others, *wq_last)
    )
    wo_moved, moved = moved[:n_moved], moved[n_moved:]
    wo_two, moved = moved[: len(wo_two)], moved[len(wo_two) :]
    wq_others, wq_last = moved[: len(wq_others)], moved[len(wq_others) :]

    wo_last = line.third(wo_two)
    wq_others += [line.swap(block, (0, 3)) for block in wq_last[1:]]
    live_there = tensor_swap(live_here, 1)
    quarter_rows = rows // 4
    live_part = lax.dynamic_slice_in_dim(
        live_flat, (tensor_at % 4) * quarter_rows, quarter_rows, 0
    ).reshape(quarter_rows, n_dp, own_width)
    live_mine = lax.all_to_all(live_part, "dp", split_axis=1, concat_axis=0)
    live_mine = live_mine.reshape(n_dp, quarter_rows, own_width)
    wq_blocks = [query_weight, *wq_moved, *wq_last, wq_swapped, *wq_others]

    grad_keep, grad_send = call(
        functools.partial(grad_kernel, line),
        place,
        (live_flat, live_here, live_there, wo_pair, *wo_moved, *wo_last),
        [shape((rows, half_cols), BF16)] * 2,
        [pltpu.VMEM((rows, half_cols), F32)] * 2,
        2 * rows * width * local_cols,
    )
    grad_come = line.swap(grad_send)
    text_flat, live_mine, _ = gate((text_flat, live_mine, grad_send))
    queries, attended = call(
        functools.partial(forward_kernel, line, relayed, image_own),
        place,
        (text_flat, kv_all, *wq_blocks),
        [shape((rows, local_cols), BF16)] * 2,
        [pltpu.VMEM((rows, local_cols), F32)],
        2 * rows * width * local_cols,
    )

    att_next = [line.shift(attended, m) for m in (1, line.n_z - 1)]
    att_swapped = line.swap(attended)
    live_pair = jnp.stack([live_mine, tensor_swap(live_mine, 2)])
    query_grad, kv_part = call(
        functools.partial(backward_kernel, image_own),
        place,
        (queries, kv_all, grad_keep, grad_come),
        [shape((rows, local_cols), BF16), shape((images, 2 * local_cols), F32)],
        (),
        10 * images * rows * local_cols,
    )
    chunk = n_dp // n_tensor
    term = call(
        functools.partial(term_kernel, line, relayed),
        place,
        (query_grad, *wq_blocks),
        [shape((n_tensor, chunk, rows, own_width), BF16)],
        (),
        2 * rows * width * local_cols,
    )
    kv_part = kv_part.reshape(n_dp, image_rows, 2 * local_cols)
    kv_grad = jnp.sum(lax.all_to_all(kv_part, "dp", split_axis=0, concat_axis=0), axis=0)
    kv_grad, term, attended, live_pair, att_swapped, *att_next = gate(
        (kv_grad.astype(BF16), term, attended, live_pair, att_swapped, *att_next)
    )

    text_parts = [term[0]]
    for k in range(n_tensor - 1, 1, -1):
        text_parts.append(tensor_swap(term[k], k))
    att_far = [line.shift(attended, m) for m in range(2, line.n_z - 1)]
    att_other_next = [line.swap(block) for block in att_next]
    kv_grad_all = everywhere(kv_grad).reshape(images, 2 * local_cols)
    kv_grad_all, term_core, live_pair, *third = gate(
        (kv_grad_all, term[1], live_pair, *att_other_next, *att_far)
    )
    att_other_next, att_far = third[:2], third[2:]

    text_parts.append(tensor_swap(term_core, 1))
    live_core = tensor_swap(live_pair, 1)
    att_other_far = [line.swap(block) for block in att_far]
    image_term = matmul(kv_grad_all[:, :local_cols], key_weight, BACK)
    image_term = image_term + matmul(kv_grad_all[:, local_cols:], value_weight, BACK)
    image_grad = to_owner(line, image_term.astype(BF16))
    image_grad = image_grad.reshape(samples, image_own, width // n_tensor)
    text_grad = functools.reduce(jnp.add, [part.astype(F32) for part in text_parts])
    text_grad = text_grad.astype(BF16).transpose(1, 0, 2)
    text_grad = text_grad.reshape(samples, tok_rows, width // n_tensor)

    att_blocks = [attended, att_next[0], *att_far, att_next[1]]
    att_others = [att_swapped, att_other_next[0], *att_other_far, att_other_next[1]]
    weight_grad = call(
        functools.partial(weight_grad_kernel, line),
        place,
        (live_pair, live_core, *att_blocks, *att_others),
        [shape((local_cols, own_width), BF16)],
        [pltpu.VMEM((local_cols, own_width), F32)],
        2 * n_dp * rows * local_cols * own_width,
    )
    return text_grad, image_grad, weight_grad


def solution(mesh):
    return jax.shard_map(
        shards,
        mesh=mesh,
        in_specs=(
            P(None, "dp", None),
            P(None, "dp", None),
            P(None, "dp", None),
            P(),
            P("dp", "tensor"),
            P("dp", "tensor"),
            P("dp", "tensor"),
            P("tensor", "dp"),
        ),
        out_specs=(P(None, "dp", "tensor"), P(None, "dp", "tensor"), P("tensor", "dp")),
        check_vma=False,
    )
```

```python
import functools

import jax
import jax.numpy as jnp
from jax import lax
from jax.experimental import pallas as pl
from jax.experimental.pallas import tpu as pltpu
from jax.sharding import PartitionSpec as P

HEAD_DIM = 128
F32 = jnp.float32
BF16 = jnp.bfloat16
BACK = (((1,), (1,)), ((), ()))
FIRST = (((0,), (0,)), ((), ()))
VMEM_LIMIT = 48 * 1024 * 1024


def matmul(a, b, dims=None):
    if dims is None:
        return jnp.dot(a, b, preferred_element_type=F32)
    return lax.dot_general(a, b, dims, preferred_element_type=F32)


class Line:
    def __init__(self):
        self.n_dp = lax.axis_size("dp")
        self.n_z = self.n_dp // 2

    def move(self, block, moves):
        pairs = [(2 * a + e, 2 * b + e) for a, b in moves for e in range(2)]
        return lax.ppermute(block, "dp", pairs)

    def swap(self, block, planes=None):
        planes = range(self.n_z) if planes is None else planes
        pairs = [(2 * a + e, 2 * a + 1 - e) for a in planes for e in range(2)]
        return lax.ppermute(block, "dp", pairs)

    def shift(self, block, distance):
        n = self.n_z
        return self.move(block, [((a + distance) % n, a) for a in range(n)])

    def first(self, block):
        if self.n_z != 4:
            return [self.shift(block, m) for m in range(1, self.n_z)]
        above = self.move(block, [(1, 0), (2, 1), (3, 2)])
        below = self.move(block, [(0, 1), (1, 2), (2, 3)])
        return [above, below]

    def second(self, moved):
        if self.n_z != 4:
            return []
        return [self.move(moved[0], [(1, 0), (2, 1)]), self.move(moved[1], [(1, 2), (2, 3)])]

    def third(self, forwarded):
        if self.n_z != 4:
            return []
        across = jnp.where(lax.axis_index("dp") < 4, forwarded[0], forwarded[1])
        return [across, self.move(across, [(1, 0), (2, 3)])]

    def slots(self, z, relayed):
        if not relayed:
            return [(m, None) for m in range(self.n_z)]
        return [
            (0, None),
            (1, z < 3),
            (3, z > 0),
            (2, None),
            (jnp.where(z == 3, 1, 3), (z == 3) | (z == 0)),
        ]


def each_block(line, place, relayed, body):
    z, x = place[0], place[1]
    for i, (m, came) in enumerate(line.slots(z, relayed)):
        plane = lax.rem(z + m, line.n_z)
        for e in range(2):
            index = 2 * plane + (x if e == 0 else 1 - x)
            if came is None:
                body(i, e, index)
            else:
                pl.when(came)(functools.partial(body, i, e, index))


def columns(index, size):
    return pl.ds(pl.multiple_of(index * size, size), size)


def probabilities(query, key, image_own):
    scores = matmul(key, query, BACK) * HEAD_DIM ** (-0.5)
    image = lax.broadcasted_iota(jnp.int32, scores.shape, 0)
    token = lax.broadcasted_iota(jnp.int32, scores.shape, 1)
    image_sample = lax.rem(lax.div(image, image_own), 2)
    same = image_sample == lax.div(token, scores.shape[1] // 2)
    scores = jnp.where(same, scores, -1e30)
    peak = jnp.max(scores, axis=0, keepdims=True)
    expo = jnp.where(same, jnp.exp(scores - peak), 0.0)
    return expo / jnp.sum(expo, axis=0, keepdims=True)


def forward_kernel(line, relayed, image_own, place, text, kv, *refs):
    n = (len(refs) - 3) // 2
    weights, (query_out, attended_out, total) = (refs[:n], refs[n : 2 * n]), refs[2 * n :]
    own_width = weights[0][0].shape[0]
    rows, cols = total.shape
    total[...] = jnp.zeros_like(total)

    def add(i, e, index):
        total[...] += matmul(text[:, columns(index, own_width)], weights[e][i][...])

    each_block(line, place, relayed, add)
    query_out[...] = total[...].astype(BF16)
    part = rows // 4
    quarter = place[2]
    for h in range(cols // HEAD_DIM):
        at = slice(h * HEAD_DIM, (h + 1) * HEAD_DIM)
        value = kv[:, cols + h * HEAD_DIM : cols + (h + 1) * HEAD_DIM]
        prob = probabilities(query_out[:, at], kv[:, at], image_own)
        attended = matmul(prob.astype(BF16), value, FIRST).astype(BF16)
        for r in range(4):
            low_bit = (quarter + r) % 2
            high_bit = (quarter // 2 + r // 2) % 2
            start = pl.multiple_of((2 * low_bit + high_bit) * part, part)
            attended_out[pl.ds(start, part), at] = attended[r * part : (r + 1) * part]


def grad_kernel(line, place, live, here, there, *refs):
    weights, (keep_out, send_out, keep, send) = refs[:-4], refs[-4:]
    own_width = weights[0].shape[1] // 2
    half = line.n_dp // 2
    core = place[2] % 2
    keep[...] = jnp.zeros_like(keep)
    send[...] = jnp.zeros_like(send)

    def add(i, e, index):
        weight = weights[i][:, e * own_width : (e + 1) * own_width]
        keep[...] += matmul(live[:, columns(index, own_width)], weight, BACK)
        inner = columns(lax.rem(index, half), own_width)
        other = jnp.where(lax.div(index, half) == core, here[:, inner], there[:, inner])
        send[...] += matmul(other, weight, BACK)

    each_block(line, place, line.n_z == 4, add)
    keep_out[...] = keep[...].astype(BF16)
    send_out[...] = send[...].astype(BF16)


def backward_kernel(image_own, place, query, kv, keep, come, query_grad, kv_grad):
    cols = query.shape[1]
    half = cols // 2
    x = place[1]
    for h in range(cols // HEAD_DIM):
        at = slice(h * HEAD_DIM, (h + 1) * HEAD_DIM)
        value_at = slice(cols + h * HEAD_DIM, cols + (h + 1) * HEAD_DIM)
        side = h * HEAD_DIM // half
        inner = slice(h * HEAD_DIM - side * half, (h + 1) * HEAD_DIM - side * half)
        grad = jnp.where(x == side, keep[:, inner], come[:, inner])
        prob = probabilities(query[:, at], kv[:, at], image_own)
        kv_grad[:, value_at] = matmul(prob.astype(BF16), grad)
        prob_grad = matmul(kv[:, value_at], grad, BACK)
        delta = jnp.sum(prob * prob_grad, axis=0, keepdims=True)
        score_grad = (prob * (prob_grad - delta) * HEAD_DIM ** (-0.5)).astype(BF16)
        kv_grad[:, at] = matmul(score_grad, query[:, at])
        query_grad[:, at] = matmul(score_grad, kv[:, at], FIRST).astype(BF16)


def term_kernel(line, relayed, place, query_grad, *refs):
    out = refs[-1]
    n = (len(refs) - 1) // 2
    weights = (refs[:n], refs[n : 2 * n])
    chunk = out.shape[1]

    def write(i, e, index):
        term = matmul(query_grad[...], weights[e][i][...], BACK)
        member = lax.bitwise_xor(lax.div(index, chunk), place[3])
        out[member, lax.rem(index, chunk)] = term.astype(BF16)

    each_block(line, place, relayed, write)


def weight_grad_kernel(line, place, *refs):
    live, refs = refs[:2], refs[2:]
    n = (len(refs) - 2) // 2
    attended, (out, total) = (refs[:n], refs[n : 2 * n]), refs[2 * n :]
    total[...] = jnp.zeros_like(total)

    def add(i, e, index):
        block = jnp.concatenate([part[i, index] for part in live for i in range(2)], axis=0)
        term = matmul(attended[e][i][...], block, FIRST)
        total[...] += term.astype(BF16).astype(F32)

    each_block(line, place, False, add)
    out[...] = total[...].astype(BF16)


def call(kernel, place, operands, outs, scratch=(), flops=0):
    moved = sum(a.size * a.dtype.itemsize for a in (*operands, *outs))
    single = len(outs) == 1
    return pl.pallas_call(
        kernel,
        out_shape=outs[0] if single else outs,
        in_specs=[pl.BlockSpec(memory_space=pltpu.SMEM)]
        + [pl.BlockSpec(memory_space=pltpu.VMEM)] * len(operands),
        out_specs=pl.BlockSpec(memory_space=pltpu.VMEM)
        if single
        else [pl.BlockSpec(memory_space=pltpu.VMEM)] * len(outs),
        scratch_shapes=list(scratch),
        compiler_params=pltpu.CompilerParams(vmem_limit_bytes=VMEM_LIMIT),
        cost_estimate=pl.CostEstimate(flops=flops, bytes_accessed=moved, transcendentals=0),
    )(place, *operands)


def to_owner(line, terms, *others):
    n_dp, n_tensor = line.n_dp, lax.axis_size("tensor")
    images, cols = terms.shape
    if line.n_z != n_tensor:
        terms = lax.all_to_all(terms, "dp", split_axis=0, concat_axis=1, tiled=True)
        terms = terms.reshape(images // n_dp, n_tensor, n_dp * cols // n_tensor)
        parts = lax.all_to_all(terms, "tensor", split_axis=1, concat_axis=0)
        return (jnp.sum(parts.astype(F32), axis=0).astype(BF16), *others)
    parts = lax.all_to_all(
        terms.reshape(n_tensor, images // n_tensor, cols), "tensor", split_axis=0, concat_axis=0
    )
    total = jnp.sum(parts.astype(F32), axis=0).astype(BF16)
    total, *others = lax.optimization_barrier((total, *others))
    total = total.reshape(2, images // n_dp, cols)
    x = lax.axis_index("dp") % 2
    come = []
    for other in range(2):
        block = jnp.where(x == other, total[0], total[1])
        pairs = [
            ((2 * z + e) * n_tensor + t, (2 * t + (e ^ other)) * n_tensor + z)
            for z in range(line.n_z)
            for e in range(2)
            for t in range(n_tensor)
        ]
        come.append(lax.ppermute(block, ("dp", "tensor"), pairs))
    rows = jnp.where(
        x == 0, jnp.concatenate(come, axis=1), jnp.concatenate(come[::-1], axis=1)
    )
    return (rows, *others)


def shards(
    text_states,
    image_states,
    out_grad,
    text_lengths,
    query_weight,
    key_weight,
    value_weight,
    out_weight,
):
    samples, tok_rows, width = text_states.shape
    image_own = image_states.shape[1]
    line = Line()
    n_dp = line.n_dp
    n_tensor = lax.axis_size("tensor")
    dp_at, tensor_at = lax.axis_index("dp"), lax.axis_index("tensor")
    x, core = dp_at % 2, tensor_at % 2
    place = jnp.stack([dp_at // 2, x, tensor_at % 4, tensor_at]).astype(jnp.int32)
    rows = samples * tok_rows
    image_rows = samples * image_own
    images = n_dp * image_rows
    local_cols = query_weight.shape[1]
    own_width = query_weight.shape[0]
    half_cols = local_cols // 2
    shape = jax.ShapeDtypeStruct

    def tensor_swap(block, bit):
        return lax.ppermute(block, "tensor", [(t, t ^ bit) for t in range(n_tensor)])

    positions = dp_at * tok_rows + lax.iota(jnp.int32, tok_rows)
    live_rows = positions[None, :] < text_lengths[:, None]
    grad_live = jnp.where(live_rows[..., None], out_grad, jnp.zeros_like(out_grad))
    text_flat = text_states.reshape(rows, width)
    live_flat = grad_live.reshape(rows, width)
    image_flat = image_states.reshape(image_rows, width)

    gate = lax.optimization_barrier

    relayed = line.n_z == 4
    image_cols = lax.all_to_all(image_flat, "dp", split_axis=1, concat_axis=0, tiled=True)
    wo_keep = lax.dynamic_slice_in_dim(out_weight, x * half_cols, half_cols, 0)
    wo_send = lax.dynamic_slice_in_dim(out_weight, (1 - x) * half_cols, half_cols, 0)
    live_half = lax.dynamic_slice_in_dim(live_flat, core * (width // 2), width // 2, 1)
    query_weight, image_cols, wo_send = gate((query_weight, image_cols, wo_send))
    wq_moved = line.first(query_weight)
    wo_come = line.swap(wo_send)
    wq_others = [line.swap(query_weight)]
    wo_pair = jnp.concatenate([wo_keep, wo_come], axis=1)
    part_kv = jnp.concatenate(
        [matmul(image_cols, key_weight), matmul(image_cols, value_weight)], axis=1
    )
    part_kv = part_kv.reshape(n_dp, image_rows, 2 * local_cols)
    kv_own = jnp.sum(lax.all_to_all(part_kv, "dp", split_axis=0, concat_axis=0), axis=0)
    kv_own, live_half, wo_pair, wq_others[0], *wq_moved = gate(
        (kv_own.astype(BF16), live_half, wo_pair, wq_others[0], *wq_moved)
    )

    n_moved = len(wq_moved)
    planes = [(0, 1, 2), (1, 2, 3)] if relayed else [None] * n_moved
    wq_two = line.second(wq_moved)
    wo_moved = line.first(wo_pair)
    above, live_here = gate((wq_moved[0], line.swap(live_half)))
    wq_others.append(line.swap(above, planes[0]))
    kv_own, live_here, *staged = gate(
        (kv_own, live_here, *wq_others, *wq_moved, *wq_two, *wo_moved)
    )
    wq_others, staged = staged[:2], staged[2:]
    wq_moved, wq_two, wo_moved = staged[:n_moved], staged[n_moved:-n_moved], staged[-n_moved:]

    def everywhere(values):
        copies = jnp.broadcast_to(values[None], (n_dp, *values.shape))
        return lax.all_to_all(copies, "dp", split_axis=0, concat_axis=0)

    wq_last = line.third(wq_two)
    wo_two = line.second(wo_moved)
    wq_others += [line.swap(block, at) for block, at in zip(wq_moved[1:], planes[1:])]
    wq_others += [line.swap(block) for block in wq_last[:1]]
    kv_all = everywhere(kv_own).reshape(images, 2 * local_cols)
    kv_all, live_here, wo_pair, live_flat, *staged = gate(
        (kv_all, live_here, wo_pair, live_flat, *wo_two, *wq_last, *wq_others)
    )
    wo_two, staged = staged[: len(wo_two)], staged[len(wo_two) :]
    wq_last, wq_others = staged[: len(wq_last)], staged[len(wq_last) :]

    wo_last = line.third(wo_two)
    wq_others += [line.swap(block, (0, 3)) for block in wq_last[1:]]
    live_there = tensor_swap(live_here, 1)
    quarter_rows = rows // 4
    live_part = lax.dynamic_slice_in_dim(
        live_flat, (tensor_at % 4) * quarter_rows, quarter_rows, 0
    ).reshape(quarter_rows, n_dp, own_width)
    live_mine = lax.all_to_all(live_part, "dp", split_axis=1, concat_axis=0)
    live_mine = live_mine.reshape(n_dp, quarter_rows, own_width)
    live_mine, live_flat = gate((live_mine, live_flat))
    wq_blocks = [query_weight, *wq_moved, *wq_last, *wq_others]

    grad_keep, grad_send = call(
        functools.partial(grad_kernel, line),
        place,
        (live_flat, live_here, live_there, wo_pair, *wo_moved, *wo_last),
        [shape((rows, half_cols), BF16)] * 2,
        [pltpu.VMEM((rows, half_cols), F32)] * 2,
        2 * rows * width * local_cols,
    )
    text_flat, grad_keep, grad_send = gate((text_flat, grad_keep, grad_send))
    grad_come = line.swap(grad_send)
    queries, attended = call(
        functools.partial(forward_kernel, line, relayed, image_own),
        place,
        (text_flat, kv_all, *wq_blocks),
        [shape((rows, local_cols), BF16)] * 2,
        [pltpu.VMEM((rows, local_cols), F32)],
        2 * rows * width * local_cols,
    )

    att_next = [line.shift(attended, m) for m in (1, line.n_z - 1)]
    att_swapped = line.swap(attended)
    live_y = tensor_swap(live_mine, 2)

    query_grad, kv_part = call(
        functools.partial(backward_kernel, image_own),
        place,
        (queries, kv_all, grad_keep, grad_come),
        [shape((rows, local_cols), BF16), shape((images, 2 * local_cols), F32)],
        (),
        10 * images * rows * local_cols,
    )
    kv_part = kv_part.reshape(n_dp, image_rows, 2 * local_cols)
    kv_grad = jnp.sum(lax.all_to_all(kv_part, "dp", split_axis=0, concat_axis=0), axis=0)
    chunk = n_dp // n_tensor
    term = call(
        functools.partial(term_kernel, line, relayed),
        place,
        (query_grad, *wq_blocks),
        [shape((n_tensor, chunk, rows, own_width), BF16)],
        (),
        2 * rows * width * local_cols,
    )
    kv_grad, term, attended, live_y, att_swapped, *att_next = gate(
        (kv_grad.astype(BF16), term, attended, live_y, att_swapped, *att_next)
    )
    att_far = [line.shift(attended, m) for m in range(2, line.n_z - 1)]
    att_other_next = [line.swap(block) for block in att_next]

    text_parts = [term[0]]
    for k in range(n_tensor - 1, 1, -1):
        text_parts.append(tensor_swap(term[k], k))
    live_pair = jnp.stack([live_mine, live_y])
    kv_grad_all = everywhere(kv_grad).reshape(images, 2 * local_cols)
    kv_grad_all, term_core, live_pair, *third = gate(
        (kv_grad_all, term[1], live_pair, *att_other_next, *att_far)
    )
    att_other_next, att_far = third[:2], third[2:]

    att_other_far = [line.swap(block) for block in att_far]
    live_core = tensor_swap(live_pair, 1)
    text_parts.append(tensor_swap(term_core, 1))
    image_term = matmul(kv_grad_all[:, :local_cols], key_weight, BACK)
    image_term = image_term + matmul(kv_grad_all[:, local_cols:], value_weight, BACK)
    image_grad, *att_other_far = to_owner(line, image_term.astype(BF16), *att_other_far)
    image_grad = image_grad.reshape(samples, image_own, width // n_tensor)
    text_grad = functools.reduce(jnp.add, [part.astype(F32) for part in text_parts])
    text_grad = text_grad.astype(BF16).transpose(1, 0, 2)
    text_grad = text_grad.reshape(samples, tok_rows, width // n_tensor)

    att_blocks = [attended, att_next[0], *att_far, att_next[1]]
    att_others = [att_swapped, att_other_next[0], *att_other_far, att_other_next[1]]
    weight_grad = call(
        functools.partial(weight_grad_kernel, line),
        place,
        (live_pair, live_core, *att_blocks, *att_others),
        [shape((local_cols, own_width), BF16)],
        [pltpu.VMEM((local_cols, own_width), F32)],
        2 * n_dp * rows * local_cols * own_width,
    )
    return text_grad, image_grad, weight_grad


def solution(mesh):
    return jax.shard_map(
        shards,
        mesh=mesh,
        in_specs=(
            P(None, "dp", None),
            P(None, "dp", None),
            P(None, "dp", None),
            P(),
            P("dp", "tensor"),
            P("dp", "tensor"),
            P("dp", "tensor"),
            P("tensor", "dp"),
        ),
        out_specs=(P(None, "dp", "tensor"), P(None, "dp", "tensor"), P("tensor", "dp")),
        check_vma=False,
    )
```

```python
import functools

import jax
import jax.numpy as jnp
from jax import lax
from jax.experimental import pallas as pl
from jax.experimental.pallas import tpu as pltpu
from jax.sharding import PartitionSpec as P

HEAD_DIM = 128
F32 = jnp.float32
BF16 = jnp.bfloat16
BACK = (((1,), (1,)), ((), ()))
FIRST = (((0,), (0,)), ((), ()))
VMEM_LIMIT = 48 * 1024 * 1024


def matmul(a, b, dims=None):
    if dims is None:
        return jnp.dot(a, b, preferred_element_type=F32)
    return lax.dot_general(a, b, dims, preferred_element_type=F32)


class Line:
    def __init__(self):
        self.n_dp = lax.axis_size("dp")
        self.n_z = self.n_dp // 2

    def move(self, block, moves):
        pairs = [(2 * a + e, 2 * b + e) for a, b in moves for e in range(2)]
        return lax.ppermute(block, "dp", pairs)

    def swap(self, block, planes=None):
        planes = range(self.n_z) if planes is None else planes
        pairs = [(2 * a + e, 2 * a + 1 - e) for a in planes for e in range(2)]
        return lax.ppermute(block, "dp", pairs)

    def shift(self, block, distance):
        n = self.n_z
        return self.move(block, [((a + distance) % n, a) for a in range(n)])

    def first(self, block):
        if self.n_z != 4:
            return [self.shift(block, m) for m in range(1, self.n_z)]
        above = self.move(block, [(1, 0), (2, 1), (3, 2)])
        below = self.move(block, [(0, 1), (1, 2), (2, 3)])
        return [above, below]

    def second(self, moved):
        if self.n_z != 4:
            return []
        return [self.move(moved[0], [(1, 0), (2, 1)]), self.move(moved[1], [(1, 2), (2, 3)])]

    def third(self, forwarded):
        if self.n_z != 4:
            return []
        across = jnp.where(lax.axis_index("dp") < 4, forwarded[0], forwarded[1])
        return [across, self.move(across, [(1, 0), (2, 3)])]

    def slots(self, z, relayed):
        if not relayed:
            return [(m, None) for m in range(self.n_z)]
        return [
            (0, None),
            (1, z < 3),
            (3, z > 0),
            (2, None),
            (jnp.where(z == 3, 1, 3), (z == 3) | (z == 0)),
        ]


def each_block(line, place, relayed, which, body):
    z, x = place[0], place[1]
    slots = line.slots(z, relayed)
    for j, at in enumerate(which):
        m, came = slots[at]
        plane = lax.rem(z + m, line.n_z)
        for e in range(2):
            index = 2 * plane + (x if e == 0 else 1 - x)
            if came is None:
                body(j, e, index)
            else:
                pl.when(came)(functools.partial(body, j, e, index))


def columns(index, size):
    return pl.ds(pl.multiple_of(index * size, size), size)


def probabilities(query, key, image_own):
    scores = matmul(key, query, BACK) * HEAD_DIM ** (-0.5)
    image = lax.broadcasted_iota(jnp.int32, scores.shape, 0)
    token = lax.broadcasted_iota(jnp.int32, scores.shape, 1)
    image_sample = lax.rem(lax.div(image, image_own), 2)
    same = image_sample == lax.div(token, scores.shape[1] // 2)
    scores = jnp.where(same, scores, -1e30)
    peak = jnp.max(scores, axis=0, keepdims=True)
    expo = jnp.where(same, jnp.exp(scores - peak), 0.0)
    return expo / jnp.sum(expo, axis=0, keepdims=True)


def query_kernel(line, relayed, which, place, text, *refs):
    n = len(which)
    weights, total = (refs[:n], refs[n : 2 * n]), refs[-1]
    own_width = weights[0][0].shape[0]
    total[...] = jnp.zeros_like(total)

    def add(j, e, index):
        total[...] += matmul(text[:, columns(index, own_width)], weights[e][j][...])

    each_block(line, place, relayed, which, add)


def forward_kernel(line, relayed, which, image_own, place, text, kv, part, *refs):
    n = len(which)
    weights, (query_out, attended_out, total) = (refs[:n], refs[n : 2 * n]), refs[2 * n :]
    rows, cols = total.shape
    total[...] = part[...]

    def add(j, e, index):
        weight = weights[e][j]
        total[...] += matmul(text[:, columns(index, weight.shape[0])], weight[...])

    each_block(line, place, relayed, which, add)
    query_out[...] = total[...].astype(BF16)
    part_rows = rows // 4
    quarter = place[2]
    for h in range(cols // HEAD_DIM):
        at = slice(h * HEAD_DIM, (h + 1) * HEAD_DIM)
        value = kv[:, cols + h * HEAD_DIM : cols + (h + 1) * HEAD_DIM]
        prob = probabilities(query_out[:, at], kv[:, at], image_own)
        attended = matmul(prob.astype(BF16), value, FIRST).astype(BF16)
        for r in range(4):
            low_bit = (quarter + r) % 2
            high_bit = (quarter // 2 + r // 2) % 2
            start = pl.multiple_of((2 * low_bit + high_bit) * part_rows, part_rows)
            attended_out[pl.ds(start, part_rows), at] = attended[
                r * part_rows : (r + 1) * part_rows
            ]


def grad_kernel(line, which, parts, place, live, here, there, *refs):
    before, refs = refs[:parts], refs[parts:]
    weights, outs = refs[: len(which)], refs[len(which) :]
    half = line.n_dp // 2
    core = place[2] % 2
    keep, send = outs[-2:]
    keep[...] = before[0][...] if parts else jnp.zeros_like(keep)
    send[...] = before[1][...] if parts else jnp.zeros_like(send)

    def add(j, e, index):
        own_width = weights[j].shape[1] // 2
        weight = weights[j][:, e * own_width : (e + 1) * own_width]
        keep[...] += matmul(live[:, columns(index, own_width)], weight, BACK)
        inner = columns(lax.rem(index, half), own_width)
        other = jnp.where(lax.div(index, half) == core, here[:, inner], there[:, inner])
        send[...] += matmul(other, weight, BACK)

    each_block(line, place, line.n_z == 4, which, add)
    if parts:
        outs[0][...] = keep[...].astype(BF16)
        outs[1][...] = send[...].astype(BF16)


def backward_kernel(image_own, place, query, kv, keep, come, query_grad, kv_grad):
    cols = query.shape[1]
    half = cols // 2
    x = place[1]
    for h in range(cols // HEAD_DIM):
        at = slice(h * HEAD_DIM, (h + 1) * HEAD_DIM)
        value_at = slice(cols + h * HEAD_DIM, cols + (h + 1) * HEAD_DIM)
        side = h * HEAD_DIM // half
        inner = slice(h * HEAD_DIM - side * half, (h + 1) * HEAD_DIM - side * half)
        grad = jnp.where(x == side, keep[:, inner], come[:, inner])
        prob = probabilities(query[:, at], kv[:, at], image_own)
        kv_grad[:, value_at] = matmul(prob.astype(BF16), grad)
        prob_grad = matmul(kv[:, value_at], grad, BACK)
        delta = jnp.sum(prob * prob_grad, axis=0, keepdims=True)
        score_grad = (prob * (prob_grad - delta) * HEAD_DIM ** (-0.5)).astype(BF16)
        kv_grad[:, at] = matmul(score_grad, query[:, at])
        query_grad[:, at] = matmul(score_grad, kv[:, at], FIRST).astype(BF16)


def term_kernel(line, relayed, place, query_grad, *refs):
    out = refs[-1]
    n = (len(refs) - 1) // 2
    weights = (refs[:n], refs[n : 2 * n])
    chunk = out.shape[1]

    def write(i, e, index):
        term = matmul(query_grad[...], weights[e][i][...], BACK)
        member = lax.bitwise_xor(lax.div(index, chunk), place[3])
        out[member, lax.rem(index, chunk)] = term.astype(BF16)

    each_block(line, place, relayed, range(n), write)


def weight_grad_kernel(line, place, *refs):
    live, refs = refs[:2], refs[2:]
    n = (len(refs) - 2) // 2
    attended, (out, total) = (refs[:n], refs[n : 2 * n]), refs[2 * n :]
    total[...] = jnp.zeros_like(total)

    def add(i, e, index):
        block = jnp.concatenate([part[i, index] for part in live for i in range(2)], axis=0)
        term = matmul(attended[e][i][...], block, FIRST)
        total[...] += term.astype(BF16).astype(F32)

    each_block(line, place, False, range(n), add)
    out[...] = total[...].astype(BF16)


def sum_kernel(place, term, *refs):
    parts, out = refs[:-1], refs[-1]
    width = term.shape[3]
    for c in range(term.shape[1]):
        total = term[0, c].astype(F32)
        for part in parts:
            total = total + part[c].astype(F32)
        out[:, c * width : (c + 1) * width] = total.astype(BF16)


def call(kernel, place, operands, outs, scratch=(), flops=0):
    moved = sum(a.size * a.dtype.itemsize for a in (*operands, *outs))
    single = len(outs) == 1
    return pl.pallas_call(
        kernel,
        out_shape=outs[0] if single else outs,
        in_specs=[pl.BlockSpec(memory_space=pltpu.SMEM)]
        + [pl.BlockSpec(memory_space=pltpu.VMEM)] * len(operands),
        out_specs=pl.BlockSpec(memory_space=pltpu.VMEM)
        if single
        else [pl.BlockSpec(memory_space=pltpu.VMEM)] * len(outs),
        scratch_shapes=list(scratch),
        compiler_params=pltpu.CompilerParams(vmem_limit_bytes=VMEM_LIMIT),
        cost_estimate=pl.CostEstimate(flops=flops, bytes_accessed=moved, transcendentals=0),
    )(place, *operands)


def to_owner(line, terms, *others):
    n_dp, n_tensor = line.n_dp, lax.axis_size("tensor")
    images, cols = terms.shape
    if line.n_z != n_tensor:
        terms = lax.all_to_all(terms, "dp", split_axis=0, concat_axis=1, tiled=True)
        terms = terms.reshape(images // n_dp, n_tensor, n_dp * cols // n_tensor)
        parts = lax.all_to_all(terms, "tensor", split_axis=1, concat_axis=0)
        return (jnp.sum(parts.astype(F32), axis=0).astype(BF16), *others)
    parts = lax.all_to_all(
        terms.reshape(n_tensor, images // n_tensor, cols), "tensor", split_axis=0, concat_axis=0
    )
    total = jnp.sum(parts.astype(F32), axis=0).astype(BF16)
    total, *others = lax.optimization_barrier((total, *others))
    total = total.reshape(2, images // n_dp, cols)
    x = lax.axis_index("dp") % 2
    come = []
    for other in range(2):
        block = jnp.where(x == other, total[0], total[1])
        pairs = [
            ((2 * z + e) * n_tensor + t, (2 * t + (e ^ other)) * n_tensor + z)
            for z in range(line.n_z)
            for e in range(2)
            for t in range(n_tensor)
        ]
        come.append(lax.ppermute(block, ("dp", "tensor"), pairs))
    rows = jnp.where(
        x == 0, jnp.concatenate(come, axis=1), jnp.concatenate(come[::-1], axis=1)
    )
    return (rows, *others)


def shards(
    text_states,
    image_states,
    out_grad,
    text_lengths,
    query_weight,
    key_weight,
    value_weight,
    out_weight,
):
    samples, tok_rows, width = text_states.shape
    image_own = image_states.shape[1]
    line = Line()
    n_dp = line.n_dp
    n_tensor = lax.axis_size("tensor")
    dp_at, tensor_at = lax.axis_index("dp"), lax.axis_index("tensor")
    x, core = dp_at % 2, tensor_at % 2
    place = jnp.stack([dp_at // 2, x, tensor_at % 4, tensor_at]).astype(jnp.int32)
    rows = samples * tok_rows
    image_rows = samples * image_own
    images = n_dp * image_rows
    local_cols = query_weight.shape[1]
    own_width = query_weight.shape[0]
    half_cols = local_cols // 2
    shape = jax.ShapeDtypeStruct

    def tensor_swap(block, bit):
        return lax.ppermute(block, "tensor", [(t, t ^ bit) for t in range(n_tensor)])

    positions = dp_at * tok_rows + lax.iota(jnp.int32, tok_rows)
    live_rows = positions[None, :] < text_lengths[:, None]
    grad_live = jnp.where(live_rows[..., None], out_grad, jnp.zeros_like(out_grad))
    text_flat = text_states.reshape(rows, width)
    live_flat = grad_live.reshape(rows, width)
    image_flat = image_states.reshape(image_rows, width)

    gate = lax.optimization_barrier

    relayed = line.n_z == 4
    image_cols = lax.all_to_all(image_flat, "dp", split_axis=1, concat_axis=0, tiled=True)
    wo_keep = lax.dynamic_slice_in_dim(out_weight, x * half_cols, half_cols, 0)
    wo_send = lax.dynamic_slice_in_dim(out_weight, (1 - x) * half_cols, half_cols, 0)
    live_half = lax.dynamic_slice_in_dim(live_flat, core * (width // 2), width // 2, 1)
    wq_moved = line.first(query_weight)
    wo_pair = jnp.concatenate([wo_keep, line.swap(wo_send)], axis=1)
    image_cols, wo_pair, live_half, wq_other, *wq_moved = gate(
        (image_cols, wo_pair, live_half, line.swap(query_weight), *wq_moved)
    )

    n_moved = len(wq_moved)
    planes = [(0, 1, 2), (1, 2, 3)] if relayed else [None] * n_moved
    wq_two = line.second(wq_moved)
    wo_moved = line.first(wo_pair)
    above, live_here = gate((wq_moved[0], line.swap(live_half)))
    wq_others = [wq_other, line.swap(above, planes[0])]
    part_kv = jnp.concatenate(
        [matmul(image_cols, key_weight), matmul(image_cols, value_weight)], axis=1
    )
    part_kv = part_kv.reshape(n_dp, image_rows, 2 * local_cols)
    kv_own = jnp.sum(lax.all_to_all(part_kv, "dp", split_axis=0, concat_axis=0), axis=0)
    kv_own, live_here, *staged = gate(
        (kv_own.astype(BF16), live_here, *wq_others, *wq_moved, *wq_two, *wo_moved)
    )
    wq_others, staged = staged[:2], staged[2:]
    wq_moved, wq_two, wo_moved = staged[:n_moved], staged[n_moved:-n_moved], staged[-n_moved:]

    def everywhere(values):
        copies = jnp.broadcast_to(values[None], (n_dp, *values.shape))
        return lax.all_to_all(copies, "dp", split_axis=0, concat_axis=0)

    wq_last = line.third(wq_two)
    wo_two = line.second(wo_moved)
    wq_others += [line.swap(block, at) for block, at in zip(wq_moved[1:], planes[1:])]
    wq_others += [line.swap(block) for block in wq_last[:1]]
    kv_all = everywhere(kv_own).reshape(images, 2 * local_cols)
    kv_all, live_here, wo_pair, live_flat, *staged = gate(
        (kv_all, live_here, wo_pair, live_flat, *wo_two, *wq_last, *wq_others)
    )
    wo_two, staged = staged[: len(wo_two)], staged[len(wo_two) :]
    wq_last, wq_others = staged[: len(wq_last)], staged[len(wq_last) :]

    wo_last = line.third(wo_two)
    wq_others += [line.swap(block, (0, 3)) for block in wq_last[1:]]
    live_there = tensor_swap(live_here, 1)
    quarter_rows = rows // 4
    live_part = lax.dynamic_slice_in_dim(
        live_flat, (tensor_at % 4) * quarter_rows, quarter_rows, 0
    ).reshape(quarter_rows, n_dp, own_width)
    live_mine = lax.all_to_all(live_part, "dp", split_axis=1, concat_axis=0)
    live_mine = live_mine.reshape(n_dp, quarter_rows, own_width)
    arrivals = [query_weight, *wq_moved, *wq_last]
    early = range(4 if relayed else len(arrivals))
    late = range(len(early), len(arrivals))
    query_part = call(
        functools.partial(query_kernel, line, relayed, early),
        place,
        (text_flat, *arrivals[: len(early)], *wq_others[: len(early)]),
        [shape((rows, local_cols), F32)],
        (),
        2 * rows * width * local_cols,
    )
    half = shape((rows, half_cols), F32)
    wo_early = [wo_pair, *wo_moved]
    grad_parts = call(
        functools.partial(grad_kernel, line, range(len(wo_early)), 0),
        place,
        (live_flat, live_here, live_there, *wo_early),
        [half] * 2,
        (),
        rows * width * local_cols,
    )

    query_part, *grad_parts = gate((query_part, *grad_parts))

    wo_late = range(len(wo_early), len(wo_early) + len(wo_last))
    grad_keep, grad_send = call(
        functools.partial(grad_kernel, line, wo_late, 2),
        place,
        (live_flat, live_here, live_there, *grad_parts, *wo_last),
        [shape((rows, half_cols), BF16)] * 2,
        [pltpu.VMEM((rows, half_cols), F32)] * 2,
        rows * width * local_cols,
    )
    text_flat, live_mine, grad_keep, grad_send = gate(
        (text_flat, live_mine, grad_keep, grad_send)
    )
    grad_come = line.swap(grad_send)
    queries, attended = call(
        functools.partial(forward_kernel, line, relayed, late, image_own),
        place,
        (text_flat, kv_all, query_part, *arrivals[len(early) :], *wq_others[len(early) :]),
        [shape((rows, local_cols), BF16)] * 2,
        [pltpu.VMEM((rows, local_cols), F32)],
        rows * width * local_cols,
    )
    wq_blocks = [*arrivals, *wq_others]

    att_next = [line.shift(attended, m) for m in (1, line.n_z - 1)]
    att_swapped = line.swap(attended)
    live_y = tensor_swap(live_mine, 2)

    query_grad, kv_part = call(
        functools.partial(backward_kernel, image_own),
        place,
        (queries, kv_all, grad_keep, grad_come),
        [shape((rows, local_cols), BF16), shape((images, 2 * local_cols), F32)],
        (),
        10 * images * rows * local_cols,
    )
    kv_part = kv_part.reshape(n_dp, image_rows, 2 * local_cols)
    kv_grad = jnp.sum(lax.all_to_all(kv_part, "dp", split_axis=0, concat_axis=0), axis=0)
    chunk = n_dp // n_tensor
    term = call(
        functools.partial(term_kernel, line, relayed),
        place,
        (query_grad, *wq_blocks),
        [shape((n_tensor, chunk, rows, own_width), BF16)],
        (),
        2 * rows * width * local_cols,
    )
    kv_grad, term, live_y = gate((kv_grad.astype(BF16), term, live_y))

    text_parts = [tensor_swap(term[k], k) for k in range(2, n_tensor)]
    live_pair = jnp.stack([live_mine, live_y])
    kv_grad_all = everywhere(kv_grad).reshape(images, 2 * local_cols)
    kv_grad_all, term, attended, att_swapped, *staged = gate(
        (kv_grad_all, term, attended, att_swapped, *att_next, *text_parts)
    )
    att_next, text_parts = staged[:2], staged[2:]

    att_far = [line.shift(attended, m) for m in range(2, line.n_z - 1)]
    att_other_next = [line.swap(block) for block in att_next]
    live_core = tensor_swap(live_pair, 1)
    text_parts.append(tensor_swap(term[1], 1))
    image_term = matmul(kv_grad_all[:, :local_cols], key_weight, BACK)
    image_term = image_term + matmul(kv_grad_all[:, local_cols:], value_weight, BACK)
    image_grad, live_core, *staged = to_owner(
        line, image_term.astype(BF16), live_core, *text_parts, *att_other_next, *att_far
    )
    text_parts, staged = staged[: n_tensor - 1], staged[n_tensor - 1 :]
    att_other_next, att_far = staged[:2], staged[2:]
    att_other_far = [line.swap(block) for block in att_far]
    image_grad = image_grad.reshape(samples, image_own, width // n_tensor)
    text_grad = call(
        sum_kernel,
        place,
        (term, *text_parts),
        [shape((rows, width // n_tensor), BF16)],
    )
    text_grad = text_grad.reshape(samples, tok_rows, width // n_tensor)

    att_blocks = [attended, att_next[0], *att_far, att_next[1]]
    att_others = [att_swapped, att_other_next[0], *att_other_far, att_other_next[1]]
    weight_grad = call(
        functools.partial(weight_grad_kernel, line),
        place,
        (live_pair, live_core, *att_blocks, *att_others),
        [shape((local_cols, own_width), BF16)],
        [pltpu.VMEM((local_cols, own_width), F32)],
        2 * n_dp * rows * local_cols * own_width,
    )
    return text_grad, image_grad, weight_grad


def solution(mesh):
    return jax.shard_map(
        shards,
        mesh=mesh,
        in_specs=(
            P(None, "dp", None),
            P(None, "dp", None),
            P(None, "dp", None),
            P(),
            P("dp", "tensor"),
            P("dp", "tensor"),
            P("dp", "tensor"),
            P("tensor", "dp"),
        ),
        out_specs=(P(None, "dp", "tensor"), P(None, "dp", "tensor"), P("tensor", "dp")),
        check_vma=False,
    )
```

```python
import functools

import jax
import jax.numpy as jnp
from jax import lax
from jax.experimental import pallas as pl
from jax.experimental.pallas import tpu as pltpu
from jax.sharding import PartitionSpec as P

HEAD_DIM = 128
F32 = jnp.float32
BF16 = jnp.bfloat16
BACK = (((1,), (1,)), ((), ()))
FIRST = (((0,), (0,)), ((), ()))
VMEM_LIMIT = 48 * 1024 * 1024


def matmul(a, b, dims=None):
    if dims is None:
        return jnp.dot(a, b, preferred_element_type=F32)
    return lax.dot_general(a, b, dims, preferred_element_type=F32)


class Line:
    def __init__(self):
        self.n_dp = lax.axis_size("dp")
        self.n_z = self.n_dp // 2

    def move(self, block, moves):
        pairs = [(2 * a + e, 2 * b + e) for a, b in moves for e in range(2)]
        return lax.ppermute(block, "dp", pairs)

    def swap(self, block, planes=None):
        planes = range(self.n_z) if planes is None else planes
        pairs = [(2 * a + e, 2 * a + 1 - e) for a in planes for e in range(2)]
        return lax.ppermute(block, "dp", pairs)

    def shift(self, block, distance):
        n = self.n_z
        return self.move(block, [((a + distance) % n, a) for a in range(n)])

    def first(self, block):
        if self.n_z != 4:
            return [self.shift(block, m) for m in range(1, self.n_z)]
        above = self.move(block, [(1, 0), (2, 1), (3, 2)])
        below = self.move(block, [(0, 1), (1, 2), (2, 3)])
        return [above, below]

    def second(self, moved):
        if self.n_z != 4:
            return []
        return [self.move(moved[0], [(1, 0), (2, 1)]), self.move(moved[1], [(1, 2), (2, 3)])]

    def third(self, forwarded):
        if self.n_z != 4:
            return []
        across = jnp.where(lax.axis_index("dp") < 4, forwarded[0], forwarded[1])
        return [across, self.move(across, [(1, 0), (2, 3)])]

    def slots(self, z, relayed):
        if not relayed:
            return [(m, None) for m in range(self.n_z)]
        return [
            (0, None),
            (1, z < 3),
            (3, z > 0),
            (2, None),
            (jnp.where(z == 3, 1, 3), (z == 3) | (z == 0)),
        ]


def each_block(line, place, relayed, which, body):
    z, x = place[0], place[1]
    slots = line.slots(z, relayed)
    for j, at in enumerate(which):
        m, came = slots[at]
        plane = lax.rem(z + m, line.n_z)
        for e in range(2):
            index = 2 * plane + (x if e == 0 else 1 - x)
            if came is None:
                body(j, e, index)
            else:
                pl.when(came)(functools.partial(body, j, e, index))


def columns(index, size):
    return pl.ds(pl.multiple_of(index * size, size), size)


def probabilities(query, key, image_own):
    scores = matmul(key, query, BACK) * HEAD_DIM ** (-0.5)
    image = lax.broadcasted_iota(jnp.int32, scores.shape, 0)
    token = lax.broadcasted_iota(jnp.int32, scores.shape, 1)
    image_sample = lax.rem(lax.div(image, image_own), 2)
    same = image_sample == lax.div(token, scores.shape[1] // 2)
    scores = jnp.where(same, scores, -1e30)
    peak = jnp.max(scores, axis=0, keepdims=True)
    expo = jnp.where(same, jnp.exp(scores - peak), 0.0)
    return expo / jnp.sum(expo, axis=0, keepdims=True)


def query_kernel(line, relayed, which, place, text, *refs):
    n = len(which)
    weights, total = (refs[:n], refs[n : 2 * n]), refs[-1]
    own_width = weights[0][0].shape[0]
    total[...] = jnp.zeros_like(total)

    def add(j, e, index):
        total[...] += matmul(text[:, columns(index, own_width)], weights[e][j][...])

    each_block(line, place, relayed, which, add)


def forward_kernel(line, relayed, which, image_own, place, text, kv, part, *refs):
    n = len(which)
    weights, (query_out, attended_out, total) = (refs[:n], refs[n : 2 * n]), refs[2 * n :]
    rows, cols = total.shape
    total[...] = part[...]

    def add(j, e, index):
        weight = weights[e][j]
        total[...] += matmul(text[:, columns(index, weight.shape[0])], weight[...])

    each_block(line, place, relayed, which, add)
    query_out[...] = total[...].astype(BF16)
    part_rows = rows // 4
    quarter = place[2]
    for h in range(cols // HEAD_DIM):
        at = slice(h * HEAD_DIM, (h + 1) * HEAD_DIM)
        value = kv[:, cols + h * HEAD_DIM : cols + (h + 1) * HEAD_DIM]
        prob = probabilities(query_out[:, at], kv[:, at], image_own)
        attended = matmul(prob.astype(BF16), value, FIRST).astype(BF16)
        for r in range(4):
            low_bit = (quarter + r) % 2
            high_bit = (quarter // 2 + r // 2) % 2
            start = pl.multiple_of((2 * low_bit + high_bit) * part_rows, part_rows)
            attended_out[pl.ds(start, part_rows), at] = attended[
                r * part_rows : (r + 1) * part_rows
            ]


def grad_kernel(line, which, parts, place, live, mine, by_core, by_y, by_both, *refs):
    before, refs = refs[:parts], refs[parts:]
    weights, outs = refs[: len(which)], refs[len(which) :]
    cut = line.n_dp // 4
    keep, send = outs[-2:]
    keep[...] = before[0][...] if parts else jnp.zeros_like(keep)
    send[...] = before[1][...] if parts else jnp.zeros_like(send)

    def add(j, e, index):
        own_width = weights[j].shape[1] // 2
        weight = weights[j][:, e * own_width : (e + 1) * own_width]
        keep[...] += matmul(live[:, columns(index, own_width)], weight, BACK)
        inner = columns(lax.rem(index, cut), own_width)
        member = lax.bitwise_xor(lax.div(index, cut), place[2])
        other = mine[:, inner]
        for at, piece in ((1, by_core), (2, by_y), (3, by_both)):
            other = jnp.where(member == at, piece[:, inner], other)
        send[...] += matmul(other, weight, BACK)

    each_block(line, place, line.n_z == 4, which, add)
    if parts:
        outs[0][...] = keep[...].astype(BF16)
        outs[1][...] = send[...].astype(BF16)


def backward_kernel(image_own, place, query, kv, keep, come, query_grad, kv_grad):
    cols = query.shape[1]
    half = cols // 2
    x = place[1]
    for h in range(cols // HEAD_DIM):
        at = slice(h * HEAD_DIM, (h + 1) * HEAD_DIM)
        value_at = slice(cols + h * HEAD_DIM, cols + (h + 1) * HEAD_DIM)
        side = h * HEAD_DIM // half
        inner = slice(h * HEAD_DIM - side * half, (h + 1) * HEAD_DIM - side * half)
        grad = jnp.where(x == side, keep[:, inner], come[:, inner])
        prob = probabilities(query[:, at], kv[:, at], image_own)
        kv_grad[:, value_at] = matmul(prob.astype(BF16), grad)
        prob_grad = matmul(kv[:, value_at], grad, BACK)
        delta = jnp.sum(prob * prob_grad, axis=0, keepdims=True)
        score_grad = (prob * (prob_grad - delta) * HEAD_DIM ** (-0.5)).astype(BF16)
        kv_grad[:, at] = matmul(score_grad, query[:, at])
        query_grad[:, at] = matmul(score_grad, kv[:, at], FIRST).astype(BF16)


def term_kernel(line, relayed, place, query_grad, *refs):
    out = refs[-1]
    n = (len(refs) - 1) // 2
    weights = (refs[:n], refs[n : 2 * n])
    chunk = out.shape[1]

    def write(i, e, index):
        term = matmul(query_grad[...], weights[e][i][...], BACK)
        member = lax.bitwise_xor(lax.div(index, chunk), place[3])
        out[member, lax.rem(index, chunk)] = term.astype(BF16)

    each_block(line, place, relayed, range(n), write)


def weight_grad_kernel(line, place, *refs):
    live, refs = refs[:2], refs[2:]
    n = (len(refs) - 2) // 2
    attended, (out, total) = (refs[:n], refs[n : 2 * n]), refs[2 * n :]
    total[...] = jnp.zeros_like(total)

    def add(i, e, index):
        block = jnp.concatenate([part[i, index] for part in live for i in range(2)], axis=0)
        term = matmul(attended[e][i][...], block, FIRST)
        total[...] += term.astype(BF16).astype(F32)

    each_block(line, place, False, range(n), add)
    out[...] = total[...].astype(BF16)


def sum_kernel(place, term, *refs):
    parts, out = refs[:-1], refs[-1]
    width = term.shape[3]
    for c in range(term.shape[1]):
        total = term[0, c].astype(F32)
        for part in parts:
            total = total + part[c].astype(F32)
        out[:, c * width : (c + 1) * width] = total.astype(BF16)


def call(kernel, place, operands, outs, scratch=(), flops=0):
    moved = sum(a.size * a.dtype.itemsize for a in (*operands, *outs))
    single = len(outs) == 1
    return pl.pallas_call(
        kernel,
        out_shape=outs[0] if single else outs,
        in_specs=[pl.BlockSpec(memory_space=pltpu.SMEM)]
        + [pl.BlockSpec(memory_space=pltpu.VMEM)] * len(operands),
        out_specs=pl.BlockSpec(memory_space=pltpu.VMEM)
        if single
        else [pl.BlockSpec(memory_space=pltpu.VMEM)] * len(outs),
        scratch_shapes=list(scratch),
        compiler_params=pltpu.CompilerParams(vmem_limit_bytes=VMEM_LIMIT),
        cost_estimate=pl.CostEstimate(flops=flops, bytes_accessed=moved, transcendentals=0),
    )(place, *operands)


def to_owner(line, terms, *others):
    n_dp, n_tensor = line.n_dp, lax.axis_size("tensor")
    images, cols = terms.shape
    if line.n_z != n_tensor:
        terms = lax.all_to_all(terms, "dp", split_axis=0, concat_axis=1, tiled=True)
        terms = terms.reshape(images // n_dp, n_tensor, n_dp * cols // n_tensor)
        parts = lax.all_to_all(terms, "tensor", split_axis=1, concat_axis=0)
        return (jnp.sum(parts.astype(F32), axis=0).astype(BF16), *others)
    parts = lax.all_to_all(
        terms.reshape(n_tensor, images // n_tensor, cols), "tensor", split_axis=0, concat_axis=0
    )
    total = jnp.sum(parts.astype(F32), axis=0).astype(BF16)
    total, *others = lax.optimization_barrier((total, *others))
    total = total.reshape(2, images // n_dp, cols)
    x = lax.axis_index("dp") % 2
    come = []
    for other in range(2):
        block = jnp.where(x == other, total[0], total[1])
        pairs = [
            ((2 * z + e) * n_tensor + t, (2 * t + (e ^ other)) * n_tensor + z)
            for z in range(line.n_z)
            for e in range(2)
            for t in range(n_tensor)
        ]
        come.append(lax.ppermute(block, ("dp", "tensor"), pairs))
    rows = jnp.where(
        x == 0, jnp.concatenate(come, axis=1), jnp.concatenate(come[::-1], axis=1)
    )
    return (rows, *others)


def shards(
    text_states,
    image_states,
    out_grad,
    text_lengths,
    query_weight,
    key_weight,
    value_weight,
    out_weight,
):
    samples, tok_rows, width = text_states.shape
    image_own = image_states.shape[1]
    line = Line()
    n_dp = line.n_dp
    n_tensor = lax.axis_size("tensor")
    dp_at, tensor_at = lax.axis_index("dp"), lax.axis_index("tensor")
    x, quarter = dp_at % 2, tensor_at % 4
    place = jnp.stack([dp_at // 2, x, quarter, tensor_at]).astype(jnp.int32)
    rows = samples * tok_rows
    image_rows = samples * image_own
    images = n_dp * image_rows
    local_cols = query_weight.shape[1]
    own_width = query_weight.shape[0]
    half_cols = local_cols // 2
    shape = jax.ShapeDtypeStruct

    def tensor_swap(block, bit):
        return lax.ppermute(block, "tensor", [(t, t ^ bit) for t in range(n_tensor)])

    positions = dp_at * tok_rows + lax.iota(jnp.int32, tok_rows)
    live_rows = positions[None, :] < text_lengths[:, None]
    grad_live = jnp.where(live_rows[..., None], out_grad, jnp.zeros_like(out_grad))
    text_flat = text_states.reshape(rows, width)
    live_flat = grad_live.reshape(rows, width)
    image_flat = image_states.reshape(image_rows, width)

    gate = lax.optimization_barrier

    relayed = line.n_z == 4
    wq_moved = line.first(query_weight)
    image_cols = lax.all_to_all(image_flat, "dp", split_axis=1, concat_axis=0, tiled=True)
    wo_keep = lax.dynamic_slice_in_dim(out_weight, x * half_cols, half_cols, 0)
    wo_send = lax.dynamic_slice_in_dim(out_weight, (1 - x) * half_cols, half_cols, 0)
    wo_pair = jnp.concatenate([wo_keep, line.swap(wo_send)], axis=1)
    quarter_cols = width // 4
    live_part = lax.dynamic_slice_in_dim(live_flat, quarter * quarter_cols, quarter_cols, 1)
    live_here = line.swap(live_part)
    quarter_rows = rows // 4
    live_rows = lax.dynamic_slice_in_dim(live_flat, quarter * quarter_rows, quarter_rows, 0)
    live_mine = lax.all_to_all(
        live_rows.reshape(quarter_rows, n_dp, own_width), "dp", split_axis=1, concat_axis=0
    )
    live_mine = live_mine.reshape(n_dp, quarter_rows, own_width)
    image_cols, wo_pair, live_here, live_mine, query_weight, *wq_moved = gate(
        (image_cols, wo_pair, live_here, live_mine, query_weight, *wq_moved)
    )

    n_moved = len(wq_moved)
    planes = [(0, 1, 2), (1, 2, 3)] if relayed else [None] * n_moved
    wq_two = line.second(wq_moved)
    wo_moved = line.first(wo_pair)
    above, wq_other = gate((wq_moved[0], line.swap(query_weight)))
    wq_others = [wq_other, line.swap(above, planes[0])]
    part_kv = jnp.concatenate(
        [matmul(image_cols, key_weight), matmul(image_cols, value_weight)], axis=1
    )
    part_kv = part_kv.reshape(n_dp, image_rows, 2 * local_cols)
    kv_own = jnp.sum(lax.all_to_all(part_kv, "dp", split_axis=0, concat_axis=0), axis=0)
    kv_own, live_here, *staged = gate(
        (kv_own.astype(BF16), live_here, *wq_others, *wq_moved, *wq_two, *wo_moved)
    )
    wq_others, staged = staged[:2], staged[2:]
    wq_moved, wq_two, wo_moved = staged[:n_moved], staged[n_moved:-n_moved], staged[-n_moved:]

    def everywhere(values):
        copies = jnp.broadcast_to(values[None], (n_dp, *values.shape))
        return lax.all_to_all(copies, "dp", split_axis=0, concat_axis=0)

    wq_last = line.third(wq_two)
    wo_two = line.second(wo_moved)
    wq_others += [line.swap(block, at) for block, at in zip(wq_moved[1:], planes[1:])]
    wq_others += [line.swap(block) for block in wq_last[:1]]
    kv_own, *wq_edge = gate((kv_own, *wq_last[1:]))
    kv_all = everywhere(kv_own).reshape(images, 2 * local_cols)
    edge_other = [line.swap(block, (0, 3)) for block in wq_edge]
    kv_all, live_here, wo_pair, live_flat, *staged = gate(
        (kv_all, live_here, wo_pair, live_flat, *wo_two, *wq_edge, *wq_others)
    )
    wo_two, staged = staged[: len(wo_two)], staged[len(wo_two) :]
    wq_last[1:], wq_others = staged[: len(wq_edge)], staged[len(wq_edge) :]

    wo_last = line.third(wo_two)
    by_y = tensor_swap(live_here, 2)
    live_pieces = [live_here, tensor_swap(live_here, 1), by_y, tensor_swap(by_y, 1)]
    wq_others += edge_other
    arrivals = [query_weight, *wq_moved, *wq_last]
    early = range(4 if relayed else len(arrivals))
    late = range(len(early), len(arrivals))
    query_part = call(
        functools.partial(query_kernel, line, relayed, early),
        place,
        (text_flat, *arrivals[: len(early)], *wq_others[: len(early)]),
        [shape((rows, local_cols), F32)],
        (),
        2 * rows * width * local_cols,
    )
    half = shape((rows, half_cols), F32)
    wo_early = [wo_pair, *wo_moved]
    grad_parts = call(
        functools.partial(grad_kernel, line, range(len(wo_early)), 0),
        place,
        (live_flat, *live_pieces, *wo_early),
        [half] * 2,
        (),
        rows * width * local_cols,
    )

    query_part, *grad_parts = gate((query_part, *grad_parts))

    wo_late = range(len(wo_early), len(wo_early) + len(wo_last))
    grad_keep, grad_send = call(
        functools.partial(grad_kernel, line, wo_late, 2),
        place,
        (live_flat, *live_pieces, *grad_parts, *wo_last),
        [shape((rows, half_cols), BF16)] * 2,
        [pltpu.VMEM((rows, half_cols), F32)] * 2,
        rows * width * local_cols,
    )
    text_flat, live_mine, grad_keep, grad_send = gate(
        (text_flat, live_mine, grad_keep, grad_send)
    )
    grad_come = line.swap(grad_send)
    queries, attended = call(
        functools.partial(forward_kernel, line, relayed, late, image_own),
        place,
        (text_flat, kv_all, query_part, *arrivals[len(early) :], *wq_others[len(early) :]),
        [shape((rows, local_cols), BF16)] * 2,
        [pltpu.VMEM((rows, local_cols), F32)],
        rows * width * local_cols,
    )
    wq_blocks = [*arrivals, *wq_others]

    att_next = [line.shift(attended, m) for m in (1, line.n_z - 1)]
    att_swapped = line.swap(attended)
    live_y = tensor_swap(live_mine, 2)

    query_grad, kv_part = call(
        functools.partial(backward_kernel, image_own),
        place,
        (queries, kv_all, grad_keep, grad_come),
        [shape((rows, local_cols), BF16), shape((images, 2 * local_cols), F32)],
        (),
        10 * images * rows * local_cols,
    )
    kv_part = kv_part.reshape(n_dp, image_rows, 2 * local_cols)
    kv_grad = jnp.sum(lax.all_to_all(kv_part, "dp", split_axis=0, concat_axis=0), axis=0)
    chunk = n_dp // n_tensor
    term = call(
        functools.partial(term_kernel, line, relayed),
        place,
        (query_grad, *wq_blocks),
        [shape((n_tensor, chunk, rows, own_width), BF16)],
        (),
        2 * rows * width * local_cols,
    )
    kv_grad, term, live_mine, live_y = gate((kv_grad.astype(BF16), term, live_mine, live_y))
    kv_grad_all = everywhere(kv_grad).reshape(images, 2 * local_cols)
    live_pair = jnp.stack([live_mine, live_y])

    text_parts = [tensor_swap(term[k], k) for k in range(2, n_tensor)]
    attended, att_swapped, *att_next = gate((attended, att_swapped, *att_next))
    att_far = [line.shift(attended, m) for m in range(2, line.n_z - 1)]
    att_other_next = [line.swap(block) for block in att_next]
    kv_grad_all, live_pair, *staged = gate((kv_grad_all, live_pair, *text_parts, *att_far))
    text_parts, att_far = staged[: n_tensor - 2], staged[n_tensor - 2 :]

    live_core = tensor_swap(live_pair, 1)
    text_parts.append(tensor_swap(term[1], 1))
    image_term = matmul(kv_grad_all[:, :local_cols], key_weight, BACK)
    image_term = image_term + matmul(kv_grad_all[:, local_cols:], value_weight, BACK)
    image_grad, live_core, *staged = to_owner(
        line, image_term.astype(BF16), live_core, *text_parts, *att_other_next, *att_far
    )
    text_parts, staged = staged[: n_tensor - 1], staged[n_tensor - 1 :]
    att_other_next, att_far = staged[:2], staged[2:]
    att_other_far = [line.swap(block) for block in att_far]
    image_grad = image_grad.reshape(samples, image_own, width // n_tensor)
    text_grad = call(
        sum_kernel,
        place,
        (term, *text_parts),
        [shape((rows, width // n_tensor), BF16)],
    )
    text_grad = text_grad.reshape(samples, tok_rows, width // n_tensor)

    att_blocks = [attended, att_next[0], *att_far, att_next[1]]
    att_others = [att_swapped, att_other_next[0], *att_other_far, att_other_next[1]]
    weight_grad = call(
        functools.partial(weight_grad_kernel, line),
        place,
        (live_pair, live_core, *att_blocks, *att_others),
        [shape((local_cols, own_width), BF16)],
        [pltpu.VMEM((local_cols, own_width), F32)],
        2 * n_dp * rows * local_cols * own_width,
    )
    return text_grad, image_grad, weight_grad


def solution(mesh):
    return jax.shard_map(
        shards,
        mesh=mesh,
        in_specs=(
            P(None, "dp", None),
            P(None, "dp", None),
            P(None, "dp", None),
            P(),
            P("dp", "tensor"),
            P("dp", "tensor"),
            P("dp", "tensor"),
            P("tensor", "dp"),
        ),
        out_specs=(P(None, "dp", "tensor"), P(None, "dp", "tensor"), P("tensor", "dp")),
        check_vma=False,
    )
```

```python
import functools

import jax
import jax.numpy as jnp
from jax import lax
from jax.experimental import pallas as pl
from jax.experimental.pallas import tpu as pltpu
from jax.sharding import PartitionSpec as P

HEAD_DIM = 128
F32 = jnp.float32
BF16 = jnp.bfloat16
BACK = (((1,), (1,)), ((), ()))
FIRST = (((0,), (0,)), ((), ()))
VMEM_LIMIT = 60 * 1024 * 1024


def matmul(a, b, dims=None):
    if dims is None:
        return jnp.dot(a, b, preferred_element_type=F32)
    return lax.dot_general(a, b, dims, preferred_element_type=F32)


class Line:
    def __init__(self):
        self.n_dp = lax.axis_size("dp")
        self.n_z = self.n_dp // 2

    def move(self, block, moves):
        pairs = [(2 * a + e, 2 * b + e) for a, b in moves for e in range(2)]
        return lax.ppermute(block, "dp", pairs)

    def swap(self, block, planes=None):
        planes = range(self.n_z) if planes is None else planes
        pairs = [(2 * a + e, 2 * a + 1 - e) for a in planes for e in range(2)]
        return lax.ppermute(block, "dp", pairs)

    def shift(self, block, distance):
        n = self.n_z
        return self.move(block, [((a + distance) % n, a) for a in range(n)])

    def first(self, block):
        if self.n_z != 4:
            return [self.shift(block, m) for m in range(1, self.n_z)]
        above = self.move(block, [(1, 0), (2, 1), (3, 2)])
        below = self.move(block, [(0, 1), (1, 2), (2, 3)])
        return [above, below]

    def second(self, moved):
        if self.n_z != 4:
            return []
        return [self.move(moved[0], [(1, 0), (2, 1)]), self.move(moved[1], [(1, 2), (2, 3)])]

    def third(self, forwarded):
        if self.n_z != 4:
            return []
        across = jnp.where(lax.axis_index("dp") < 4, forwarded[0], forwarded[1])
        return [across, self.move(across, [(1, 0), (2, 3)])]

    def slots(self, z, relayed):
        if not relayed:
            return [(m, None) for m in range(self.n_z)]
        return [
            (0, None),
            (1, z < 3),
            (3, z > 0),
            (2, None),
            (jnp.where(z == 3, 1, 3), (z == 3) | (z == 0)),
        ]


def each_block(line, place, relayed, which, body):
    z, x = place[0], place[1]
    slots = line.slots(z, relayed)
    for j, at in enumerate(which):
        m, came = slots[at]
        plane = lax.rem(z + m, line.n_z)
        for e in range(2):
            index = 2 * plane + (x if e == 0 else 1 - x)
            if came is None:
                body(j, e, index)
            else:
                pl.when(came)(functools.partial(body, j, e, index))


def columns(index, size):
    return pl.ds(pl.multiple_of(index * size, size), size)


def probabilities(query, key, image_own):
    scores = matmul(key, query, BACK) * HEAD_DIM ** (-0.5)
    image = lax.broadcasted_iota(jnp.int32, scores.shape, 0)
    token = lax.broadcasted_iota(jnp.int32, scores.shape, 1)
    image_sample = lax.rem(lax.div(image, image_own), 2)
    same = image_sample == lax.div(token, scores.shape[1] // 2)
    scores = jnp.where(same, scores, -1e30)
    peak = jnp.max(scores, axis=0, keepdims=True)
    expo = jnp.where(same, jnp.exp(scores - peak), 0.0)
    return expo / jnp.sum(expo, axis=0, keepdims=True)


def query_kernel(line, relayed, which, place, text, *refs):
    n = len(which)
    weights, total = (refs[:n], refs[n : 2 * n]), refs[-1]
    own_width = weights[0][0].shape[0]
    total[...] = jnp.zeros_like(total)

    def add(j, e, index):
        total[...] += matmul(text[:, columns(index, own_width)], weights[e][j][...])

    each_block(line, place, relayed, which, add)


def forward_kernel(line, relayed, which, image_own, place, text, kv, part, *refs):
    n = len(which)
    weights, (query_out, attended_out, total) = (refs[:n], refs[n : 2 * n]), refs[2 * n :]
    rows, cols = total.shape
    total[...] = part[...]

    def add(j, e, index):
        weight = weights[e][j]
        total[...] += matmul(text[:, columns(index, weight.shape[0])], weight[...])

    each_block(line, place, relayed, which, add)
    query_out[...] = total[...].astype(BF16)
    part_rows = rows // 4
    quarter = place[2]
    for h in range(cols // HEAD_DIM):
        at = slice(h * HEAD_DIM, (h + 1) * HEAD_DIM)
        value = kv[:, cols + h * HEAD_DIM : cols + (h + 1) * HEAD_DIM]
        prob = probabilities(query_out[:, at], kv[:, at], image_own)
        attended = matmul(prob.astype(BF16), value, FIRST).astype(BF16)
        for r in range(4):
            low_bit = (quarter + r) % 2
            high_bit = (quarter // 2 + r // 2) % 2
            start = pl.multiple_of((2 * low_bit + high_bit) * part_rows, part_rows)
            attended_out[pl.ds(start, part_rows), at] = attended[
                r * part_rows : (r + 1) * part_rows
            ]


def grad_kernel(line, which, parts, place, live, mine, by_core, by_y, by_both, *refs):
    before, refs = refs[:parts], refs[parts:]
    weights, outs = refs[: len(which)], refs[len(which) :]
    cut = line.n_dp // 4
    keep, send = outs[-2:]
    keep[...] = before[0][...] if parts else jnp.zeros_like(keep)
    send[...] = before[1][...] if parts else jnp.zeros_like(send)

    def add(j, e, index):
        own_width = weights[j].shape[1] // 2
        weight = weights[j][:, e * own_width : (e + 1) * own_width]
        keep[...] += matmul(live[:, columns(index, own_width)], weight, BACK)
        inner = columns(lax.rem(index, cut), own_width)
        member = lax.bitwise_xor(lax.div(index, cut), place[2])
        other = mine[:, inner]
        for at, piece in ((1, by_core), (2, by_y), (3, by_both)):
            other = jnp.where(member == at, piece[:, inner], other)
        send[...] += matmul(other, weight, BACK)

    each_block(line, place, line.n_z == 4, which, add)
    if parts:
        outs[0][...] = keep[...].astype(BF16)
        outs[1][...] = send[...].astype(BF16)


def backward_kernel(image_own, place, query, kv, keep, come, query_grad, kv_grad):
    cols = query.shape[1]
    half = cols // 2
    x = place[1]
    for h in range(cols // HEAD_DIM):
        at = slice(h * HEAD_DIM, (h + 1) * HEAD_DIM)
        value_at = slice(cols + h * HEAD_DIM, cols + (h + 1) * HEAD_DIM)
        side = h * HEAD_DIM // half
        inner = slice(h * HEAD_DIM - side * half, (h + 1) * HEAD_DIM - side * half)
        grad = jnp.where(x == side, keep[:, inner], come[:, inner])
        prob = probabilities(query[:, at], kv[:, at], image_own)
        kv_grad[:, value_at] = matmul(prob.astype(BF16), grad)
        prob_grad = matmul(kv[:, value_at], grad, BACK)
        delta = jnp.sum(prob * prob_grad, axis=0, keepdims=True)
        score_grad = (prob * (prob_grad - delta) * HEAD_DIM ** (-0.5)).astype(BF16)
        kv_grad[:, at] = matmul(score_grad, query[:, at])
        query_grad[:, at] = matmul(score_grad, kv[:, at], FIRST).astype(BF16)


def term_kernel(line, relayed, place, query_grad, *refs):
    out = refs[-1]
    n = (len(refs) - 1) // 2
    weights = (refs[:n], refs[n : 2 * n])
    chunk = out.shape[1]

    def write(i, e, index):
        term = matmul(query_grad[...], weights[e][i][...], BACK)
        out[lax.div(index, chunk), lax.rem(index, chunk)] = term.astype(BF16)

    each_block(line, place, relayed, range(n), write)


def weight_grad_kernel(line, place, *refs):
    live, refs = refs[:2], refs[2:]
    n = (len(refs) - 2) // 2
    attended, (out, total) = (refs[:n], refs[n : 2 * n]), refs[2 * n :]
    total[...] = jnp.zeros_like(total)

    def add(i, e, index):
        block = jnp.concatenate([part[i, index] for part in live for i in range(2)], axis=0)
        term = matmul(attended[e][i][...], block, FIRST)
        total[...] += term.astype(BF16).astype(F32)

    each_block(line, place, False, range(n), add)
    out[...] = total[...].astype(BF16)


def sum_kernel(place, parts, out):
    width = parts.shape[3]
    for c in range(parts.shape[1]):
        total = parts[0, c].astype(F32)
        for k in range(1, parts.shape[0]):
            total = total + parts[k, c].astype(F32)
        out[:, c * width : (c + 1) * width] = total.astype(BF16)


def call(kernel, place, operands, outs, scratch=(), flops=0):
    moved = sum(a.size * a.dtype.itemsize for a in (*operands, *outs))
    single = len(outs) == 1
    return pl.pallas_call(
        kernel,
        out_shape=outs[0] if single else outs,
        in_specs=[pl.BlockSpec(memory_space=pltpu.SMEM)]
        + [pl.BlockSpec(memory_space=pltpu.VMEM)] * len(operands),
        out_specs=pl.BlockSpec(memory_space=pltpu.VMEM)
        if single
        else [pl.BlockSpec(memory_space=pltpu.VMEM)] * len(outs),
        scratch_shapes=list(scratch),
        compiler_params=pltpu.CompilerParams(vmem_limit_bytes=VMEM_LIMIT),
        cost_estimate=pl.CostEstimate(flops=flops, bytes_accessed=moved, transcendentals=0),
    )(place, *operands)


def to_owner(line, terms, *others):
    n_dp, n_tensor = line.n_dp, lax.axis_size("tensor")
    images, cols = terms.shape
    if line.n_z != n_tensor:
        terms = lax.all_to_all(terms, "dp", split_axis=0, concat_axis=1, tiled=True)
        terms = terms.reshape(images // n_dp, n_tensor, n_dp * cols // n_tensor)
        parts = lax.all_to_all(terms, "tensor", split_axis=1, concat_axis=0)
        return (jnp.sum(parts.astype(F32), axis=0).astype(BF16), *others)
    parts = lax.all_to_all(
        terms.reshape(n_tensor, images // n_tensor, cols), "tensor", split_axis=0, concat_axis=0
    )
    total = jnp.sum(parts.astype(F32), axis=0).astype(BF16)
    total, *others = lax.optimization_barrier((total, *others))
    total = total.reshape(2, images // n_dp, cols)
    x = lax.axis_index("dp") % 2
    come = []
    for other in range(2):
        block = jnp.where(x == other, total[0], total[1])
        pairs = [
            ((2 * z + e) * n_tensor + t, (2 * t + (e ^ other)) * n_tensor + z)
            for z in range(line.n_z)
            for e in range(2)
            for t in range(n_tensor)
        ]
        come.append(lax.ppermute(block, ("dp", "tensor"), pairs))
    rows = jnp.where(
        x == 0, jnp.concatenate(come, axis=1), jnp.concatenate(come[::-1], axis=1)
    )
    return (rows, *others)


def shards(
    text_states,
    image_states,
    out_grad,
    text_lengths,
    query_weight,
    key_weight,
    value_weight,
    out_weight,
):
    samples, tok_rows, width = text_states.shape
    image_own = image_states.shape[1]
    line = Line()
    n_dp = line.n_dp
    n_tensor = lax.axis_size("tensor")
    dp_at, tensor_at = lax.axis_index("dp"), lax.axis_index("tensor")
    x, quarter = dp_at % 2, tensor_at % 4
    place = jnp.stack([dp_at // 2, x, quarter, tensor_at]).astype(jnp.int32)
    rows = samples * tok_rows
    image_rows = samples * image_own
    images = n_dp * image_rows
    local_cols = query_weight.shape[1]
    own_width = query_weight.shape[0]
    half_cols = local_cols // 2
    shape = jax.ShapeDtypeStruct

    def tensor_swap(block, bit):
        return lax.ppermute(block, "tensor", [(t, t ^ bit) for t in range(n_tensor)])

    positions = dp_at * tok_rows + lax.iota(jnp.int32, tok_rows)
    live_rows = positions[None, :] < text_lengths[:, None]
    grad_live = jnp.where(live_rows[..., None], out_grad, jnp.zeros_like(out_grad))
    text_flat = text_states.reshape(rows, width)
    live_flat = grad_live.reshape(rows, width)
    image_flat = image_states.reshape(image_rows, width)

    gate = lax.optimization_barrier

    relayed = line.n_z == 4
    wq_moved = line.first(query_weight)
    image_cols = lax.all_to_all(image_flat, "dp", split_axis=1, concat_axis=0, tiled=True)
    wo_keep = lax.dynamic_slice_in_dim(out_weight, x * half_cols, half_cols, 0)
    wo_send = lax.dynamic_slice_in_dim(out_weight, (1 - x) * half_cols, half_cols, 0)
    wo_pair = jnp.concatenate([wo_keep, line.swap(wo_send)], axis=1)
    quarter_cols = width // 4
    live_part = lax.dynamic_slice_in_dim(live_flat, quarter * quarter_cols, quarter_cols, 1)
    live_here = line.swap(live_part)
    image_cols, wo_pair, live_here, live_flat, query_weight, *wq_moved = gate(
        (image_cols, wo_pair, live_here, live_flat, query_weight, *wq_moved)
    )

    n_moved = len(wq_moved)
    planes = [(0, 1, 2), (1, 2, 3)] if relayed else [None] * n_moved
    wq_two = line.second(wq_moved)
    wo_moved = line.first(wo_pair)
    above, wq_other = gate((wq_moved[0], line.swap(query_weight)))
    wq_others = [wq_other, line.swap(above, planes[0])]
    part_kv = jnp.concatenate(
        [matmul(image_cols, key_weight), matmul(image_cols, value_weight)], axis=1
    )
    part_kv = part_kv.reshape(n_dp, image_rows, 2 * local_cols)
    kv_own = jnp.sum(lax.all_to_all(part_kv, "dp", split_axis=0, concat_axis=0), axis=0)
    kv_own, live_here, live_flat, *staged = gate(
        (kv_own.astype(BF16), live_here, live_flat, *wq_others, *wq_moved, *wq_two, *wo_moved)
    )
    wq_others, staged = staged[:2], staged[2:]
    wq_moved, wq_two, wo_moved = staged[:n_moved], staged[n_moved:-n_moved], staged[-n_moved:]

    def everywhere(values):
        copies = jnp.broadcast_to(values[None], (n_dp, *values.shape))
        return lax.all_to_all(copies, "dp", split_axis=0, concat_axis=0)

    wq_last = line.third(wq_two)
    wo_two = line.second(wo_moved)
    wq_others += [line.swap(block, at) for block, at in zip(wq_moved[1:], planes[1:])]
    wq_others += [line.swap(block) for block in wq_last[:1]]
    kv_all = everywhere(kv_own).reshape(images, 2 * local_cols)
    quarter_rows = rows // 4
    live_rows = lax.dynamic_slice_in_dim(live_flat, quarter * quarter_rows, quarter_rows, 0)
    live_mine = lax.all_to_all(
        live_rows.reshape(quarter_rows, n_dp, own_width), "dp", split_axis=1, concat_axis=0
    )
    live_mine = live_mine.reshape(n_dp, quarter_rows, own_width)
    kv_all, live_here, live_mine, wo_pair, live_flat, *staged = gate(
        (kv_all, live_here, live_mine, wo_pair, live_flat, *wo_two, *wq_last, *wq_others)
    )
    wo_two, staged = staged[: len(wo_two)], staged[len(wo_two) :]
    wq_last, wq_others = staged[: len(wq_last)], staged[len(wq_last) :]

    wo_last = line.third(wo_two)
    by_y = tensor_swap(live_here, 2)
    live_pieces = [live_here, tensor_swap(live_here, 1), by_y, tensor_swap(by_y, 1)]
    wq_others += [line.swap(block, (0, 3)) for block in wq_last[1:]]
    arrivals = [query_weight, *wq_moved, *wq_last]
    early = range(4 if relayed else len(arrivals))
    late = range(len(early), len(arrivals))
    query_part = call(
        functools.partial(query_kernel, line, relayed, early),
        place,
        (text_flat, *arrivals[: len(early)], *wq_others[: len(early)]),
        [shape((rows, local_cols), F32)],
        (),
        2 * rows * width * local_cols,
    )
    half = shape((rows, half_cols), F32)
    wo_early = [wo_pair, *wo_moved]
    grad_parts = call(
        functools.partial(grad_kernel, line, range(len(wo_early)), 0),
        place,
        (live_flat, *live_pieces, *wo_early),
        [half] * 2,
        (),
        rows * width * local_cols,
    )

    query_part, *grad_parts = gate((query_part, *grad_parts))

    wo_late = range(len(wo_early), len(wo_early) + len(wo_last))
    grad_keep, grad_send = call(
        functools.partial(grad_kernel, line, wo_late, 2),
        place,
        (live_flat, *live_pieces, *grad_parts, *wo_last),
        [shape((rows, half_cols), BF16)] * 2,
        [pltpu.VMEM((rows, half_cols), F32)] * 2,
        rows * width * local_cols,
    )
    text_flat, live_mine, grad_keep, grad_send = gate(
        (text_flat, live_mine, grad_keep, grad_send)
    )
    grad_come = line.swap(grad_send)
    queries, attended = call(
        functools.partial(forward_kernel, line, relayed, late, image_own),
        place,
        (text_flat, kv_all, query_part, *arrivals[len(early) :], *wq_others[len(early) :]),
        [shape((rows, local_cols), BF16)] * 2,
        [pltpu.VMEM((rows, local_cols), F32)],
        rows * width * local_cols,
    )
    wq_blocks = [*arrivals, *wq_others]

    att_next = [line.shift(attended, m) for m in (1, line.n_z - 1)]
    att_swapped = line.swap(attended)
    live_y = tensor_swap(live_mine, 2)

    query_grad, kv_part = call(
        functools.partial(backward_kernel, image_own),
        place,
        (queries, kv_all, grad_keep, grad_come),
        [shape((rows, local_cols), BF16), shape((images, 2 * local_cols), F32)],
        (),
        10 * images * rows * local_cols,
    )
    kv_part = kv_part.reshape(n_dp, image_rows, 2 * local_cols)
    kv_grad = jnp.sum(lax.all_to_all(kv_part, "dp", split_axis=0, concat_axis=0), axis=0)
    chunk = n_dp // n_tensor
    term = call(
        functools.partial(term_kernel, line, relayed),
        place,
        (query_grad, *wq_blocks),
        [shape((n_tensor, chunk, rows, own_width), BF16)],
        (),
        2 * rows * width * local_cols,
    )
    kv_grad, term, live_mine, live_y = gate((kv_grad.astype(BF16), term, live_mine, live_y))
    kv_grad_all = everywhere(kv_grad).reshape(images, 2 * local_cols)
    live_pair = jnp.stack([live_mine, live_y])

    text_parts = lax.all_to_all(term, "tensor", split_axis=0, concat_axis=0).reshape(term.shape)
    attended, att_swapped, *att_next = gate((attended, att_swapped, *att_next))
    att_far = [line.shift(attended, m) for m in range(2, line.n_z - 1)]
    att_other_next = [line.swap(block) for block in att_next]
    live_core = tensor_swap(live_pair, 1)

    image_term = matmul(kv_grad_all[:, :local_cols], key_weight, BACK)
    image_term = image_term + matmul(kv_grad_all[:, local_cols:], value_weight, BACK)
    image_grad, text_parts, live_core, *staged = to_owner(
        line, image_term.astype(BF16), text_parts, live_core, *att_other_next, *att_far
    )
    att_other_next, att_far = staged[:2], staged[2:]
    att_other_far = [line.swap(block) for block in att_far]
    image_grad = image_grad.reshape(samples, image_own, width // n_tensor)
    text_grad = call(
        sum_kernel, place, (text_parts,), [shape((rows, width // n_tensor), BF16)]
    )
    text_grad = text_grad.reshape(samples, tok_rows, width // n_tensor)

    att_blocks = [attended, att_next[0], *att_far, att_next[1]]
    att_others = [att_swapped, att_other_next[0], *att_other_far, att_other_next[1]]
    weight_grad = call(
        functools.partial(weight_grad_kernel, line),
        place,
        (live_pair, live_core, *att_blocks, *att_others),
        [shape((local_cols, own_width), BF16)],
        [pltpu.VMEM((local_cols, own_width), F32)],
        2 * n_dp * rows * local_cols * own_width,
    )
    return text_grad, image_grad, weight_grad


def solution(mesh):
    return jax.shard_map(
        shards,
        mesh=mesh,
        in_specs=(
            P(None, "dp", None),
            P(None, "dp", None),
            P(None, "dp", None),
            P(),
            P("dp", "tensor"),
            P("dp", "tensor"),
            P("dp", "tensor"),
            P("tensor", "dp"),
        ),
        out_specs=(P(None, "dp", "tensor"), P(None, "dp", "tensor"), P("tensor", "dp")),
        check_vma=False,
    )
```

```python
import functools

import jax
import jax.numpy as jnp
from jax import lax
from jax.experimental import pallas as pl
from jax.experimental.pallas import tpu as pltpu
from jax.sharding import PartitionSpec as P

HEAD_DIM = 128
F32 = jnp.float32
BF16 = jnp.bfloat16
BACK = (((1,), (1,)), ((), ()))
FIRST = (((0,), (0,)), ((), ()))
VMEM_LIMIT = 60 * 1024 * 1024


def matmul(a, b, dims=None):
    if dims is None:
        return jnp.dot(a, b, preferred_element_type=F32)
    return lax.dot_general(a, b, dims, preferred_element_type=F32)


class Line:
    def __init__(self):
        self.n_dp = lax.axis_size("dp")
        self.n_z = self.n_dp // 2

    def move(self, block, moves):
        pairs = [(2 * a + e, 2 * b + e) for a, b in moves for e in range(2)]
        return lax.ppermute(block, "dp", pairs)

    def swap(self, block, planes=None):
        planes = range(self.n_z) if planes is None else planes
        pairs = [(2 * a + e, 2 * a + 1 - e) for a in planes for e in range(2)]
        return lax.ppermute(block, "dp", pairs)

    def shift(self, block, distance):
        n = self.n_z
        return self.move(block, [((a + distance) % n, a) for a in range(n)])

    def first(self, block):
        if self.n_z != 4:
            return [self.shift(block, m) for m in range(1, self.n_z)]
        above = self.move(block, [(1, 0), (2, 1), (3, 2)])
        below = self.move(block, [(0, 1), (1, 2), (2, 3)])
        return [above, below]

    def second(self, moved):
        if self.n_z != 4:
            return []
        return [self.move(moved[0], [(1, 0), (2, 1)]), self.move(moved[1], [(1, 2), (2, 3)])]

    def third(self, forwarded):
        if self.n_z != 4:
            return []
        across = jnp.where(lax.axis_index("dp") < 4, forwarded[0], forwarded[1])
        return [across, self.move(across, [(1, 0), (2, 3)])]

    def slots(self, z, relayed):
        if not relayed:
            return [(m, None) for m in range(self.n_z)]
        return [
            (0, None),
            (1, z < 3),
            (3, z > 0),
            (2, None),
            (jnp.where(z == 3, 1, 3), (z == 3) | (z == 0)),
        ]


def each_block(line, place, relayed, which, body):
    z, x = place[0], place[1]
    slots = line.slots(z, relayed)
    for j, at in enumerate(which):
        m, came = slots[at]
        plane = lax.rem(z + m, line.n_z)
        for e in range(2):
            index = 2 * plane + (x if e == 0 else 1 - x)
            if came is None:
                body(j, e, index)
            else:
                pl.when(came)(functools.partial(body, j, e, index))


def columns(index, size):
    return pl.ds(pl.multiple_of(index * size, size), size)


def probabilities(query, key, image_own):
    scores = matmul(key, query, BACK) * HEAD_DIM ** (-0.5)
    image = lax.broadcasted_iota(jnp.int32, scores.shape, 0)
    token = lax.broadcasted_iota(jnp.int32, scores.shape, 1)
    image_sample = lax.rem(lax.div(image, image_own), 2)
    same = image_sample == lax.div(token, scores.shape[1] // 2)
    scores = jnp.where(same, scores, -1e30)
    peak = jnp.max(scores, axis=0, keepdims=True)
    expo = jnp.where(same, jnp.exp(scores - peak), 0.0)
    return expo / jnp.sum(expo, axis=0, keepdims=True)


def query_kernel(line, relayed, which, place, text, *refs):
    n = len(which)
    weights, total = (refs[:n], refs[n : 2 * n]), refs[-1]
    own_width = weights[0][0].shape[0]
    total[...] = jnp.zeros_like(total)

    def add(j, e, index):
        total[...] += matmul(text[:, columns(index, own_width)], weights[e][j][...])

    each_block(line, place, relayed, which, add)


def forward_kernel(line, relayed, which, image_own, place, text, kv, part, *refs):
    n = len(which)
    weights, (query_out, attended_out, total) = (refs[:n], refs[n : 2 * n]), refs[2 * n :]
    rows, cols = total.shape
    total[...] = part[...]

    def add(j, e, index):
        weight = weights[e][j]
        total[...] += matmul(text[:, columns(index, weight.shape[0])], weight[...])

    each_block(line, place, relayed, which, add)
    query_out[...] = total[...].astype(BF16)
    part_rows = rows // 4
    quarter = place[2]
    for h in range(cols // HEAD_DIM):
        at = slice(h * HEAD_DIM, (h + 1) * HEAD_DIM)
        value = kv[:, cols + h * HEAD_DIM : cols + (h + 1) * HEAD_DIM]
        prob = probabilities(query_out[:, at], kv[:, at], image_own)
        attended = matmul(prob.astype(BF16), value, FIRST).astype(BF16)
        for r in range(4):
            low_bit = (quarter + r) % 2
            high_bit = (quarter // 2 + r // 2) % 2
            start = pl.multiple_of((2 * low_bit + high_bit) * part_rows, part_rows)
            attended_out[pl.ds(start, part_rows), at] = attended[
                r * part_rows : (r + 1) * part_rows
            ]


def grad_kernel(line, which, parts, place, live, mine, by_core, by_y, by_both, *refs):
    before, refs = refs[:parts], refs[parts:]
    weights, outs = refs[: len(which)], refs[len(which) :]
    cut = line.n_dp // 4
    keep, send = outs[-2:]
    keep[...] = before[0][...] if parts else jnp.zeros_like(keep)
    send[...] = before[1][...] if parts else jnp.zeros_like(send)

    def add(j, e, index):
        own_width = weights[j].shape[1] // 2
        weight = weights[j][:, e * own_width : (e + 1) * own_width]
        keep[...] += matmul(live[:, columns(index, own_width)], weight, BACK)
        inner = columns(lax.rem(index, cut), own_width)
        member = lax.bitwise_xor(lax.div(index, cut), place[2])
        other = mine[:, inner]
        for at, piece in ((1, by_core), (2, by_y), (3, by_both)):
            other = jnp.where(member == at, piece[:, inner], other)
        send[...] += matmul(other, weight, BACK)

    each_block(line, place, line.n_z == 4, which, add)
    if parts:
        outs[0][...] = keep[...].astype(BF16)
        outs[1][...] = send[...].astype(BF16)


def backward_kernel(image_own, place, query, kv, keep, come, query_grad, kv_grad):
    cols = query.shape[1]
    half = cols // 2
    x = place[1]
    for h in range(cols // HEAD_DIM):
        at = slice(h * HEAD_DIM, (h + 1) * HEAD_DIM)
        value_at = slice(cols + h * HEAD_DIM, cols + (h + 1) * HEAD_DIM)
        side = h * HEAD_DIM // half
        inner = slice(h * HEAD_DIM - side * half, (h + 1) * HEAD_DIM - side * half)
        grad = jnp.where(x == side, keep[:, inner], come[:, inner])
        prob = probabilities(query[:, at], kv[:, at], image_own)
        kv_grad[:, value_at] = matmul(prob.astype(BF16), grad)
        prob_grad = matmul(kv[:, value_at], grad, BACK)
        delta = jnp.sum(prob * prob_grad, axis=0, keepdims=True)
        score_grad = (prob * (prob_grad - delta) * HEAD_DIM ** (-0.5)).astype(BF16)
        kv_grad[:, at] = matmul(score_grad, query[:, at])
        query_grad[:, at] = matmul(score_grad, kv[:, at], FIRST).astype(BF16)


def term_kernel(line, relayed, place, query_grad, *refs):
    out = refs[-1]
    n = (len(refs) - 1) // 2
    weights = (refs[:n], refs[n : 2 * n])
    chunk = out.shape[1]

    def write(i, e, index):
        term = matmul(query_grad[...], weights[e][i][...], BACK)
        out[lax.div(index, chunk), lax.rem(index, chunk)] = term.astype(BF16)

    each_block(line, place, relayed, range(n), write)


def weight_grad_kernel(line, place, *refs):
    live, refs = refs[:2], refs[2:]
    n = (len(refs) - 2) // 2
    attended, (out, total) = (refs[:n], refs[n : 2 * n]), refs[2 * n :]
    total[...] = jnp.zeros_like(total)

    def add(i, e, index):
        block = jnp.concatenate([part[i, index] for part in live for i in range(2)], axis=0)
        term = matmul(attended[e][i][...], block, FIRST)
        total[...] += term.astype(BF16).astype(F32)

    each_block(line, place, False, range(n), add)
    out[...] = total[...].astype(BF16)


def sum_kernel(place, parts, out):
    width = parts.shape[3]
    for c in range(parts.shape[1]):
        total = parts[0, c].astype(F32)
        for k in range(1, parts.shape[0]):
            total = total + parts[k, c].astype(F32)
        out[:, c * width : (c + 1) * width] = total.astype(BF16)


def call(kernel, place, operands, outs, scratch=(), flops=0):
    moved = sum(a.size * a.dtype.itemsize for a in (*operands, *outs))
    single = len(outs) == 1
    return pl.pallas_call(
        kernel,
        out_shape=outs[0] if single else outs,
        in_specs=[pl.BlockSpec(memory_space=pltpu.SMEM)]
        + [pl.BlockSpec(memory_space=pltpu.VMEM)] * len(operands),
        out_specs=pl.BlockSpec(memory_space=pltpu.VMEM)
        if single
        else [pl.BlockSpec(memory_space=pltpu.VMEM)] * len(outs),
        scratch_shapes=list(scratch),
        compiler_params=pltpu.CompilerParams(vmem_limit_bytes=VMEM_LIMIT),
        cost_estimate=pl.CostEstimate(flops=flops, bytes_accessed=moved, transcendentals=0),
    )(place, *operands)


def to_owner(line, terms, *others):
    n_dp, n_tensor = line.n_dp, lax.axis_size("tensor")
    images, cols = terms.shape
    if line.n_z != n_tensor:
        terms = lax.all_to_all(terms, "dp", split_axis=0, concat_axis=1, tiled=True)
        terms = terms.reshape(images // n_dp, n_tensor, n_dp * cols // n_tensor)
        parts = lax.all_to_all(terms, "tensor", split_axis=1, concat_axis=0)
        return (jnp.sum(parts.astype(F32), axis=0).astype(BF16), *others)
    parts = lax.all_to_all(
        terms.reshape(n_tensor, images // n_tensor, cols), "tensor", split_axis=0, concat_axis=0
    )
    total = jnp.sum(parts.astype(F32), axis=0).astype(BF16)
    total, *others = lax.optimization_barrier((total, *others))
    total = total.reshape(2, images // n_dp, cols)
    x = lax.axis_index("dp") % 2
    come = []
    for other in range(2):
        block = jnp.where(x == other, total[0], total[1])
        pairs = [
            ((2 * z + e) * n_tensor + t, (2 * t + (e ^ other)) * n_tensor + z)
            for z in range(line.n_z)
            for e in range(2)
            for t in range(n_tensor)
        ]
        come.append(lax.ppermute(block, ("dp", "tensor"), pairs))
    rows = jnp.where(
        x == 0, jnp.concatenate(come, axis=1), jnp.concatenate(come[::-1], axis=1)
    )
    return (rows, *others)


def shards(
    text_states,
    image_states,
    out_grad,
    text_lengths,
    query_weight,
    key_weight,
    value_weight,
    out_weight,
):
    samples, tok_rows, width = text_states.shape
    image_own = image_states.shape[1]
    line = Line()
    n_dp = line.n_dp
    n_tensor = lax.axis_size("tensor")
    dp_at, tensor_at = lax.axis_index("dp"), lax.axis_index("tensor")
    x, quarter = dp_at % 2, tensor_at % 4
    place = jnp.stack([dp_at // 2, x, quarter, tensor_at]).astype(jnp.int32)
    rows = samples * tok_rows
    image_rows = samples * image_own
    images = n_dp * image_rows
    local_cols = query_weight.shape[1]
    own_width = query_weight.shape[0]
    half_cols = local_cols // 2
    shape = jax.ShapeDtypeStruct

    def tensor_swap(block, bit):
        return lax.ppermute(block, "tensor", [(t, t ^ bit) for t in range(n_tensor)])

    positions = dp_at * tok_rows + lax.iota(jnp.int32, tok_rows)
    live_rows = positions[None, :] < text_lengths[:, None]
    grad_live = jnp.where(live_rows[..., None], out_grad, jnp.zeros_like(out_grad))
    text_flat = text_states.reshape(rows, width)
    live_flat = grad_live.reshape(rows, width)
    image_flat = image_states.reshape(image_rows, width)

    gate = lax.optimization_barrier

    relayed = line.n_z == 4
    wq_moved = line.first(query_weight)
    quarter_rows = rows // 4
    live_rows = lax.dynamic_slice_in_dim(live_flat, quarter * quarter_rows, quarter_rows, 0)
    both = jnp.concatenate([live_rows, image_flat], axis=0).reshape(-1, n_dp, own_width)
    both = lax.all_to_all(both, "dp", split_axis=1, concat_axis=0)
    both = both.reshape(n_dp, quarter_rows + image_rows, own_width)
    wo_keep = lax.dynamic_slice_in_dim(out_weight, x * half_cols, half_cols, 0)
    wo_send = lax.dynamic_slice_in_dim(out_weight, (1 - x) * half_cols, half_cols, 0)
    wo_pair = jnp.concatenate([wo_keep, line.swap(wo_send)], axis=1)
    quarter_cols = width // 4
    live_part = lax.dynamic_slice_in_dim(live_flat, quarter * quarter_cols, quarter_cols, 1)
    live_here = line.swap(live_part)
    both, wo_pair, live_here, query_weight, *wq_moved = gate(
        (both, wo_pair, live_here, query_weight, *wq_moved)
    )
    live_mine = both[:, :quarter_rows]
    image_cols = both[:, quarter_rows:].reshape(images, own_width)

    n_moved = len(wq_moved)
    planes = [(0, 1, 2), (1, 2, 3)] if relayed else [None] * n_moved
    wq_two = line.second(wq_moved)
    wo_moved = line.first(wo_pair)
    above, wq_other = gate((wq_moved[0], line.swap(query_weight)))
    wq_others = [wq_other, line.swap(above, planes[0])]
    part_kv = jnp.concatenate(
        [matmul(image_cols, key_weight), matmul(image_cols, value_weight)], axis=1
    )
    part_kv = part_kv.reshape(n_dp, image_rows, 2 * local_cols)
    kv_own = jnp.sum(lax.all_to_all(part_kv, "dp", split_axis=0, concat_axis=0), axis=0)
    kv_own, live_here, *staged = gate(
        (kv_own.astype(BF16), live_here, *wq_others, *wq_moved, *wq_two, *wo_moved)
    )
    wq_others, staged = staged[:2], staged[2:]
    wq_moved, wq_two, wo_moved = staged[:n_moved], staged[n_moved:-n_moved], staged[-n_moved:]

    def everywhere(values):
        copies = jnp.broadcast_to(values[None], (n_dp, *values.shape))
        return lax.all_to_all(copies, "dp", split_axis=0, concat_axis=0)

    wq_last = line.third(wq_two)
    wo_two = line.second(wo_moved)
    wq_others += [line.swap(block, at) for block, at in zip(wq_moved[1:], planes[1:])]
    wq_others += [line.swap(block) for block in wq_last[:1]]
    kv_all = everywhere(kv_own).reshape(images, 2 * local_cols)
    kv_all, live_here, wo_pair, live_flat, *staged = gate(
        (kv_all, live_here, wo_pair, live_flat, *wo_two, *wq_last, *wq_others)
    )
    wo_two, staged = staged[: len(wo_two)], staged[len(wo_two) :]
    wq_last, wq_others = staged[: len(wq_last)], staged[len(wq_last) :]

    wo_last = line.third(wo_two)
    by_y = tensor_swap(live_here, 2)
    live_pieces = [live_here, tensor_swap(live_here, 1), by_y, tensor_swap(by_y, 1)]
    wq_others += [line.swap(block, (0, 3)) for block in wq_last[1:]]
    arrivals = [query_weight, *wq_moved, *wq_last]
    early = range(4 if relayed else len(arrivals))
    late = range(len(early), len(arrivals))
    query_part = call(
        functools.partial(query_kernel, line, relayed, early),
        place,
        (text_flat, *arrivals[: len(early)], *wq_others[: len(early)]),
        [shape((rows, local_cols), F32)],
        (),
        2 * rows * width * local_cols,
    )
    half = shape((rows, half_cols), F32)
    wo_early = [wo_pair, *wo_moved]
    grad_parts = call(
        functools.partial(grad_kernel, line, range(len(wo_early)), 0),
        place,
        (live_flat, *live_pieces, *wo_early),
        [half] * 2,
        (),
        rows * width * local_cols,
    )

    query_part, *grad_parts = gate((query_part, *grad_parts))

    wo_late = range(len(wo_early), len(wo_early) + len(wo_last))
    grad_keep, grad_send = call(
        functools.partial(grad_kernel, line, wo_late, 2),
        place,
        (live_flat, *live_pieces, *grad_parts, *wo_last),
        [shape((rows, half_cols), BF16)] * 2,
        [pltpu.VMEM((rows, half_cols), F32)] * 2,
        rows * width * local_cols,
    )
    text_flat, grad_keep, grad_send = gate((text_flat, grad_keep, grad_send))
    grad_come = line.swap(grad_send)
    queries, attended = call(
        functools.partial(forward_kernel, line, relayed, late, image_own),
        place,
        (text_flat, kv_all, query_part, *arrivals[len(early) :], *wq_others[len(early) :]),
        [shape((rows, local_cols), BF16)] * 2,
        [pltpu.VMEM((rows, local_cols), F32)],
        rows * width * local_cols,
    )
    wq_blocks = [*arrivals, *wq_others]

    att_next = [line.shift(attended, m) for m in (1, line.n_z - 1)]
    att_far = [line.shift(attended, m) for m in range(2, line.n_z - 1)]
    att_swapped = line.swap(attended)
    query_grad, kv_part = call(
        functools.partial(backward_kernel, image_own),
        place,
        (queries, kv_all, grad_keep, grad_come),
        [shape((rows, local_cols), BF16), shape((images, 2 * local_cols), F32)],
        (),
        10 * images * rows * local_cols,
    )
    kv_part = kv_part.reshape(n_dp, image_rows, 2 * local_cols)
    kv_grad = jnp.sum(lax.all_to_all(kv_part, "dp", split_axis=0, concat_axis=0), axis=0)
    chunk = n_dp // n_tensor
    term = call(
        functools.partial(term_kernel, line, relayed),
        place,
        (query_grad, *wq_blocks),
        [shape((n_tensor, chunk, rows, own_width), BF16)],
        (),
        2 * rows * width * local_cols,
    )
    kv_grad, term, live_mine, att_swapped, *att_next = gate(
        (kv_grad.astype(BF16), term, live_mine, att_swapped, *att_next)
    )
    kv_grad_all = everywhere(kv_grad).reshape(images, 2 * local_cols)

    text_parts = lax.all_to_all(term, "tensor", split_axis=0, concat_axis=0).reshape(term.shape)
    att_other_next = [line.swap(block) for block in att_next]
    live_pair = jnp.stack([live_mine, tensor_swap(live_mine, 2)])
    kv_grad_all, text_parts, live_pair, *staged = gate(
        (kv_grad_all, text_parts, live_pair, *att_other_next, *att_far)
    )
    att_other_next, att_far = staged[:2], staged[2:]
    att_other_far = [line.swap(block) for block in att_far]
    live_core = tensor_swap(live_pair, 1)

    image_term = matmul(kv_grad_all[:, :local_cols], key_weight, BACK)
    image_term = image_term + matmul(kv_grad_all[:, local_cols:], value_weight, BACK)
    image_grad, live_core, *att_other_far = to_owner(
        line, image_term.astype(BF16), live_core, *att_other_far
    )
    image_grad = image_grad.reshape(samples, image_own, width // n_tensor)
    text_grad = call(
        sum_kernel, place, (text_parts,), [shape((rows, width // n_tensor), BF16)]
    )
    text_grad = text_grad.reshape(samples, tok_rows, width // n_tensor)

    att_blocks = [attended, att_next[0], *att_far, att_next[1]]
    att_others = [att_swapped, att_other_next[0], *att_other_far, att_other_next[1]]
    weight_grad = call(
        functools.partial(weight_grad_kernel, line),
        place,
        (live_pair, live_core, *att_blocks, *att_others),
        [shape((local_cols, own_width), BF16)],
        [pltpu.VMEM((local_cols, own_width), F32)],
        2 * n_dp * rows * local_cols * own_width,
    )
    return text_grad, image_grad, weight_grad


def solution(mesh):
    return jax.shard_map(
        shards,
        mesh=mesh,
        in_specs=(
            P(None, "dp", None),
            P(None, "dp", None),
            P(None, "dp", None),
            P(),
            P("dp", "tensor"),
            P("dp", "tensor"),
            P("dp", "tensor"),
            P("tensor", "dp"),
        ),
        out_specs=(P(None, "dp", "tensor"), P(None, "dp", "tensor"), P("tensor", "dp")),
        check_vma=False,
    )
```

```python
import functools

import jax
import jax.numpy as jnp
from jax import lax
from jax.experimental import pallas as pl
from jax.experimental.pallas import tpu as pltpu
from jax.sharding import PartitionSpec as P

HEAD_DIM = 128
F32 = jnp.float32
BF16 = jnp.bfloat16
BACK = (((1,), (1,)), ((), ()))
FIRST = (((0,), (0,)), ((), ()))
VMEM_LIMIT = 48 * 1024 * 1024


def matmul(a, b, dims=None):
    if dims is None:
        return jnp.dot(a, b, preferred_element_type=F32)
    return lax.dot_general(a, b, dims, preferred_element_type=F32)


class Line:
    def __init__(self):
        self.n_dp = lax.axis_size("dp")
        self.n_z = self.n_dp // 2

    def move(self, block, moves):
        pairs = [(2 * a + e, 2 * b + e) for a, b in moves for e in range(2)]
        return lax.ppermute(block, "dp", pairs)

    def swap(self, block, planes=None):
        planes = range(self.n_z) if planes is None else planes
        pairs = [(2 * a + e, 2 * a + 1 - e) for a in planes for e in range(2)]
        return lax.ppermute(block, "dp", pairs)

    def shift(self, block, distance):
        n = self.n_z
        return self.move(block, [((a + distance) % n, a) for a in range(n)])

    def first(self, block):
        if self.n_z != 4:
            return [self.shift(block, m) for m in range(1, self.n_z)]
        above = self.move(block, [(1, 0), (2, 1), (3, 2)])
        below = self.move(block, [(0, 1), (1, 2), (2, 3)])
        return [above, below]

    def second(self, moved):
        if self.n_z != 4:
            return []
        return [self.move(moved[0], [(1, 0), (2, 1)]), self.move(moved[1], [(1, 2), (2, 3)])]

    def third(self, forwarded):
        if self.n_z != 4:
            return []
        across = jnp.where(lax.axis_index("dp") < 4, forwarded[0], forwarded[1])
        return [across, self.move(across, [(1, 0), (2, 3)])]

    def slots(self, z, relayed):
        if not relayed:
            return [(m, None) for m in range(self.n_z)]
        return [
            (0, None),
            (1, z < 3),
            (3, z > 0),
            (2, None),
            (jnp.where(z == 3, 1, 3), (z == 3) | (z == 0)),
        ]


def each_block(line, place, relayed, which, body):
    z, x = place[0], place[1]
    slots = line.slots(z, relayed)
    for j, at in enumerate(which):
        m, came = slots[at]
        plane = lax.rem(z + m, line.n_z)
        for e in range(2):
            index = 2 * plane + (x if e == 0 else 1 - x)
            if came is None:
                body(j, e, index)
            else:
                pl.when(came)(functools.partial(body, j, e, index))


def columns(index, size):
    return pl.ds(pl.multiple_of(index * size, size), size)


def probabilities(query, key, image_own):
    scores = matmul(key, query, BACK) * HEAD_DIM ** (-0.5)
    image = lax.broadcasted_iota(jnp.int32, scores.shape, 0)
    token = lax.broadcasted_iota(jnp.int32, scores.shape, 1)
    image_sample = lax.rem(lax.div(image, image_own), 2)
    same = image_sample == lax.div(token, scores.shape[1] // 2)
    scores = jnp.where(same, scores, -1e30)
    peak = jnp.max(scores, axis=0, keepdims=True)
    expo = jnp.where(same, jnp.exp(scores - peak), 0.0)
    return expo / jnp.sum(expo, axis=0, keepdims=True)


def query_kernel(line, relayed, which, place, text, *refs):
    n = len(which)
    weights, total = (refs[:n], refs[n : 2 * n]), refs[-1]
    own_width = weights[0][0].shape[0]
    total[...] = jnp.zeros_like(total)

    def add(j, e, index):
        total[...] += matmul(text[:, columns(index, own_width)], weights[e][j][...])

    each_block(line, place, relayed, which, add)


def forward_kernel(line, relayed, which, image_own, place, text, kv, part, *refs):
    n = len(which)
    weights, (query_out, attended_out, total) = (refs[:n], refs[n : 2 * n]), refs[2 * n :]
    rows, cols = total.shape
    total[...] = part[...]

    def add(j, e, index):
        weight = weights[e][j]
        total[...] += matmul(text[:, columns(index, weight.shape[0])], weight[...])

    each_block(line, place, relayed, which, add)
    query_out[...] = total[...].astype(BF16)
    part_rows = rows // 4
    quarter = place[2]
    for h in range(cols // HEAD_DIM):
        at = slice(h * HEAD_DIM, (h + 1) * HEAD_DIM)
        value = kv[:, cols + h * HEAD_DIM : cols + (h + 1) * HEAD_DIM]
        prob = probabilities(query_out[:, at], kv[:, at], image_own)
        attended = matmul(prob.astype(BF16), value, FIRST).astype(BF16)
        for r in range(4):
            low_bit = (quarter + r) % 2
            high_bit = (quarter // 2 + r // 2) % 2
            start = pl.multiple_of((2 * low_bit + high_bit) * part_rows, part_rows)
            attended_out[pl.ds(start, part_rows), at] = attended[
                r * part_rows : (r + 1) * part_rows
            ]


def grad_kernel(line, which, parts, place, live, mine, by_core, by_y, by_both, *refs):
    before, refs = refs[:parts], refs[parts:]
    weights, outs = refs[: len(which)], refs[len(which) :]
    cut = line.n_dp // 4
    keep, send = outs[-2:]
    keep[...] = before[0][...] if parts else jnp.zeros_like(keep)
    send[...] = before[1][...] if parts else jnp.zeros_like(send)

    def add(j, e, index):
        own_width = weights[j].shape[1] // 2
        weight = weights[j][:, e * own_width : (e + 1) * own_width]
        keep[...] += matmul(live[:, columns(index, own_width)], weight, BACK)
        inner = columns(lax.rem(index, cut), own_width)
        member = lax.bitwise_xor(lax.div(index, cut), place[2])
        other = mine[:, inner]
        for at, piece in ((1, by_core), (2, by_y), (3, by_both)):
            other = jnp.where(member == at, piece[:, inner], other)
        send[...] += matmul(other, weight, BACK)

    each_block(line, place, line.n_z == 4, which, add)
    if parts:
        outs[0][...] = keep[...].astype(BF16)
        outs[1][...] = send[...].astype(BF16)


def backward_kernel(image_own, place, query, kv, keep, come, query_grad, kv_grad):
    cols = query.shape[1]
    half = cols // 2
    x = place[1]
    for h in range(cols // HEAD_DIM):
        at = slice(h * HEAD_DIM, (h + 1) * HEAD_DIM)
        value_at = slice(cols + h * HEAD_DIM, cols + (h + 1) * HEAD_DIM)
        side = h * HEAD_DIM // half
        inner = slice(h * HEAD_DIM - side * half, (h + 1) * HEAD_DIM - side * half)
        grad = jnp.where(x == side, keep[:, inner], come[:, inner])
        prob = probabilities(query[:, at], kv[:, at], image_own)
        kv_grad[:, value_at] = matmul(prob.astype(BF16), grad)
        prob_grad = matmul(kv[:, value_at], grad, BACK)
        delta = jnp.sum(prob * prob_grad, axis=0, keepdims=True)
        score_grad = (prob * (prob_grad - delta) * HEAD_DIM ** (-0.5)).astype(BF16)
        kv_grad[:, at] = matmul(score_grad, query[:, at])
        query_grad[:, at] = matmul(score_grad, kv[:, at], FIRST).astype(BF16)


def term_kernel(line, relayed, place, query_grad, *refs):
    out = refs[-1]
    n = (len(refs) - 1) // 2
    weights = (refs[:n], refs[n : 2 * n])
    chunk = out.shape[1]

    def write(i, e, index):
        term = matmul(query_grad[...], weights[e][i][...], BACK)
        out[lax.div(index, chunk), lax.rem(index, chunk)] = term.astype(BF16)

    each_block(line, place, relayed, range(n), write)


def weight_grad_kernel(place, own_pair, core_pair, attended, out, total):
    total[...] = jnp.zeros_like(total)
    for d in range(attended.shape[0]):
        parts = [pair[i, d] for pair in (own_pair, core_pair) for i in range(2)]
        term = matmul(attended[d], jnp.concatenate(parts, axis=0), FIRST)
        total[...] += term.astype(BF16).astype(F32)
    out[...] = total[...].astype(BF16)


def sum_kernel(place, parts, out):
    width = parts.shape[3]
    for c in range(parts.shape[1]):
        total = parts[0, c].astype(F32)
        for k in range(1, parts.shape[0]):
            total = total + parts[k, c].astype(F32)
        out[:, c * width : (c + 1) * width] = total.astype(BF16)


def call(kernel, place, operands, outs, scratch=(), flops=0):
    moved = sum(a.size * a.dtype.itemsize for a in (*operands, *outs))
    single = len(outs) == 1
    return pl.pallas_call(
        kernel,
        out_shape=outs[0] if single else outs,
        in_specs=[pl.BlockSpec(memory_space=pltpu.SMEM)]
        + [pl.BlockSpec(memory_space=pltpu.VMEM)] * len(operands),
        out_specs=pl.BlockSpec(memory_space=pltpu.VMEM)
        if single
        else [pl.BlockSpec(memory_space=pltpu.VMEM)] * len(outs),
        scratch_shapes=list(scratch),
        compiler_params=pltpu.CompilerParams(vmem_limit_bytes=VMEM_LIMIT),
        cost_estimate=pl.CostEstimate(flops=flops, bytes_accessed=moved, transcendentals=0),
    )(place, *operands)


def to_owner(line, terms, *others):
    n_dp, n_tensor = line.n_dp, lax.axis_size("tensor")
    images, cols = terms.shape
    if line.n_z != n_tensor:
        terms = lax.all_to_all(terms, "dp", split_axis=0, concat_axis=1, tiled=True)
        terms = terms.reshape(images // n_dp, n_tensor, n_dp * cols // n_tensor)
        parts = lax.all_to_all(terms, "tensor", split_axis=1, concat_axis=0)
        return (jnp.sum(parts.astype(F32), axis=0).astype(BF16), *others)
    parts = lax.all_to_all(
        terms.reshape(n_tensor, images // n_tensor, cols), "tensor", split_axis=0, concat_axis=0
    )
    total = jnp.sum(parts.astype(F32), axis=0).astype(BF16)
    total, *others = lax.optimization_barrier((total, *others))
    total = total.reshape(2, images // n_dp, cols)
    x = lax.axis_index("dp") % 2
    come = []
    for other in range(2):
        block = jnp.where(x == other, total[0], total[1])
        pairs = [
            ((2 * z + e) * n_tensor + t, (2 * t + (e ^ other)) * n_tensor + z)
            for z in range(line.n_z)
            for e in range(2)
            for t in range(n_tensor)
        ]
        come.append(lax.ppermute(block, ("dp", "tensor"), pairs))
    rows = jnp.where(
        x == 0, jnp.concatenate(come, axis=1), jnp.concatenate(come[::-1], axis=1)
    )
    return (rows, *others)


def shards(
    text_states,
    image_states,
    out_grad,
    text_lengths,
    query_weight,
    key_weight,
    value_weight,
    out_weight,
):
    samples, tok_rows, width = text_states.shape
    image_own = image_states.shape[1]
    line = Line()
    n_dp = line.n_dp
    n_tensor = lax.axis_size("tensor")
    dp_at, tensor_at = lax.axis_index("dp"), lax.axis_index("tensor")
    x, quarter = dp_at % 2, tensor_at % 4
    place = jnp.stack([dp_at // 2, x, quarter, tensor_at]).astype(jnp.int32)
    rows = samples * tok_rows
    image_rows = samples * image_own
    images = n_dp * image_rows
    local_cols = query_weight.shape[1]
    own_width = query_weight.shape[0]
    half_cols = local_cols // 2
    shape = jax.ShapeDtypeStruct

    def tensor_swap(block, bit):
        return lax.ppermute(block, "tensor", [(t, t ^ bit) for t in range(n_tensor)])

    positions = dp_at * tok_rows + lax.iota(jnp.int32, tok_rows)
    live_rows = positions[None, :] < text_lengths[:, None]
    grad_live = jnp.where(live_rows[..., None], out_grad, jnp.zeros_like(out_grad))
    text_flat = text_states.reshape(rows, width)
    live_flat = grad_live.reshape(rows, width)
    image_flat = image_states.reshape(image_rows, width)

    gate = lax.optimization_barrier

    relayed = line.n_z == 4
    wq_moved = line.first(query_weight)
    image_cols = lax.all_to_all(image_flat, "dp", split_axis=1, concat_axis=0, tiled=True)
    wo_keep = lax.dynamic_slice_in_dim(out_weight, x * half_cols, half_cols, 0)
    wo_send = lax.dynamic_slice_in_dim(out_weight, (1 - x) * half_cols, half_cols, 0)
    wo_pair = jnp.concatenate([wo_keep, line.swap(wo_send)], axis=1)
    quarter_cols = width // 4
    live_part = lax.dynamic_slice_in_dim(live_flat, quarter * quarter_cols, quarter_cols, 1)
    live_here = line.swap(live_part)
    image_cols, wo_pair, live_here, live_flat, query_weight, *wq_moved = gate(
        (image_cols, wo_pair, live_here, live_flat, query_weight, *wq_moved)
    )

    n_moved = len(wq_moved)
    planes = [(0, 1, 2), (1, 2, 3)] if relayed else [None] * n_moved
    wq_two = line.second(wq_moved)
    wo_moved = line.first(wo_pair)
    above, wq_other = gate((wq_moved[0], line.swap(query_weight)))
    wq_others = [wq_other, line.swap(above, planes[0])]
    part_kv = jnp.concatenate(
        [matmul(image_cols, key_weight), matmul(image_cols, value_weight)], axis=1
    )
    part_kv = part_kv.reshape(n_dp, image_rows, 2 * local_cols)
    kv_own = jnp.sum(lax.all_to_all(part_kv, "dp", split_axis=0, concat_axis=0), axis=0)
    kv_own, live_here, live_flat, *staged = gate(
        (kv_own.astype(BF16), live_here, live_flat, *wq_others, *wq_moved, *wq_two, *wo_moved)
    )
    wq_others, staged = staged[:2], staged[2:]
    wq_moved, wq_two, wo_moved = staged[:n_moved], staged[n_moved:-n_moved], staged[-n_moved:]

    def everywhere(values):
        copies = jnp.broadcast_to(values[None], (n_dp, *values.shape))
        return lax.all_to_all(copies, "dp", split_axis=0, concat_axis=0)

    wq_last = line.third(wq_two)
    wo_two = line.second(wo_moved)
    wq_others += [line.swap(block, at) for block, at in zip(wq_moved[1:], planes[1:])]
    wq_others += [line.swap(block) for block in wq_last[:1]]
    kv_all = everywhere(kv_own).reshape(images, 2 * local_cols)
    kv_all, live_here, wo_pair, live_flat, *staged = gate(
        (kv_all, live_here, wo_pair, live_flat, *wo_two, *wq_last, *wq_others)
    )
    wo_two, staged = staged[: len(wo_two)], staged[len(wo_two) :]
    wq_last, wq_others = staged[: len(wq_last)], staged[len(wq_last) :]

    wo_last = line.third(wo_two)
    by_y = tensor_swap(live_here, 2)
    live_pieces = [live_here, tensor_swap(live_here, 1), by_y, tensor_swap(by_y, 1)]
    wq_others += [line.swap(block, (0, 3)) for block in wq_last[1:]]
    arrivals = [query_weight, *wq_moved, *wq_last]
    early = range(4 if relayed else len(arrivals))
    late = range(len(early), len(arrivals))
    query_part = call(
        functools.partial(query_kernel, line, relayed, early),
        place,
        (text_flat, *arrivals[: len(early)], *wq_others[: len(early)]),
        [shape((rows, local_cols), F32)],
        (),
        2 * rows * width * local_cols,
    )
    half = shape((rows, half_cols), F32)
    wo_early = [wo_pair, *wo_moved]
    grad_parts = call(
        functools.partial(grad_kernel, line, range(len(wo_early)), 0),
        place,
        (live_flat, *live_pieces, *wo_early),
        [half] * 2,
        (),
        rows * width * local_cols,
    )

    query_part, *grad_parts = gate((query_part, *grad_parts))

    wo_late = range(len(wo_early), len(wo_early) + len(wo_last))
    grad_keep, grad_send = call(
        functools.partial(grad_kernel, line, wo_late, 2),
        place,
        (live_flat, *live_pieces, *grad_parts, *wo_last),
        [shape((rows, half_cols), BF16)] * 2,
        [pltpu.VMEM((rows, half_cols), F32)] * 2,
        rows * width * local_cols,
    )
    text_flat, live_flat, grad_keep, grad_send = gate(
        (text_flat, live_flat, grad_keep, grad_send)
    )
    grad_come = line.swap(grad_send)
    queries, attended = call(
        functools.partial(forward_kernel, line, relayed, late, image_own),
        place,
        (text_flat, kv_all, query_part, *arrivals[len(early) :], *wq_others[len(early) :]),
        [shape((rows, local_cols), BF16)] * 2,
        [pltpu.VMEM((rows, local_cols), F32)],
        rows * width * local_cols,
    )
    wq_blocks = [*arrivals, *wq_others]

    attended_all = lax.all_gather(attended, "dp", axis=0)
    query_grad, kv_part = call(
        functools.partial(backward_kernel, image_own),
        place,
        (queries, kv_all, grad_keep, grad_come),
        [shape((rows, local_cols), BF16), shape((images, 2 * local_cols), F32)],
        (),
        10 * images * rows * local_cols,
    )
    kv_part = kv_part.reshape(n_dp, image_rows, 2 * local_cols)
    kv_grad = jnp.sum(lax.all_to_all(kv_part, "dp", split_axis=0, concat_axis=0), axis=0)
    chunk = n_dp // n_tensor
    term = call(
        functools.partial(term_kernel, line, relayed),
        place,
        (query_grad, *wq_blocks),
        [shape((n_tensor, chunk, rows, own_width), BF16)],
        (),
        2 * rows * width * local_cols,
    )
    kv_grad, term = gate((kv_grad.astype(BF16), term))
    kv_grad_all = everywhere(kv_grad).reshape(images, 2 * local_cols)

    text_parts = lax.all_to_all(term, "tensor", split_axis=0, concat_axis=0).reshape(term.shape)
    kv_grad_all, text_parts, live_flat = gate((kv_grad_all, text_parts, live_flat))
    quarter_rows = rows // 4
    live_rows = lax.dynamic_slice_in_dim(live_flat, quarter * quarter_rows, quarter_rows, 0)
    live_mine = lax.all_to_all(
        live_rows.reshape(quarter_rows, n_dp, own_width), "dp", split_axis=1, concat_axis=0
    )
    live_mine = live_mine.reshape(n_dp, quarter_rows, own_width)
    live_pair = jnp.stack([live_mine, tensor_swap(live_mine, 2)])
    live_core = tensor_swap(live_pair, 1)

    image_term = matmul(kv_grad_all[:, :local_cols], key_weight, BACK)
    image_term = image_term + matmul(kv_grad_all[:, local_cols:], value_weight, BACK)
    image_grad, live_core = to_owner(line, image_term.astype(BF16), live_core)
    image_grad = image_grad.reshape(samples, image_own, width // n_tensor)
    text_grad = call(
        sum_kernel, place, (text_parts,), [shape((rows, width // n_tensor), BF16)]
    )
    text_grad = text_grad.reshape(samples, tok_rows, width // n_tensor)

    weight_grad = call(
        weight_grad_kernel,
        place,
        (live_pair, live_core, attended_all),
        [shape((local_cols, own_width), BF16)],
        [pltpu.VMEM((local_cols, own_width), F32)],
        2 * n_dp * rows * local_cols * own_width,
    )
    return text_grad, image_grad, weight_grad


def solution(mesh):
    return jax.shard_map(
        shards,
        mesh=mesh,
        in_specs=(
            P(None, "dp", None),
            P(None, "dp", None),
            P(None, "dp", None),
            P(),
            P("dp", "tensor"),
            P("dp", "tensor"),
            P("dp", "tensor"),
            P("tensor", "dp"),
        ),
        out_specs=(P(None, "dp", "tensor"), P(None, "dp", "tensor"), P("tensor", "dp")),
        check_vma=False,
    )
```

```python
import functools

import jax
import jax.numpy as jnp
from jax import lax
from jax.experimental import pallas as pl
from jax.experimental.pallas import tpu as pltpu
from jax.sharding import PartitionSpec as P

HEAD_DIM = 128
F32 = jnp.float32
BF16 = jnp.bfloat16
BACK = (((1,), (1,)), ((), ()))
FIRST = (((0,), (0,)), ((), ()))
VMEM_LIMIT = 60 * 1024 * 1024


def matmul(a, b, dims=None):
    if dims is None:
        return jnp.dot(a, b, preferred_element_type=F32)
    return lax.dot_general(a, b, dims, preferred_element_type=F32)


class Line:
    def __init__(self):
        self.n_dp = lax.axis_size("dp")
        self.n_z = self.n_dp // 2

    def move(self, block, moves):
        pairs = [(2 * a + e, 2 * b + e) for a, b in moves for e in range(2)]
        return lax.ppermute(block, "dp", pairs)

    def swap(self, block, planes=None):
        planes = range(self.n_z) if planes is None else planes
        pairs = [(2 * a + e, 2 * a + 1 - e) for a in planes for e in range(2)]
        return lax.ppermute(block, "dp", pairs)

    def shift(self, block, distance):
        n = self.n_z
        return self.move(block, [((a + distance) % n, a) for a in range(n)])

    def first(self, block):
        if self.n_z != 4:
            return [self.shift(block, m) for m in range(1, self.n_z)]
        above = self.move(block, [(1, 0), (2, 1), (3, 2)])
        below = self.move(block, [(0, 1), (1, 2), (2, 3)])
        return [above, below]

    def second(self, moved):
        if self.n_z != 4:
            return []
        return [self.move(moved[0], [(1, 0), (2, 1)]), self.move(moved[1], [(1, 2), (2, 3)])]

    def third(self, forwarded):
        if self.n_z != 4:
            return []
        across = jnp.where(lax.axis_index("dp") < 4, forwarded[0], forwarded[1])
        return [across, self.move(across, [(1, 0), (2, 3)])]

    def slots(self, z, relayed):
        if not relayed:
            return [(m, None) for m in range(self.n_z)]
        return [
            (0, None),
            (1, z < 3),
            (3, z > 0),
            (2, None),
            (jnp.where(z == 3, 1, 3), (z == 3) | (z == 0)),
        ]


def each_block(line, place, relayed, which, body):
    z, x = place[0], place[1]
    slots = line.slots(z, relayed)
    for j, at in enumerate(which):
        m, came = slots[at]
        plane = lax.rem(z + m, line.n_z)
        for e in range(2):
            index = 2 * plane + (x if e == 0 else 1 - x)
            if came is None:
                body(j, e, index)
            else:
                pl.when(came)(functools.partial(body, j, e, index))


def columns(index, size):
    return pl.ds(pl.multiple_of(index * size, size), size)


def probabilities(query, key, image_own):
    scores = matmul(key, query, BACK) * HEAD_DIM ** (-0.5)
    image = lax.broadcasted_iota(jnp.int32, scores.shape, 0)
    token = lax.broadcasted_iota(jnp.int32, scores.shape, 1)
    image_sample = lax.rem(lax.div(image, image_own), 2)
    same = image_sample == lax.div(token, scores.shape[1] // 2)
    scores = jnp.where(same, scores, -1e30)
    peak = jnp.max(scores, axis=0, keepdims=True)
    expo = jnp.where(same, jnp.exp(scores - peak), 0.0)
    return expo / jnp.sum(expo, axis=0, keepdims=True)


def query_kernel(line, relayed, which, place, text, *refs):
    n = len(which)
    weights, total = (refs[:n], refs[n : 2 * n]), refs[-1]
    own_width = weights[0][0].shape[0]
    total[...] = jnp.zeros_like(total)

    def add(j, e, index):
        total[...] += matmul(text[:, columns(index, own_width)], weights[e][j][...])

    each_block(line, place, relayed, which, add)


def forward_kernel(line, relayed, which, image_own, place, text, kv, part, *refs):
    n = len(which)
    weights, (query_out, attended_out, total) = (refs[:n], refs[n : 2 * n]), refs[2 * n :]
    rows, cols = total.shape
    total[...] = part[...]

    def add(j, e, index):
        weight = weights[e][j]
        total[...] += matmul(text[:, columns(index, weight.shape[0])], weight[...])

    each_block(line, place, relayed, which, add)
    query_out[...] = total[...].astype(BF16)
    part_rows = rows // 4
    quarter = place[2]
    for h in range(cols // HEAD_DIM):
        at = slice(h * HEAD_DIM, (h + 1) * HEAD_DIM)
        value = kv[:, cols + h * HEAD_DIM : cols + (h + 1) * HEAD_DIM]
        prob = probabilities(query_out[:, at], kv[:, at], image_own)
        attended = matmul(prob.astype(BF16), value, FIRST).astype(BF16)
        for r in range(4):
            low_bit = (quarter + r) % 2
            high_bit = (quarter // 2 + r // 2) % 2
            start = pl.multiple_of((2 * low_bit + high_bit) * part_rows, part_rows)
            attended_out[pl.ds(start, part_rows), at] = attended[
                r * part_rows : (r + 1) * part_rows
            ]


def grad_kernel(line, which, parts, place, live, mine, by_core, by_y, by_both, *refs):
    before, refs = refs[:parts], refs[parts:]
    weights, outs = refs[: len(which)], refs[len(which) :]
    cut = line.n_dp // 4
    keep, send = outs[-2:]
    keep[...] = before[0][...] if parts else jnp.zeros_like(keep)
    send[...] = before[1][...] if parts else jnp.zeros_like(send)

    def add(j, e, index):
        own_width = weights[j].shape[1] // 2
        weight = weights[j][:, e * own_width : (e + 1) * own_width]
        keep[...] += matmul(live[:, columns(index, own_width)], weight, BACK)
        inner = columns(lax.rem(index, cut), own_width)
        member = lax.bitwise_xor(lax.div(index, cut), place[2])
        other = mine[:, inner]
        for at, piece in ((1, by_core), (2, by_y), (3, by_both)):
            other = jnp.where(member == at, piece[:, inner], other)
        send[...] += matmul(other, weight, BACK)

    each_block(line, place, line.n_z == 4, which, add)
    if parts:
        outs[0][...] = keep[...].astype(BF16)
        outs[1][...] = send[...].astype(BF16)


def backward_kernel(image_own, place, query, kv, keep, come, query_grad, kv_grad):
    cols = query.shape[1]
    half = cols // 2
    x = place[1]
    for h in range(cols // HEAD_DIM):
        at = slice(h * HEAD_DIM, (h + 1) * HEAD_DIM)
        value_at = slice(cols + h * HEAD_DIM, cols + (h + 1) * HEAD_DIM)
        side = h * HEAD_DIM // half
        inner = slice(h * HEAD_DIM - side * half, (h + 1) * HEAD_DIM - side * half)
        grad = jnp.where(x == side, keep[:, inner], come[:, inner])
        prob = probabilities(query[:, at], kv[:, at], image_own)
        kv_grad[:, value_at] = matmul(prob.astype(BF16), grad)
        prob_grad = matmul(kv[:, value_at], grad, BACK)
        delta = jnp.sum(prob * prob_grad, axis=0, keepdims=True)
        score_grad = (prob * (prob_grad - delta) * HEAD_DIM ** (-0.5)).astype(BF16)
        kv_grad[:, at] = matmul(score_grad, query[:, at])
        query_grad[:, at] = matmul(score_grad, kv[:, at], FIRST).astype(BF16)


def term_kernel(line, relayed, place, query_grad, *refs):
    out = refs[-1]
    n = (len(refs) - 1) // 2
    weights = (refs[:n], refs[n : 2 * n])
    chunk = out.shape[1]

    def write(i, e, index):
        term = matmul(query_grad[...], weights[e][i][...], BACK)
        member = lax.bitwise_xor(lax.div(index, chunk), place[3])
        out[member, lax.rem(index, chunk)] = term.astype(BF16)

    each_block(line, place, relayed, range(n), write)


def weight_grad_kernel(line, place, *refs):
    live, refs = refs[:2], refs[2:]
    n = (len(refs) - 2) // 2
    attended, (out, total) = (refs[:n], refs[n : 2 * n]), refs[2 * n :]
    total[...] = jnp.zeros_like(total)

    def add(i, e, index):
        block = jnp.concatenate([part[i, index] for part in live for i in range(2)], axis=0)
        term = matmul(attended[e][i][...], block, FIRST)
        total[...] += term.astype(BF16).astype(F32)

    each_block(line, place, False, range(n), add)
    out[...] = total[...].astype(BF16)


def sum_kernel(place, term, *refs):
    parts, out = refs[:-1], refs[-1]
    width = term.shape[3]
    for c in range(term.shape[1]):
        total = term[0, c].astype(F32)
        for part in parts:
            total = total + part[c].astype(F32)
        out[:, c * width : (c + 1) * width] = total.astype(BF16)


def call(kernel, place, operands, outs, scratch=(), flops=0):
    moved = sum(a.size * a.dtype.itemsize for a in (*operands, *outs))
    single = len(outs) == 1
    return pl.pallas_call(
        kernel,
        out_shape=outs[0] if single else outs,
        in_specs=[pl.BlockSpec(memory_space=pltpu.SMEM)]
        + [pl.BlockSpec(memory_space=pltpu.VMEM)] * len(operands),
        out_specs=pl.BlockSpec(memory_space=pltpu.VMEM)
        if single
        else [pl.BlockSpec(memory_space=pltpu.VMEM)] * len(outs),
        scratch_shapes=list(scratch),
        compiler_params=pltpu.CompilerParams(vmem_limit_bytes=VMEM_LIMIT),
        cost_estimate=pl.CostEstimate(flops=flops, bytes_accessed=moved, transcendentals=0),
    )(place, *operands)


def to_owner(line, terms, *others):
    n_dp, n_tensor = line.n_dp, lax.axis_size("tensor")
    images, cols = terms.shape
    if line.n_z != n_tensor:
        terms = lax.all_to_all(terms, "dp", split_axis=0, concat_axis=1, tiled=True)
        terms = terms.reshape(images // n_dp, n_tensor, n_dp * cols // n_tensor)
        parts = lax.all_to_all(terms, "tensor", split_axis=1, concat_axis=0)
        return (jnp.sum(parts.astype(F32), axis=0).astype(BF16), *others)
    parts = lax.all_to_all(
        terms.reshape(n_tensor, images // n_tensor, cols), "tensor", split_axis=0, concat_axis=0
    )
    total = jnp.sum(parts.astype(F32), axis=0).astype(BF16)
    total, *others = lax.optimization_barrier((total, *others))
    total = total.reshape(2, images // n_dp, cols)
    x = lax.axis_index("dp") % 2
    come = []
    for other in range(2):
        block = jnp.where(x == other, total[0], total[1])
        pairs = [
            ((2 * z + e) * n_tensor + t, (2 * t + (e ^ other)) * n_tensor + z)
            for z in range(line.n_z)
            for e in range(2)
            for t in range(n_tensor)
        ]
        come.append(lax.ppermute(block, ("dp", "tensor"), pairs))
    rows = jnp.where(
        x == 0, jnp.concatenate(come, axis=1), jnp.concatenate(come[::-1], axis=1)
    )
    return (rows, *others)


def shards(
    text_states,
    image_states,
    out_grad,
    text_lengths,
    query_weight,
    key_weight,
    value_weight,
    out_weight,
):
    samples, tok_rows, width = text_states.shape
    image_own = image_states.shape[1]
    line = Line()
    n_dp = line.n_dp
    n_tensor = lax.axis_size("tensor")
    dp_at, tensor_at = lax.axis_index("dp"), lax.axis_index("tensor")
    x, quarter = dp_at % 2, tensor_at % 4
    place = jnp.stack([dp_at // 2, x, quarter, tensor_at]).astype(jnp.int32)
    rows = samples * tok_rows
    image_rows = samples * image_own
    images = n_dp * image_rows
    local_cols = query_weight.shape[1]
    own_width = query_weight.shape[0]
    half_cols = local_cols // 2
    shape = jax.ShapeDtypeStruct

    def tensor_swap(block, bit):
        return lax.ppermute(block, "tensor", [(t, t ^ bit) for t in range(n_tensor)])

    positions = dp_at * tok_rows + lax.iota(jnp.int32, tok_rows)
    live_rows = positions[None, :] < text_lengths[:, None]
    grad_live = jnp.where(live_rows[..., None], out_grad, jnp.zeros_like(out_grad))
    text_flat = text_states.reshape(rows, width)
    live_flat = grad_live.reshape(rows, width)
    image_flat = image_states.reshape(image_rows, width)

    gate = lax.optimization_barrier

    relayed = line.n_z == 4
    wq_moved = line.first(query_weight)
    image_cols = lax.all_to_all(image_flat, "dp", split_axis=1, concat_axis=0, tiled=True)
    wo_keep = lax.dynamic_slice_in_dim(out_weight, x * half_cols, half_cols, 0)
    wo_send = lax.dynamic_slice_in_dim(out_weight, (1 - x) * half_cols, half_cols, 0)
    wo_pair = jnp.concatenate([wo_keep, line.swap(wo_send)], axis=1)
    quarter_cols = width // 4
    live_part = lax.dynamic_slice_in_dim(live_flat, quarter * quarter_cols, quarter_cols, 1)
    live_here = line.swap(live_part)
    image_cols, wo_pair, live_here, query_weight, *wq_moved = gate(
        (image_cols, wo_pair, live_here, query_weight, *wq_moved)
    )

    n_moved = len(wq_moved)
    planes = [(0, 1, 2), (1, 2, 3)] if relayed else [None] * n_moved
    wq_two = line.second(wq_moved)
    wo_moved = line.first(wo_pair)
    above, wq_other = gate((wq_moved[0], line.swap(query_weight)))
    wq_others = [wq_other, line.swap(above, planes[0])]
    part_kv = jnp.concatenate(
        [matmul(image_cols, key_weight), matmul(image_cols, value_weight)], axis=1
    )
    part_kv = part_kv.reshape(n_dp, image_rows, 2 * local_cols)
    kv_own = jnp.sum(lax.all_to_all(part_kv, "dp", split_axis=0, concat_axis=0), axis=0)
    kv_own, live_here, *staged = gate(
        (kv_own.astype(BF16), live_here, *wq_others, *wq_moved, *wq_two, *wo_moved)
    )
    wq_others, staged = staged[:2], staged[2:]
    wq_moved, wq_two, wo_moved = staged[:n_moved], staged[n_moved:-n_moved], staged[-n_moved:]

    def everywhere(values):
        copies = jnp.broadcast_to(values[None], (n_dp, *values.shape))
        return lax.all_to_all(copies, "dp", split_axis=0, concat_axis=0)

    wq_last = line.third(wq_two)
    wo_two = line.second(wo_moved)
    wq_others += [line.swap(block, at) for block, at in zip(wq_moved[1:], planes[1:])]
    wq_others += [line.swap(block) for block in wq_last[:1]]
    kv_all = everywhere(kv_own).reshape(images, 2 * local_cols)
    kv_all, live_here, wo_pair, live_flat, *staged = gate(
        (kv_all, live_here, wo_pair, live_flat, *wo_two, *wq_last, *wq_others)
    )
    wo_two, staged = staged[: len(wo_two)], staged[len(wo_two) :]
    wq_last, wq_others = staged[: len(wq_last)], staged[len(wq_last) :]

    wo_last = line.third(wo_two)
    quarter_rows = rows // 4
    live_rows = lax.dynamic_slice_in_dim(live_flat, quarter * quarter_rows, quarter_rows, 0)
    live_mine = lax.all_to_all(
        live_rows.reshape(quarter_rows, n_dp, own_width), "dp", split_axis=1, concat_axis=0
    )
    live_mine = live_mine.reshape(n_dp, quarter_rows, own_width)
    by_y = tensor_swap(live_here, 2)
    live_pieces = [live_here, tensor_swap(live_here, 1), by_y, tensor_swap(by_y, 1)]
    wq_others += [line.swap(block, (0, 3)) for block in wq_last[1:]]
    arrivals = [query_weight, *wq_moved, *wq_last]
    early = range(4 if relayed else len(arrivals))
    late = range(len(early), len(arrivals))
    query_part = call(
        functools.partial(query_kernel, line, relayed, early),
        place,
        (text_flat, *arrivals[: len(early)], *wq_others[: len(early)]),
        [shape((rows, local_cols), F32)],
        (),
        2 * rows * width * local_cols,
    )
    half = shape((rows, half_cols), F32)
    wo_early = [wo_pair, *wo_moved]
    grad_parts = call(
        functools.partial(grad_kernel, line, range(len(wo_early)), 0),
        place,
        (live_flat, *live_pieces, *wo_early),
        [half] * 2,
        (),
        rows * width * local_cols,
    )

    query_part, *grad_parts = gate((query_part, *grad_parts))

    wo_late = range(len(wo_early), len(wo_early) + len(wo_last))
    grad_keep, grad_send = call(
        functools.partial(grad_kernel, line, wo_late, 2),
        place,
        (live_flat, *live_pieces, *grad_parts, *wo_last),
        [shape((rows, half_cols), BF16)] * 2,
        [pltpu.VMEM((rows, half_cols), F32)] * 2,
        rows * width * local_cols,
    )
    text_flat, live_mine, grad_keep, grad_send = gate(
        (text_flat, live_mine, grad_keep, grad_send)
    )
    grad_come = line.swap(grad_send)
    queries, attended = call(
        functools.partial(forward_kernel, line, relayed, late, image_own),
        place,
        (text_flat, kv_all, query_part, *arrivals[len(early) :], *wq_others[len(early) :]),
        [shape((rows, local_cols), BF16)] * 2,
        [pltpu.VMEM((rows, local_cols), F32)],
        rows * width * local_cols,
    )
    wq_blocks = [*arrivals, *wq_others]

    att_next = [line.shift(attended, m) for m in (1, line.n_z - 1)]
    att_swapped = line.swap(attended)
    live_y = tensor_swap(live_mine, 2)

    query_grad, kv_part = call(
        functools.partial(backward_kernel, image_own),
        place,
        (queries, kv_all, grad_keep, grad_come),
        [shape((rows, local_cols), BF16), shape((images, 2 * local_cols), F32)],
        (),
        10 * images * rows * local_cols,
    )
    kv_part = kv_part.reshape(n_dp, image_rows, 2 * local_cols)
    kv_grad = jnp.sum(lax.all_to_all(kv_part, "dp", split_axis=0, concat_axis=0), axis=0)
    chunk = n_dp // n_tensor
    term = call(
        functools.partial(term_kernel, line, relayed),
        place,
        (query_grad, *wq_blocks),
        [shape((n_tensor, chunk, rows, own_width), BF16)],
        (),
        2 * rows * width * local_cols,
    )
    kv_grad, term, live_y = gate((kv_grad.astype(BF16), term, live_y))
    kv_grad_all = everywhere(kv_grad).reshape(images, 2 * local_cols)
    live_pair = jnp.stack([live_mine, live_y])

    text_parts = [tensor_swap(term[k], k) for k in range(2, n_tensor)]
    attended, att_swapped, *att_next = gate((attended, att_swapped, *att_next))
    att_far = [line.shift(attended, m) for m in range(2, line.n_z - 1)]
    att_other_next = [line.swap(block) for block in att_next]
    kv_grad_all, term, live_pair, *staged = gate(
        (kv_grad_all, term, live_pair, *att_other_next, *text_parts, *att_far)
    )
    att_other_next, staged = staged[:2], staged[2:]
    text_parts, att_far = staged[: n_tensor - 2], staged[n_tensor - 2 :]

    att_other_far = [line.swap(block) for block in att_far]
    live_core = tensor_swap(live_pair, 1)
    text_parts.append(tensor_swap(term[1], 1))
    image_term = matmul(kv_grad_all[:, :local_cols], key_weight, BACK)
    image_term = image_term + matmul(kv_grad_all[:, local_cols:], value_weight, BACK)
    image_grad, live_core, text_parts[-1], *att_other_far = to_owner(
        line, image_term.astype(BF16), live_core, text_parts[-1], *att_other_far
    )
    image_grad = image_grad.reshape(samples, image_own, width // n_tensor)
    text_grad = call(
        sum_kernel, place, (term, *text_parts), [shape((rows, width // n_tensor), BF16)]
    )
    text_grad = text_grad.reshape(samples, tok_rows, width // n_tensor)

    att_blocks = [attended, att_next[0], *att_far, att_next[1]]
    att_others = [att_swapped, att_other_next[0], *att_other_far, att_other_next[1]]
    weight_grad = call(
        functools.partial(weight_grad_kernel, line),
        place,
        (live_pair, live_core, *att_blocks, *att_others),
        [shape((local_cols, own_width), BF16)],
        [pltpu.VMEM((local_cols, own_width), F32)],
        2 * n_dp * rows * local_cols * own_width,
    )
    return text_grad, image_grad, weight_grad


def solution(mesh):
    return jax.shard_map(
        shards,
        mesh=mesh,
        in_specs=(
            P(None, "dp", None),
            P(None, "dp", None),
            P(None, "dp", None),
            P(),
            P("dp", "tensor"),
            P("dp", "tensor"),
            P("dp", "tensor"),
            P("tensor", "dp"),
        ),
        out_specs=(P(None, "dp", "tensor"), P(None, "dp", "tensor"), P("tensor", "dp")),
        check_vma=False,
    )
```

```python
import functools

import jax
import jax.numpy as jnp
from jax import lax
from jax.experimental import pallas as pl
from jax.experimental.pallas import tpu as pltpu
from jax.sharding import PartitionSpec as P

HEAD_DIM = 128
F32 = jnp.float32
BF16 = jnp.bfloat16
BACK = (((1,), (1,)), ((), ()))
FIRST = (((0,), (0,)), ((), ()))
VMEM_LIMIT = 60 * 1024 * 1024


def matmul(a, b, dims=None):
    if dims is None:
        return jnp.dot(a, b, preferred_element_type=F32)
    return lax.dot_general(a, b, dims, preferred_element_type=F32)


class Line:
    def __init__(self):
        self.n_dp = lax.axis_size("dp")
        self.n_z = self.n_dp // 2

    def move(self, block, moves):
        pairs = [(2 * a + e, 2 * b + e) for a, b in moves for e in range(2)]
        return lax.ppermute(block, "dp", pairs)

    def swap(self, block, planes=None):
        planes = range(self.n_z) if planes is None else planes
        pairs = [(2 * a + e, 2 * a + 1 - e) for a in planes for e in range(2)]
        return lax.ppermute(block, "dp", pairs)

    def shift(self, block, distance):
        n = self.n_z
        return self.move(block, [((a + distance) % n, a) for a in range(n)])

    def first(self, block):
        if self.n_z != 4:
            return [self.shift(block, m) for m in range(1, self.n_z)]
        above = self.move(block, [(1, 0), (2, 1), (3, 2)])
        below = self.move(block, [(0, 1), (1, 2), (2, 3)])
        return [above, below]

    def second(self, moved):
        if self.n_z != 4:
            return []
        return [self.move(moved[0], [(1, 0), (2, 1)]), self.move(moved[1], [(1, 2), (2, 3)])]

    def third(self, forwarded):
        if self.n_z != 4:
            return []
        across = jnp.where(lax.axis_index("dp") < 4, forwarded[0], forwarded[1])
        return [across, self.move(across, [(1, 0), (2, 3)])]

    def slots(self, z, relayed):
        if not relayed:
            return [(m, None) for m in range(self.n_z)]
        return [
            (0, None),
            (1, z < 3),
            (3, z > 0),
            (2, None),
            (jnp.where(z == 3, 1, 3), (z == 3) | (z == 0)),
        ]


def each_block(line, place, relayed, which, body):
    z, x = place[0], place[1]
    slots = line.slots(z, relayed)
    for j, at in enumerate(which):
        m, came = slots[at]
        plane = lax.rem(z + m, line.n_z)
        for e in range(2):
            index = 2 * plane + (x if e == 0 else 1 - x)
            if came is None:
                body(j, e, index)
            else:
                pl.when(came)(functools.partial(body, j, e, index))


def columns(index, size):
    return pl.ds(pl.multiple_of(index * size, size), size)


def probabilities(query, key, image_own):
    scores = matmul(key, query, BACK) * HEAD_DIM ** (-0.5)
    image = lax.broadcasted_iota(jnp.int32, scores.shape, 0)
    token = lax.broadcasted_iota(jnp.int32, scores.shape, 1)
    image_sample = lax.rem(lax.div(image, image_own), 2)
    same = image_sample == lax.div(token, scores.shape[1] // 2)
    scores = jnp.where(same, scores, -1e30)
    peak = jnp.max(scores, axis=0, keepdims=True)
    expo = jnp.where(same, jnp.exp(scores - peak), 0.0)
    return expo / jnp.sum(expo, axis=0, keepdims=True)


def query_kernel(line, relayed, which, place, text, *refs):
    n = len(which)
    weights, total = (refs[:n], refs[n : 2 * n]), refs[-1]
    own_width = weights[0][0].shape[0]
    total[...] = jnp.zeros_like(total)

    def add(j, e, index):
        total[...] += matmul(text[:, columns(index, own_width)], weights[e][j][...])

    each_block(line, place, relayed, which, add)


def forward_kernel(line, relayed, which, image_own, place, text, kv, part, *refs):
    n = len(which)
    weights, (query_out, attended_out, total) = (refs[:n], refs[n : 2 * n]), refs[2 * n :]
    rows, cols = total.shape
    total[...] = part[...]

    def add(j, e, index):
        weight = weights[e][j]
        total[...] += matmul(text[:, columns(index, weight.shape[0])], weight[...])

    each_block(line, place, relayed, which, add)
    query_out[...] = total[...].astype(BF16)
    part_rows = rows // 4
    quarter = place[2]
    for h in range(cols // HEAD_DIM):
        at = slice(h * HEAD_DIM, (h + 1) * HEAD_DIM)
        value = kv[:, cols + h * HEAD_DIM : cols + (h + 1) * HEAD_DIM]
        prob = probabilities(query_out[:, at], kv[:, at], image_own)
        attended = matmul(prob.astype(BF16), value, FIRST).astype(BF16)
        for r in range(4):
            low_bit = (quarter + r) % 2
            high_bit = (quarter // 2 + r // 2) % 2
            start = pl.multiple_of((2 * low_bit + high_bit) * part_rows, part_rows)
            attended_out[pl.ds(start, part_rows), at] = attended[
                r * part_rows : (r + 1) * part_rows
            ]


def grad_kernel(line, which, parts, place, live, mine, by_core, by_y, by_both, *refs):
    before, refs = refs[:parts], refs[parts:]
    weights, outs = refs[: len(which)], refs[len(which) :]
    cut = line.n_dp // 4
    keep, send = outs[-2:]
    keep[...] = before[0][...] if parts else jnp.zeros_like(keep)
    send[...] = before[1][...] if parts else jnp.zeros_like(send)

    def add(j, e, index):
        own_width = weights[j].shape[1] // 2
        weight = weights[j][:, e * own_width : (e + 1) * own_width]
        keep[...] += matmul(live[:, columns(index, own_width)], weight, BACK)
        inner = columns(lax.rem(index, cut), own_width)
        member = lax.bitwise_xor(lax.div(index, cut), place[2])
        other = mine[:, inner]
        for at, piece in ((1, by_core), (2, by_y), (3, by_both)):
            other = jnp.where(member == at, piece[:, inner], other)
        send[...] += matmul(other, weight, BACK)

    each_block(line, place, line.n_z == 4, which, add)
    if parts:
        outs[0][...] = keep[...].astype(BF16)
        outs[1][...] = send[...].astype(BF16)


def backward_kernel(image_own, place, query, kv, keep, come, query_grad, kv_grad):
    cols = query.shape[1]
    half = cols // 2
    x = place[1]
    for h in range(cols // HEAD_DIM):
        at = slice(h * HEAD_DIM, (h + 1) * HEAD_DIM)
        value_at = slice(cols + h * HEAD_DIM, cols + (h + 1) * HEAD_DIM)
        side = h * HEAD_DIM // half
        inner = slice(h * HEAD_DIM - side * half, (h + 1) * HEAD_DIM - side * half)
        grad = jnp.where(x == side, keep[:, inner], come[:, inner])
        prob = probabilities(query[:, at], kv[:, at], image_own)
        kv_grad[:, value_at] = matmul(prob.astype(BF16), grad)
        prob_grad = matmul(kv[:, value_at], grad, BACK)
        delta = jnp.sum(prob * prob_grad, axis=0, keepdims=True)
        score_grad = (prob * (prob_grad - delta) * HEAD_DIM ** (-0.5)).astype(BF16)
        kv_grad[:, at] = matmul(score_grad, query[:, at])
        query_grad[:, at] = matmul(score_grad, kv[:, at], FIRST).astype(BF16)


def term_kernel(line, relayed, place, query_grad, *refs):
    out = refs[-1]
    n = (len(refs) - 1) // 2
    weights = (refs[:n], refs[n : 2 * n])
    chunk = out.shape[1]

    def write(i, e, index):
        term = matmul(query_grad[...], weights[e][i][...], BACK)
        member = lax.bitwise_xor(lax.div(index, chunk), place[3])
        out[member, lax.rem(index, chunk)] = term.astype(BF16)

    each_block(line, place, relayed, range(n), write)


def weight_grad_kernel(line, place, *refs):
    live, refs = refs[:2], refs[2:]
    n = (len(refs) - 2) // 2
    attended, (out, total) = (refs[:n], refs[n : 2 * n]), refs[2 * n :]
    total[...] = jnp.zeros_like(total)

    def add(i, e, index):
        block = jnp.concatenate([part[i, index] for part in live for i in range(2)], axis=0)
        term = matmul(attended[e][i][...], block, FIRST)
        total[...] += term.astype(BF16).astype(F32)

    each_block(line, place, False, range(n), add)
    out[...] = total[...].astype(BF16)


def sum_kernel(place, term, *refs):
    parts, out = refs[:-1], refs[-1]
    width = term.shape[3]
    for c in range(term.shape[1]):
        total = term[0, c].astype(F32)
        for part in parts:
            total = total + part[c].astype(F32)
        out[:, c * width : (c + 1) * width] = total.astype(BF16)


def call(kernel, place, operands, outs, scratch=(), flops=0):
    moved = sum(a.size * a.dtype.itemsize for a in (*operands, *outs))
    single = len(outs) == 1
    return pl.pallas_call(
        kernel,
        out_shape=outs[0] if single else outs,
        in_specs=[pl.BlockSpec(memory_space=pltpu.SMEM)]
        + [pl.BlockSpec(memory_space=pltpu.VMEM)] * len(operands),
        out_specs=pl.BlockSpec(memory_space=pltpu.VMEM)
        if single
        else [pl.BlockSpec(memory_space=pltpu.VMEM)] * len(outs),
        scratch_shapes=list(scratch),
        compiler_params=pltpu.CompilerParams(vmem_limit_bytes=VMEM_LIMIT),
        cost_estimate=pl.CostEstimate(flops=flops, bytes_accessed=moved, transcendentals=0),
    )(place, *operands)


def to_owner(line, terms, *others):
    n_dp, n_tensor = line.n_dp, lax.axis_size("tensor")
    images, cols = terms.shape
    if line.n_z != n_tensor:
        terms = lax.all_to_all(terms, "dp", split_axis=0, concat_axis=1, tiled=True)
        terms = terms.reshape(images // n_dp, n_tensor, n_dp * cols // n_tensor)
        parts = lax.all_to_all(terms, "tensor", split_axis=1, concat_axis=0)
        return (jnp.sum(parts.astype(F32), axis=0).astype(BF16), *others)
    parts = lax.all_to_all(
        terms.reshape(n_tensor, images // n_tensor, cols), "tensor", split_axis=0, concat_axis=0
    )
    total = jnp.sum(parts.astype(F32), axis=0).astype(BF16)
    total, *others = lax.optimization_barrier((total, *others))
    total = total.reshape(2, images // n_dp, cols)
    x = lax.axis_index("dp") % 2
    come = []
    for other in range(2):
        block = jnp.where(x == other, total[0], total[1])
        pairs = [
            ((2 * z + e) * n_tensor + t, (2 * t + (e ^ other)) * n_tensor + z)
            for z in range(line.n_z)
            for e in range(2)
            for t in range(n_tensor)
        ]
        come.append(lax.ppermute(block, ("dp", "tensor"), pairs))
    rows = jnp.where(
        x == 0, jnp.concatenate(come, axis=1), jnp.concatenate(come[::-1], axis=1)
    )
    return (rows, *others)


def shards(
    text_states,
    image_states,
    out_grad,
    text_lengths,
    query_weight,
    key_weight,
    value_weight,
    out_weight,
):
    samples, tok_rows, width = text_states.shape
    image_own = image_states.shape[1]
    line = Line()
    n_dp = line.n_dp
    n_tensor = lax.axis_size("tensor")
    dp_at, tensor_at = lax.axis_index("dp"), lax.axis_index("tensor")
    x, quarter = dp_at % 2, tensor_at % 4
    place = jnp.stack([dp_at // 2, x, quarter, tensor_at]).astype(jnp.int32)
    rows = samples * tok_rows
    image_rows = samples * image_own
    images = n_dp * image_rows
    local_cols = query_weight.shape[1]
    own_width = query_weight.shape[0]
    half_cols = local_cols // 2
    shape = jax.ShapeDtypeStruct

    def tensor_swap(block, bit):
        return lax.ppermute(block, "tensor", [(t, t ^ bit) for t in range(n_tensor)])

    positions = dp_at * tok_rows + lax.iota(jnp.int32, tok_rows)
    live_rows = positions[None, :] < text_lengths[:, None]
    grad_live = jnp.where(live_rows[..., None], out_grad, jnp.zeros_like(out_grad))
    text_flat = text_states.reshape(rows, width)
    live_flat = grad_live.reshape(rows, width)
    image_flat = image_states.reshape(image_rows, width)

    gate = lax.optimization_barrier

    relayed = line.n_z == 4
    wq_moved = line.first(query_weight)
    image_cols = lax.all_to_all(image_flat, "dp", split_axis=1, concat_axis=0, tiled=True)
    wo_keep = lax.dynamic_slice_in_dim(out_weight, x * half_cols, half_cols, 0)
    wo_send = lax.dynamic_slice_in_dim(out_weight, (1 - x) * half_cols, half_cols, 0)
    wo_pair = jnp.concatenate([wo_keep, line.swap(wo_send)], axis=1)
    quarter_cols = width // 4
    live_part = lax.dynamic_slice_in_dim(live_flat, quarter * quarter_cols, quarter_cols, 1)
    live_here = line.swap(live_part)
    image_cols, wo_pair, live_here, query_weight, *wq_moved = gate(
        (image_cols, wo_pair, live_here, query_weight, *wq_moved)
    )

    n_moved = len(wq_moved)
    planes = [(0, 1, 2), (1, 2, 3)] if relayed else [None] * n_moved
    wq_two = line.second(wq_moved)
    wo_moved = line.first(wo_pair)
    above, wq_other = gate((wq_moved[0], line.swap(query_weight)))
    wq_others = [wq_other, line.swap(above, planes[0])]
    part_kv = jnp.concatenate(
        [matmul(image_cols, key_weight), matmul(image_cols, value_weight)], axis=1
    )
    part_kv = part_kv.reshape(n_dp, image_rows, 2 * local_cols)
    kv_own = jnp.sum(lax.all_to_all(part_kv, "dp", split_axis=0, concat_axis=0), axis=0)
    kv_own, live_here, *staged = gate(
        (kv_own.astype(BF16), live_here, *wq_others, *wq_moved, *wq_two, *wo_moved)
    )
    wq_others, staged = staged[:2], staged[2:]
    wq_moved, wq_two, wo_moved = staged[:n_moved], staged[n_moved:-n_moved], staged[-n_moved:]

    def everywhere(values):
        copies = jnp.broadcast_to(values[None], (n_dp, *values.shape))
        return lax.all_to_all(copies, "dp", split_axis=0, concat_axis=0)

    wq_last = line.third(wq_two)
    wo_two = line.second(wo_moved)
    wq_others += [line.swap(block, at) for block, at in zip(wq_moved[1:], planes[1:])]
    wq_others += [line.swap(block) for block in wq_last[:1]]
    kv_all = everywhere(kv_own).reshape(images, 2 * local_cols)
    kv_all, live_here, wo_pair, live_flat, *staged = gate(
        (kv_all, live_here, wo_pair, live_flat, *wo_two, *wq_last, *wq_others)
    )
    wo_two, staged = staged[: len(wo_two)], staged[len(wo_two) :]
    wq_last, wq_others = staged[: len(wq_last)], staged[len(wq_last) :]

    wo_last = line.third(wo_two)
    quarter_rows = rows // 4
    live_rows = lax.dynamic_slice_in_dim(live_flat, quarter * quarter_rows, quarter_rows, 0)
    live_mine = lax.all_to_all(
        live_rows.reshape(quarter_rows, n_dp, own_width), "dp", split_axis=1, concat_axis=0
    )
    live_mine = live_mine.reshape(n_dp, quarter_rows, own_width)
    by_y = tensor_swap(live_here, 2)
    live_pieces = [live_here, tensor_swap(live_here, 1), by_y, tensor_swap(by_y, 1)]
    wq_others += [line.swap(block, (0, 3)) for block in wq_last[1:]]
    arrivals = [query_weight, *wq_moved, *wq_last]
    early = range(4 if relayed else len(arrivals))
    late = range(len(early), len(arrivals))
    query_part = call(
        functools.partial(query_kernel, line, relayed, early),
        place,
        (text_flat, *arrivals[: len(early)], *wq_others[: len(early)]),
        [shape((rows, local_cols), F32)],
        (),
        2 * rows * width * local_cols,
    )

    half = shape((rows, half_cols), F32)
    wo_early = [wo_pair, *wo_moved]
    grad_parts = call(
        functools.partial(grad_kernel, line, range(len(wo_early)), 0),
        place,
        (live_flat, *live_pieces, *wo_early),
        [half] * 2,
        (),
        rows * width * local_cols,
    )

    query_part, *grad_parts = gate((query_part, *grad_parts))

    wo_late = range(len(wo_early), len(wo_early) + len(wo_last))
    grad_keep, grad_send = call(
        functools.partial(grad_kernel, line, wo_late, 2),
        place,
        (live_flat, *live_pieces, *grad_parts, *wo_last),
        [shape((rows, half_cols), BF16)] * 2,
        [pltpu.VMEM((rows, half_cols), F32)] * 2,
        rows * width * local_cols,
    )
    text_flat, live_mine, grad_keep, grad_send = gate(
        (text_flat, live_mine, grad_keep, grad_send)
    )
    grad_come = line.swap(grad_send)
    queries, attended = call(
        functools.partial(forward_kernel, line, relayed, late, image_own),
        place,
        (text_flat, kv_all, query_part, *arrivals[len(early) :], *wq_others[len(early) :]),
        [shape((rows, local_cols), BF16)] * 2,
        [pltpu.VMEM((rows, local_cols), F32)],
        rows * width * local_cols,
    )
    wq_blocks = [*arrivals, *wq_others]

    att_next = [line.shift(attended, m) for m in (1, line.n_z - 1)]
    attended, grad_come = gate((attended, grad_come))
    att_swapped = line.swap(attended)
    live_y = tensor_swap(live_mine, 2)

    query_grad, kv_part = call(
        functools.partial(backward_kernel, image_own),
        place,
        (queries, kv_all, grad_keep, grad_come),
        [shape((rows, local_cols), BF16), shape((images, 2 * local_cols), F32)],
        (),
        10 * images * rows * local_cols,
    )
    chunk = n_dp // n_tensor
    term = call(
        functools.partial(term_kernel, line, relayed),
        place,
        (query_grad, *wq_blocks),
        [shape((n_tensor, chunk, rows, own_width), BF16)],
        (),
        2 * rows * width * local_cols,
    )
    kv_part, term, live_y, attended, att_swapped, *att_next = gate(
        (kv_part, term, live_y, attended, att_swapped, *att_next)
    )

    kv_part = kv_part.reshape(n_dp, image_rows, 2 * local_cols)
    kv_grad = jnp.sum(lax.all_to_all(kv_part, "dp", split_axis=0, concat_axis=0), axis=0)
    kv_grad_all = everywhere(kv_grad.astype(BF16)).reshape(images, 2 * local_cols)
    text_parts = [tensor_swap(term[k], k) for k in range(2, n_tensor)]
    att_far = [line.shift(attended, m) for m in range(2, line.n_z - 1)]
    att_other_next = [line.swap(block) for block in att_next]
    live_pair = jnp.stack([live_mine, live_y])
    kv_grad_all, term, live_pair, *staged = gate(
        (kv_grad_all, term, live_pair, *att_other_next, *text_parts, *att_far)
    )
    att_other_next, staged = staged[:2], staged[2:]
    text_parts, att_far = staged[: n_tensor - 2], staged[n_tensor - 2 :]

    att_other_far = [line.swap(block) for block in att_far]
    live_core = tensor_swap(live_pair, 1)
    text_parts.append(tensor_swap(term[1], 1))
    image_term = matmul(kv_grad_all[:, :local_cols], key_weight, BACK)
    image_term = image_term + matmul(kv_grad_all[:, local_cols:], value_weight, BACK)
    text_grad = call(
        sum_kernel, place, (term, *text_parts), [shape((rows, width // n_tensor), BF16)]
    )
    image_grad, live_core, text_grad, *att_other_far = to_owner(
        line, image_term.astype(BF16), live_core, text_grad, *att_other_far
    )
    image_grad = image_grad.reshape(samples, image_own, width // n_tensor)
    text_grad = text_grad.reshape(samples, tok_rows, width // n_tensor)

    att_blocks = [attended, att_next[0], *att_far, att_next[1]]
    att_others = [att_swapped, att_other_next[0], *att_other_far, att_other_next[1]]
    weight_grad = call(
        functools.partial(weight_grad_kernel, line),
        place,
        (live_pair, live_core, *att_blocks, *att_others),
        [shape((local_cols, own_width), BF16)],
        [pltpu.VMEM((local_cols, own_width), F32)],
        2 * n_dp * rows * local_cols * own_width,
    )
    return text_grad, image_grad, weight_grad


def solution(mesh):
    return jax.shard_map(
        shards,
        mesh=mesh,
        in_specs=(
            P(None, "dp", None),
            P(None, "dp", None),
            P(None, "dp", None),
            P(),
            P("dp", "tensor"),
            P("dp", "tensor"),
            P("dp", "tensor"),
            P("tensor", "dp"),
        ),
        out_specs=(P(None, "dp", "tensor"), P(None, "dp", "tensor"), P("tensor", "dp")),
        check_vma=False,
    )
```

```python
import functools

import jax
import jax.numpy as jnp
from jax import lax
from jax.experimental import pallas as pl
from jax.experimental.pallas import tpu as pltpu
from jax.sharding import PartitionSpec as P

HEAD_DIM = 128
F32 = jnp.float32
BF16 = jnp.bfloat16
BACK = (((1,), (1,)), ((), ()))
FIRST = (((0,), (0,)), ((), ()))
VMEM_LIMIT = 60 * 1024 * 1024


def matmul(a, b, dims=None):
    if dims is None:
        return jnp.dot(a, b, preferred_element_type=F32)
    return lax.dot_general(a, b, dims, preferred_element_type=F32)


class Line:
    def __init__(self):
        self.n_dp = lax.axis_size("dp")
        self.n_z = self.n_dp // 2

    def move(self, block, moves):
        pairs = [(2 * a + e, 2 * b + e) for a, b in moves for e in range(2)]
        return lax.ppermute(block, "dp", pairs)

    def swap(self, block, planes=None):
        planes = range(self.n_z) if planes is None else planes
        pairs = [(2 * a + e, 2 * a + 1 - e) for a in planes for e in range(2)]
        return lax.ppermute(block, "dp", pairs)

    def shift(self, block, distance):
        n = self.n_z
        return self.move(block, [((a + distance) % n, a) for a in range(n)])

    def first(self, block):
        if self.n_z != 4:
            return [self.shift(block, m) for m in range(1, self.n_z)]
        above = self.move(block, [(1, 0), (2, 1), (3, 2)])
        below = self.move(block, [(0, 1), (1, 2), (2, 3)])
        return [above, below]

    def second(self, moved):
        if self.n_z != 4:
            return []
        return [self.move(moved[0], [(1, 0), (2, 1)]), self.move(moved[1], [(1, 2), (2, 3)])]

    def third(self, forwarded):
        if self.n_z != 4:
            return []
        across = jnp.where(lax.axis_index("dp") < 4, forwarded[0], forwarded[1])
        return [across, self.move(across, [(1, 0), (2, 3)])]

    def slots(self, z, relayed):
        if not relayed:
            return [(m, None) for m in range(self.n_z)]
        return [
            (0, None),
            (1, z < 3),
            (3, z > 0),
            (2, None),
            (jnp.where(z == 3, 1, 3), (z == 3) | (z == 0)),
        ]


def each_block(line, place, relayed, which, body):
    z, x = place[0], place[1]
    slots = line.slots(z, relayed)
    for j, at in enumerate(which):
        m, came = slots[at]
        plane = lax.rem(z + m, line.n_z)
        for e in range(2):
            index = 2 * plane + (x if e == 0 else 1 - x)
            if came is None:
                body(j, e, index)
            else:
                pl.when(came)(functools.partial(body, j, e, index))


def columns(index, size):
    return pl.ds(pl.multiple_of(index * size, size), size)


def probabilities(query, key, image_own):
    scores = matmul(key, query, BACK) * HEAD_DIM ** (-0.5)
    image = lax.broadcasted_iota(jnp.int32, scores.shape, 0)
    token = lax.broadcasted_iota(jnp.int32, scores.shape, 1)
    image_sample = lax.rem(lax.div(image, image_own), 2)
    same = image_sample == lax.div(token, scores.shape[1] // 2)
    scores = jnp.where(same, scores, -1e30)
    peak = jnp.max(scores, axis=0, keepdims=True)
    expo = jnp.where(same, jnp.exp(scores - peak), 0.0)
    return expo / jnp.sum(expo, axis=0, keepdims=True)


def query_kernel(line, relayed, which, place, text, *refs):
    n = len(which)
    weights, total = (refs[:n], refs[n : 2 * n]), refs[-1]
    own_width = weights[0][0].shape[0]
    total[...] = jnp.zeros_like(total)

    def add(j, e, index):
        total[...] += matmul(text[:, columns(index, own_width)], weights[e][j][...])

    each_block(line, place, relayed, which, add)


def forward_kernel(line, relayed, which, image_own, place, text, kv, part, *refs):
    n = len(which)
    weights, (query_out, attended_out, total) = (refs[:n], refs[n : 2 * n]), refs[2 * n :]
    rows, cols = total.shape
    total[...] = part[...]

    def add(j, e, index):
        weight = weights[e][j]
        total[...] += matmul(text[:, columns(index, weight.shape[0])], weight[...])

    each_block(line, place, relayed, which, add)
    query_out[...] = total[...].astype(BF16)
    part_rows = rows // 4
    quarter = place[2]
    for h in range(cols // HEAD_DIM):
        at = slice(h * HEAD_DIM, (h + 1) * HEAD_DIM)
        value = kv[:, cols + h * HEAD_DIM : cols + (h + 1) * HEAD_DIM]
        prob = probabilities(query_out[:, at], kv[:, at], image_own)
        attended = matmul(prob.astype(BF16), value, FIRST).astype(BF16)
        for r in range(4):
            low_bit = (quarter + r) % 2
            high_bit = (quarter // 2 + r // 2) % 2
            start = pl.multiple_of((2 * low_bit + high_bit) * part_rows, part_rows)
            attended_out[pl.ds(start, part_rows), at] = attended[
                r * part_rows : (r + 1) * part_rows
            ]


def grad_kernel(line, which, parts, place, live, mine, by_core, by_y, by_both, *refs):
    before, refs = refs[:parts], refs[parts:]
    weights, outs = refs[: len(which)], refs[len(which) :]
    cut = line.n_dp // 4
    keep, send = outs[-2:]
    keep[...] = before[0][...] if parts else jnp.zeros_like(keep)
    send[...] = before[1][...] if parts else jnp.zeros_like(send)

    def add(j, e, index):
        own_width = weights[j].shape[1] // 2
        weight = weights[j][:, e * own_width : (e + 1) * own_width]
        keep[...] += matmul(live[:, columns(index, own_width)], weight, BACK)
        inner = columns(lax.rem(index, cut), own_width)
        member = lax.bitwise_xor(lax.div(index, cut), place[2])
        other = mine[:, inner]
        for at, piece in ((1, by_core), (2, by_y), (3, by_both)):
            other = jnp.where(member == at, piece[:, inner], other)
        send[...] += matmul(other, weight, BACK)

    each_block(line, place, line.n_z == 4, which, add)
    if parts:
        outs[0][...] = keep[...].astype(BF16)
        outs[1][...] = send[...].astype(BF16)


def backward_kernel(image_own, place, query, kv, keep, come, query_grad, kv_grad):
    cols = query.shape[1]
    half = cols // 2
    x = place[1]
    for h in range(cols // HEAD_DIM):
        at = slice(h * HEAD_DIM, (h + 1) * HEAD_DIM)
        value_at = slice(cols + h * HEAD_DIM, cols + (h + 1) * HEAD_DIM)
        side = h * HEAD_DIM // half
        inner = slice(h * HEAD_DIM - side * half, (h + 1) * HEAD_DIM - side * half)
        grad = jnp.where(x == side, keep[:, inner], come[:, inner])
        prob = probabilities(query[:, at], kv[:, at], image_own)
        kv_grad[:, value_at] = matmul(prob.astype(BF16), grad)
        prob_grad = matmul(kv[:, value_at], grad, BACK)
        delta = jnp.sum(prob * prob_grad, axis=0, keepdims=True)
        score_grad = (prob * (prob_grad - delta) * HEAD_DIM ** (-0.5)).astype(BF16)
        kv_grad[:, at] = matmul(score_grad, query[:, at])
        query_grad[:, at] = matmul(score_grad, kv[:, at], FIRST).astype(BF16)


def term_kernel(line, relayed, place, query_grad, *refs):
    out = refs[-1]
    n = (len(refs) - 1) // 2
    weights = (refs[:n], refs[n : 2 * n])
    chunk = out.shape[1]

    def write(i, e, index):
        term = matmul(query_grad[...], weights[e][i][...], BACK)
        member = lax.bitwise_xor(lax.div(index, chunk), place[3])
        out[member, lax.rem(index, chunk)] = term.astype(BF16)

    each_block(line, place, relayed, range(n), write)


def weight_grad_kernel(line, place, *refs):
    live, refs = refs[:2], refs[2:]
    n = (len(refs) - 2) // 2
    attended, (out, total) = (refs[:n], refs[n : 2 * n]), refs[2 * n :]
    total[...] = jnp.zeros_like(total)

    def add(i, e, index):
        block = jnp.concatenate([part[i, index] for part in live for i in range(2)], axis=0)
        term = matmul(attended[e][i][...], block, FIRST)
        total[...] += term.astype(BF16).astype(F32)

    each_block(line, place, False, range(n), add)
    out[...] = total[...].astype(BF16)


def sum_kernel(place, term, *refs):
    parts, out = refs[:-1], refs[-1]
    width = term.shape[3]
    for c in range(term.shape[1]):
        total = term[0, c].astype(F32)
        for part in parts:
            total = total + part[c].astype(F32)
        out[:, c * width : (c + 1) * width] = total.astype(BF16)


def call(kernel, place, operands, outs, scratch=(), flops=0):
    moved = sum(a.size * a.dtype.itemsize for a in (*operands, *outs))
    single = len(outs) == 1
    return pl.pallas_call(
        kernel,
        out_shape=outs[0] if single else outs,
        in_specs=[pl.BlockSpec(memory_space=pltpu.SMEM)]
        + [pl.BlockSpec(memory_space=pltpu.VMEM)] * len(operands),
        out_specs=pl.BlockSpec(memory_space=pltpu.VMEM)
        if single
        else [pl.BlockSpec(memory_space=pltpu.VMEM)] * len(outs),
        scratch_shapes=list(scratch),
        compiler_params=pltpu.CompilerParams(vmem_limit_bytes=VMEM_LIMIT),
        cost_estimate=pl.CostEstimate(flops=flops, bytes_accessed=moved, transcendentals=0),
    )(place, *operands)


def to_owner(line, terms, *others):
    n_dp, n_tensor = line.n_dp, lax.axis_size("tensor")
    images, cols = terms.shape
    if line.n_z != n_tensor:
        terms = lax.all_to_all(terms, "dp", split_axis=0, concat_axis=1, tiled=True)
        terms = terms.reshape(images // n_dp, n_tensor, n_dp * cols // n_tensor)
        parts = lax.all_to_all(terms, "tensor", split_axis=1, concat_axis=0)
        return (jnp.sum(parts.astype(F32), axis=0).astype(BF16), *others)
    parts = lax.all_to_all(
        terms.reshape(n_tensor, images // n_tensor, cols), "tensor", split_axis=0, concat_axis=0
    )
    total = jnp.sum(parts.astype(F32), axis=0).astype(BF16)
    total, *others = lax.optimization_barrier((total, *others))
    total = total.reshape(2, images // n_dp, cols)
    x = lax.axis_index("dp") % 2
    come = []
    for other in range(2):
        block = jnp.where(x == other, total[0], total[1])
        pairs = [
            ((2 * z + e) * n_tensor + t, (2 * t + (e ^ other)) * n_tensor + z)
            for z in range(line.n_z)
            for e in range(2)
            for t in range(n_tensor)
        ]
        come.append(lax.ppermute(block, ("dp", "tensor"), pairs))
    rows = jnp.where(
        x == 0, jnp.concatenate(come, axis=1), jnp.concatenate(come[::-1], axis=1)
    )
    return (rows, *others)


def shards(
    text_states,
    image_states,
    out_grad,
    text_lengths,
    query_weight,
    key_weight,
    value_weight,
    out_weight,
):
    samples, tok_rows, width = text_states.shape
    image_own = image_states.shape[1]
    line = Line()
    n_dp = line.n_dp
    n_tensor = lax.axis_size("tensor")
    dp_at, tensor_at = lax.axis_index("dp"), lax.axis_index("tensor")
    x, quarter = dp_at % 2, tensor_at % 4
    place = jnp.stack([dp_at // 2, x, quarter, tensor_at]).astype(jnp.int32)
    rows = samples * tok_rows
    image_rows = samples * image_own
    images = n_dp * image_rows
    local_cols = query_weight.shape[1]
    own_width = query_weight.shape[0]
    half_cols = local_cols // 2
    shape = jax.ShapeDtypeStruct

    def tensor_swap(block, bit):
        return lax.ppermute(block, "tensor", [(t, t ^ bit) for t in range(n_tensor)])

    positions = dp_at * tok_rows + lax.iota(jnp.int32, tok_rows)
    live_rows = positions[None, :] < text_lengths[:, None]
    grad_live = jnp.where(live_rows[..., None], out_grad, jnp.zeros_like(out_grad))
    text_flat = text_states.reshape(rows, width)
    live_flat = grad_live.reshape(rows, width)
    image_flat = image_states.reshape(image_rows, width)

    gate = lax.optimization_barrier

    relayed = line.n_z == 4
    wq_moved = line.first(query_weight)
    image_cols = lax.all_to_all(image_flat, "dp", split_axis=1, concat_axis=0, tiled=True)
    wo_keep = lax.dynamic_slice_in_dim(out_weight, x * half_cols, half_cols, 0)
    wo_send = lax.dynamic_slice_in_dim(out_weight, (1 - x) * half_cols, half_cols, 0)
    wo_pair = jnp.concatenate([wo_keep, line.swap(wo_send)], axis=1)
    quarter_cols = width // 4
    live_part = lax.dynamic_slice_in_dim(live_flat, quarter * quarter_cols, quarter_cols, 1)
    live_here = line.swap(live_part)
    image_cols, wo_pair, live_here, query_weight, *wq_moved = gate(
        (image_cols, wo_pair, live_here, query_weight, *wq_moved)
    )

    n_moved = len(wq_moved)
    planes = [(0, 1, 2), (1, 2, 3)] if relayed else [None] * n_moved
    wq_two = line.second(wq_moved)
    wo_moved = line.first(wo_pair)
    above, wq_other = gate((wq_moved[0], line.swap(query_weight)))
    wq_others = [wq_other, line.swap(above, planes[0])]
    part_kv = jnp.concatenate(
        [matmul(image_cols, key_weight), matmul(image_cols, value_weight)], axis=1
    )
    part_kv = part_kv.reshape(n_dp, image_rows, 2 * local_cols)
    kv_own = jnp.sum(lax.all_to_all(part_kv, "dp", split_axis=0, concat_axis=0), axis=0)
    kv_own, live_here, *staged = gate(
        (kv_own.astype(BF16), live_here, *wq_others, *wq_moved, *wq_two, *wo_moved)
    )
    wq_others, staged = staged[:2], staged[2:]
    wq_moved, wq_two, wo_moved = staged[:n_moved], staged[n_moved:-n_moved], staged[-n_moved:]

    def everywhere(values):
        copies = jnp.broadcast_to(values[None], (n_dp, *values.shape))
        return lax.all_to_all(copies, "dp", split_axis=0, concat_axis=0)

    wq_last = line.third(wq_two)
    wo_two = line.second(wo_moved)
    wq_others += [line.swap(block, at) for block, at in zip(wq_moved[1:], planes[1:])]
    wq_others += [line.swap(block) for block in wq_last[:1]]
    kv_all = everywhere(kv_own).reshape(images, 2 * local_cols)
    early = range(2 if relayed else 1 + n_moved)
    query_part = call(
        functools.partial(query_kernel, line, relayed, early),
        place,
        (text_flat, query_weight, *wq_moved[: len(early) - 1], *wq_others[: len(early)]),
        [shape((rows, local_cols), F32)],
        (),
        rows * width * local_cols,
    )
    kv_all, query_part, live_here, wo_pair, live_flat, *staged = gate(
        (kv_all, query_part, live_here, wo_pair, live_flat, *wo_two, *wq_last, *wq_others)
    )
    wo_two, staged = staged[: len(wo_two)], staged[len(wo_two) :]
    wq_last, wq_others = staged[: len(wq_last)], staged[len(wq_last) :]

    wo_last = line.third(wo_two)
    by_y = tensor_swap(live_here, 2)
    live_pieces = [live_here, tensor_swap(live_here, 1), by_y, tensor_swap(by_y, 1)]
    wq_others += [line.swap(block, (0, 3)) for block in wq_last[1:]]
    half = shape((rows, half_cols), F32)
    wo_early = [wo_pair, *wo_moved]
    grad_parts = call(
        functools.partial(grad_kernel, line, range(len(wo_early)), 0),
        place,
        (live_flat, *live_pieces, *wo_early),
        [half] * 2,
        (),
        rows * width * local_cols,
    )

    arrivals = [query_weight, *wq_moved, *wq_last]
    late = range(len(early), len(arrivals))

    wo_late = range(len(wo_early), len(wo_early) + len(wo_last))
    grad_keep, grad_send = call(
        functools.partial(grad_kernel, line, wo_late, 2),
        place,
        (live_flat, *live_pieces, *grad_parts, *wo_last),
        [shape((rows, half_cols), BF16)] * 2,
        [pltpu.VMEM((rows, half_cols), F32)] * 2,
        rows * width * local_cols,
    )
    text_flat, grad_keep, grad_send = gate((text_flat, grad_keep, grad_send))
    grad_come = line.swap(grad_send)
    queries, attended = call(
        functools.partial(forward_kernel, line, relayed, late, image_own),
        place,
        (text_flat, kv_all, query_part, *arrivals[len(early) :], *wq_others[len(early) :]),
        [shape((rows, local_cols), BF16)] * 2,
        [pltpu.VMEM((rows, local_cols), F32)],
        rows * width * local_cols,
    )
    wq_blocks = [*arrivals, *wq_others]

    att_next = [line.shift(attended, m) for m in (1, line.n_z - 1)]
    attended, grad_come = gate((attended, grad_come))
    att_swapped = line.swap(attended)

    query_grad, kv_part = call(
        functools.partial(backward_kernel, image_own),
        place,
        (queries, kv_all, grad_keep, grad_come),
        [shape((rows, local_cols), BF16), shape((images, 2 * local_cols), F32)],
        (),
        10 * images * rows * local_cols,
    )
    chunk = n_dp // n_tensor
    term = call(
        functools.partial(term_kernel, line, relayed),
        place,
        (query_grad, *wq_blocks),
        [shape((n_tensor, chunk, rows, own_width), BF16)],
        (),
        2 * rows * width * local_cols,
    )
    term, live_flat = gate((term, live_flat))
    quarter_rows = rows // 4
    live_rows = lax.dynamic_slice_in_dim(live_flat, quarter * quarter_rows, quarter_rows, 0)
    live_mine = lax.all_to_all(
        live_rows.reshape(quarter_rows, n_dp, own_width), "dp", split_axis=1, concat_axis=0
    )
    live_mine = live_mine.reshape(n_dp, quarter_rows, own_width)
    kv_part, term, attended, att_swapped, *att_next = gate(
        (kv_part, term, attended, att_swapped, *att_next)
    )

    kv_part = kv_part.reshape(n_dp, image_rows, 2 * local_cols)
    kv_grad = jnp.sum(lax.all_to_all(kv_part, "dp", split_axis=0, concat_axis=0), axis=0)
    kv_grad, live_mine = gate((kv_grad.astype(BF16), live_mine))
    kv_grad_all = everywhere(kv_grad).reshape(images, 2 * local_cols)
    text_parts = [tensor_swap(term[k], k) for k in range(2, n_tensor)]
    att_far = [line.shift(attended, m) for m in range(2, line.n_z - 1)]
    att_other_next = [line.swap(block) for block in att_next]
    live_pair = jnp.stack([live_mine, tensor_swap(live_mine, 2)])
    kv_grad_all, term, live_pair, *staged = gate(
        (kv_grad_all, term, live_pair, *att_other_next, *text_parts, *att_far)
    )
    att_other_next, staged = staged[:2], staged[2:]
    text_parts, att_far = staged[: n_tensor - 2], staged[n_tensor - 2 :]

    att_other_far = [line.swap(block) for block in att_far]
    live_core = tensor_swap(live_pair, 1)
    text_parts.append(tensor_swap(term[1], 1))
    image_term = matmul(kv_grad_all[:, :local_cols], key_weight, BACK)
    image_term = image_term + matmul(kv_grad_all[:, local_cols:], value_weight, BACK)
    text_grad = call(
        sum_kernel, place, (term, *text_parts), [shape((rows, width // n_tensor), BF16)]
    )
    image_grad, live_core, text_grad, *att_other_far = to_owner(
        line, image_term.astype(BF16), live_core, text_grad, *att_other_far
    )
    image_grad = image_grad.reshape(samples, image_own, width // n_tensor)
    text_grad = text_grad.reshape(samples, tok_rows, width // n_tensor)

    att_blocks = [attended, att_next[0], *att_far, att_next[1]]
    att_others = [att_swapped, att_other_next[0], *att_other_far, att_other_next[1]]
    weight_grad = call(
        functools.partial(weight_grad_kernel, line),
        place,
        (live_pair, live_core, *att_blocks, *att_others),
        [shape((local_cols, own_width), BF16)],
        [pltpu.VMEM((local_cols, own_width), F32)],
        2 * n_dp * rows * local_cols * own_width,
    )
    return text_grad, image_grad, weight_grad


def solution(mesh):
    return jax.shard_map(
        shards,
        mesh=mesh,
        in_specs=(
            P(None, "dp", None),
            P(None, "dp", None),
            P(None, "dp", None),
            P(),
            P("dp", "tensor"),
            P("dp", "tensor"),
            P("dp", "tensor"),
            P("tensor", "dp"),
        ),
        out_specs=(P(None, "dp", "tensor"), P(None, "dp", "tensor"), P("tensor", "dp")),
        check_vma=False,
    )
```

```python
import functools

import jax
import jax.numpy as jnp
from jax import lax
from jax.experimental import pallas as pl
from jax.experimental.pallas import tpu as pltpu
from jax.sharding import PartitionSpec as P

HEAD_DIM = 128
F32 = jnp.float32
BF16 = jnp.bfloat16
BACK = (((1,), (1,)), ((), ()))
FIRST = (((0,), (0,)), ((), ()))
VMEM_LIMIT = 60 * 1024 * 1024


def matmul(a, b, dims=None):
    if dims is None:
        return jnp.dot(a, b, preferred_element_type=F32)
    return lax.dot_general(a, b, dims, preferred_element_type=F32)


class Line:
    def __init__(self):
        self.n_dp = lax.axis_size("dp")
        self.n_z = self.n_dp // 2

    def move(self, block, moves):
        pairs = [(2 * a + e, 2 * b + e) for a, b in moves for e in range(2)]
        return lax.ppermute(block, "dp", pairs)

    def swap(self, block, planes=None):
        planes = range(self.n_z) if planes is None else planes
        pairs = [(2 * a + e, 2 * a + 1 - e) for a in planes for e in range(2)]
        return lax.ppermute(block, "dp", pairs)

    def shift(self, block, distance):
        n = self.n_z
        return self.move(block, [((a + distance) % n, a) for a in range(n)])

    def first(self, block):
        if self.n_z != 4:
            return [self.shift(block, m) for m in range(1, self.n_z)]
        above = self.move(block, [(1, 0), (2, 1), (3, 2)])
        below = self.move(block, [(0, 1), (1, 2), (2, 3)])
        return [above, below]

    def second(self, moved):
        if self.n_z != 4:
            return []
        return [self.move(moved[0], [(1, 0), (2, 1)]), self.move(moved[1], [(1, 2), (2, 3)])]

    def third(self, forwarded):
        if self.n_z != 4:
            return []
        across = jnp.where(lax.axis_index("dp") < 4, forwarded[0], forwarded[1])
        return [across, self.move(across, [(1, 0), (2, 3)])]

    def slots(self, z, relayed):
        if not relayed:
            return [(m, None) for m in range(self.n_z)]
        return [
            (0, None),
            (1, z < 3),
            (3, z > 0),
            (2, None),
            (jnp.where(z == 3, 1, 3), (z == 3) | (z == 0)),
        ]


def each_block(line, place, relayed, which, body):
    z, x = place[0], place[1]
    slots = line.slots(z, relayed)
    for j, at in enumerate(which):
        m, came = slots[at]
        plane = lax.rem(z + m, line.n_z)
        for e in range(2):
            index = 2 * plane + (x if e == 0 else 1 - x)
            if came is None:
                body(j, e, index)
            else:
                pl.when(came)(functools.partial(body, j, e, index))


def columns(index, size):
    return pl.ds(pl.multiple_of(index * size, size), size)


def probabilities(query, key, image_own):
    scores = matmul(key, query, BACK) * HEAD_DIM ** (-0.5)
    image = lax.broadcasted_iota(jnp.int32, scores.shape, 0)
    token = lax.broadcasted_iota(jnp.int32, scores.shape, 1)
    image_sample = lax.rem(lax.div(image, image_own), 2)
    same = image_sample == lax.div(token, scores.shape[1] // 2)
    scores = jnp.where(same, scores, -1e30)
    peak = jnp.max(scores, axis=0, keepdims=True)
    expo = jnp.where(same, jnp.exp(scores - peak), 0.0)
    return expo / jnp.sum(expo, axis=0, keepdims=True)


def query_kernel(line, relayed, which, place, text, *refs):
    n = len(which)
    weights, total = (refs[:n], refs[n : 2 * n]), refs[-1]
    own_width = weights[0][0].shape[0]
    total[...] = jnp.zeros_like(total)

    def add(j, e, index):
        total[...] += matmul(text[:, columns(index, own_width)], weights[e][j][...])

    each_block(line, place, relayed, which, add)


def forward_kernel(line, relayed, which, image_own, place, text, kv, part, *refs):
    n = len(which)
    weights, (query_out, attended_out, total) = (refs[:n], refs[n : 2 * n]), refs[2 * n :]
    rows, cols = total.shape
    total[...] = part[...]

    def add(j, e, index):
        weight = weights[e][j]
        total[...] += matmul(text[:, columns(index, weight.shape[0])], weight[...])

    each_block(line, place, relayed, which, add)
    query_out[...] = total[...].astype(BF16)
    part_rows = rows // 4
    quarter = place[2]
    for h in range(cols // HEAD_DIM):
        at = slice(h * HEAD_DIM, (h + 1) * HEAD_DIM)
        value = kv[:, cols + h * HEAD_DIM : cols + (h + 1) * HEAD_DIM]
        prob = probabilities(query_out[:, at], kv[:, at], image_own)
        attended = matmul(prob.astype(BF16), value, FIRST).astype(BF16)
        for r in range(4):
            low_bit = (quarter + r) % 2
            high_bit = (quarter // 2 + r // 2) % 2
            start = pl.multiple_of((2 * low_bit + high_bit) * part_rows, part_rows)
            attended_out[pl.ds(start, part_rows), at] = attended[
                r * part_rows : (r + 1) * part_rows
            ]


def grad_kernel(line, which, parts, place, live, mine, by_core, by_y, by_both, *refs):
    before, refs = refs[:parts], refs[parts:]
    weights, outs = refs[: len(which)], refs[len(which) :]
    cut = line.n_dp // 4
    keep, send = outs[-2:]
    keep[...] = before[0][...] if parts else jnp.zeros_like(keep)
    send[...] = before[1][...] if parts else jnp.zeros_like(send)

    def add(j, e, index):
        own_width = weights[j].shape[1] // 2
        weight = weights[j][:, e * own_width : (e + 1) * own_width]
        keep[...] += matmul(live[:, columns(index, own_width)], weight, BACK)
        inner = columns(lax.rem(index, cut), own_width)
        member = lax.bitwise_xor(lax.div(index, cut), place[2])
        other = mine[:, inner]
        for at, piece in ((1, by_core), (2, by_y), (3, by_both)):
            other = jnp.where(member == at, piece[:, inner], other)
        send[...] += matmul(other, weight, BACK)

    each_block(line, place, line.n_z == 4, which, add)
    if parts:
        outs[0][...] = keep[...].astype(BF16)
        outs[1][...] = send[...].astype(BF16)


def backward_kernel(image_own, place, query, kv, keep, come, query_grad, kv_grad):
    cols = query.shape[1]
    half = cols // 2
    x = place[1]
    for h in range(cols // HEAD_DIM):
        at = slice(h * HEAD_DIM, (h + 1) * HEAD_DIM)
        value_at = slice(cols + h * HEAD_DIM, cols + (h + 1) * HEAD_DIM)
        side = h * HEAD_DIM // half
        inner = slice(h * HEAD_DIM - side * half, (h + 1) * HEAD_DIM - side * half)
        grad = jnp.where(x == side, keep[:, inner], come[:, inner])
        prob = probabilities(query[:, at], kv[:, at], image_own)
        kv_grad[:, value_at] = matmul(prob.astype(BF16), grad)
        prob_grad = matmul(kv[:, value_at], grad, BACK)
        delta = jnp.sum(prob * prob_grad, axis=0, keepdims=True)
        score_grad = (prob * (prob_grad - delta) * HEAD_DIM ** (-0.5)).astype(BF16)
        kv_grad[:, at] = matmul(score_grad, query[:, at])
        query_grad[:, at] = matmul(score_grad, kv[:, at], FIRST).astype(BF16)


def term_kernel(line, relayed, place, query_grad, *refs):
    out = refs[-1]
    n = (len(refs) - 1) // 2
    weights = (refs[:n], refs[n : 2 * n])
    chunk = out.shape[1]

    def write(i, e, index):
        term = matmul(query_grad[...], weights[e][i][...], BACK)
        out[lax.div(index, chunk), lax.rem(index, chunk)] = term.astype(BF16)

    each_block(line, place, relayed, range(n), write)


def weight_grad_kernel(line, which, parts, place, own_pair, core_pair, *refs):
    before, refs = refs[:parts], refs[parts:]
    n = len(which)
    attended, outs = (refs[:n], refs[n : 2 * n]), refs[2 * n :]
    total = outs[-1]
    total[...] = before[0][...] if parts else jnp.zeros_like(total)

    def add(j, e, index):
        block = [pair[i, index] for pair in (own_pair, core_pair) for i in range(2)]
        term = matmul(attended[e][j][...], jnp.concatenate(block, axis=0), FIRST)
        total[...] += term.astype(BF16).astype(F32)

    each_block(line, place, False, which, add)
    if parts:
        outs[0][...] = total[...].astype(BF16)


def sum_kernel(place, parts, out):
    width = parts.shape[3]
    for c in range(parts.shape[1]):
        total = parts[0, c].astype(F32)
        for k in range(1, parts.shape[0]):
            total = total + parts[k, c].astype(F32)
        out[:, c * width : (c + 1) * width] = total.astype(BF16)


def call(kernel, place, operands, outs, scratch=(), flops=0):
    moved = sum(a.size * a.dtype.itemsize for a in (*operands, *outs))
    single = len(outs) == 1
    return pl.pallas_call(
        kernel,
        out_shape=outs[0] if single else outs,
        in_specs=[pl.BlockSpec(memory_space=pltpu.SMEM)]
        + [pl.BlockSpec(memory_space=pltpu.VMEM)] * len(operands),
        out_specs=pl.BlockSpec(memory_space=pltpu.VMEM)
        if single
        else [pl.BlockSpec(memory_space=pltpu.VMEM)] * len(outs),
        scratch_shapes=list(scratch),
        compiler_params=pltpu.CompilerParams(vmem_limit_bytes=VMEM_LIMIT),
        cost_estimate=pl.CostEstimate(flops=flops, bytes_accessed=moved, transcendentals=0),
    )(place, *operands)


def to_owner(line, terms, *others):
    n_dp, n_tensor = line.n_dp, lax.axis_size("tensor")
    images, cols = terms.shape
    if line.n_z != n_tensor:
        terms = lax.all_to_all(terms, "dp", split_axis=0, concat_axis=1, tiled=True)
        terms = terms.reshape(images // n_dp, n_tensor, n_dp * cols // n_tensor)
        parts = lax.all_to_all(terms, "tensor", split_axis=1, concat_axis=0)
        return (jnp.sum(parts.astype(F32), axis=0).astype(BF16), *others)
    parts = lax.all_to_all(
        terms.reshape(n_tensor, images // n_tensor, cols), "tensor", split_axis=0, concat_axis=0
    )
    total = jnp.sum(parts.astype(F32), axis=0).astype(BF16)
    total, *others = lax.optimization_barrier((total, *others))
    total = total.reshape(2, images // n_dp, cols)
    x = lax.axis_index("dp") % 2
    come = []
    for other in range(2):
        block = jnp.where(x == other, total[0], total[1])
        pairs = [
            ((2 * z + e) * n_tensor + t, (2 * t + (e ^ other)) * n_tensor + z)
            for z in range(line.n_z)
            for e in range(2)
            for t in range(n_tensor)
        ]
        come.append(lax.ppermute(block, ("dp", "tensor"), pairs))
    rows = jnp.where(
        x == 0, jnp.concatenate(come, axis=1), jnp.concatenate(come[::-1], axis=1)
    )
    return (rows, *others)


def shards(
    text_states,
    image_states,
    out_grad,
    text_lengths,
    query_weight,
    key_weight,
    value_weight,
    out_weight,
):
    samples, tok_rows, width = text_states.shape
    image_own = image_states.shape[1]
    line = Line()
    n_dp = line.n_dp
    n_tensor = lax.axis_size("tensor")
    dp_at, tensor_at = lax.axis_index("dp"), lax.axis_index("tensor")
    x, quarter = dp_at % 2, tensor_at % 4
    place = jnp.stack([dp_at // 2, x, quarter]).astype(jnp.int32)
    rows = samples * tok_rows
    image_rows = samples * image_own
    images = n_dp * image_rows
    local_cols = query_weight.shape[1]
    own_width = query_weight.shape[0]
    half_cols = local_cols // 2
    shape = jax.ShapeDtypeStruct

    def tensor_swap(block, bit):
        return lax.ppermute(block, "tensor", [(t, t ^ bit) for t in range(n_tensor)])

    positions = dp_at * tok_rows + lax.iota(jnp.int32, tok_rows)
    live_rows = positions[None, :] < text_lengths[:, None]
    grad_live = jnp.where(live_rows[..., None], out_grad, jnp.zeros_like(out_grad))
    text_flat = text_states.reshape(rows, width)
    live_flat = grad_live.reshape(rows, width)
    image_flat = image_states.reshape(image_rows, width)

    gate = lax.optimization_barrier

    relayed = line.n_z == 4
    wq_moved = line.first(query_weight)
    image_cols = lax.all_to_all(image_flat, "dp", split_axis=1, concat_axis=0, tiled=True)
    wo_keep = lax.dynamic_slice_in_dim(out_weight, x * half_cols, half_cols, 0)
    wo_send = lax.dynamic_slice_in_dim(out_weight, (1 - x) * half_cols, half_cols, 0)
    wo_pair = jnp.concatenate([wo_keep, line.swap(wo_send)], axis=1)
    quarter_cols = width // 4
    live_part = lax.dynamic_slice_in_dim(live_flat, quarter * quarter_cols, quarter_cols, 1)
    live_here = line.swap(live_part)
    image_cols, wo_pair, live_here, query_weight, *wq_moved = gate(
        (image_cols, wo_pair, live_here, query_weight, *wq_moved)
    )

    n_moved = len(wq_moved)
    planes = [(0, 1, 2), (1, 2, 3)] if relayed else [None] * n_moved
    wq_two = line.second(wq_moved)
    wo_moved = line.first(wo_pair)
    above, wq_other = gate((wq_moved[0], line.swap(query_weight)))
    wq_others = [wq_other, line.swap(above, planes[0])]
    part_kv = jnp.concatenate(
        [matmul(image_cols, key_weight), matmul(image_cols, value_weight)], axis=1
    )
    part_kv = part_kv.reshape(n_dp, image_rows, 2 * local_cols)
    kv_own = jnp.sum(lax.all_to_all(part_kv, "dp", split_axis=0, concat_axis=0), axis=0)
    kv_own, live_here, *staged = gate(
        (kv_own.astype(BF16), live_here, *wq_others, *wq_moved, *wq_two, *wo_moved)
    )
    wq_others, staged = staged[:2], staged[2:]
    wq_moved, wq_two, wo_moved = staged[:n_moved], staged[n_moved:-n_moved], staged[-n_moved:]

    def everywhere(values):
        copies = jnp.broadcast_to(values[None], (n_dp, *values.shape))
        return lax.all_to_all(copies, "dp", split_axis=0, concat_axis=0)

    wq_last = line.third(wq_two)
    wo_two = line.second(wo_moved)
    wq_others += [line.swap(block, at) for block, at in zip(wq_moved[1:], planes[1:])]
    wq_others += [line.swap(block) for block in wq_last[:1]]
    kv_all = everywhere(kv_own).reshape(images, 2 * local_cols)
    early = range(2 if relayed else 1 + n_moved)
    query_part = call(
        functools.partial(query_kernel, line, relayed, early),
        place,
        (text_flat, query_weight, *wq_moved[: len(early) - 1], *wq_others[: len(early)]),
        [shape((rows, local_cols), F32)],
        (),
        rows * width * local_cols,
    )
    kv_all, query_part, live_here, wo_pair, live_flat, *staged = gate(
        (kv_all, query_part, live_here, wo_pair, live_flat, *wo_two, *wq_last, *wq_others)
    )
    wo_two, staged = staged[: len(wo_two)], staged[len(wo_two) :]
    wq_last, wq_others = staged[: len(wq_last)], staged[len(wq_last) :]

    wo_last = line.third(wo_two)
    by_y = tensor_swap(live_here, 2)
    live_late, by_y = gate((live_flat, by_y))
    quarter_rows = rows // 4
    live_rows = lax.dynamic_slice_in_dim(live_late, quarter * quarter_rows, quarter_rows, 0)
    live_mine = lax.all_to_all(
        live_rows.reshape(quarter_rows, n_dp, own_width), "dp", split_axis=1, concat_axis=0
    )
    live_mine = live_mine.reshape(n_dp, quarter_rows, own_width)
    live_pieces = [live_here, tensor_swap(live_here, 1), by_y, tensor_swap(by_y, 1)]
    wq_others += [line.swap(block, (0, 3)) for block in wq_last[1:]]
    half = shape((rows, half_cols), F32)
    wo_early = [wo_pair, *wo_moved]
    grad_parts = call(
        functools.partial(grad_kernel, line, range(len(wo_early)), 0),
        place,
        (live_flat, *live_pieces, *wo_early),
        [half] * 2,
        (),
        rows * width * local_cols,
    )

    arrivals = [query_weight, *wq_moved, *wq_last]
    late = range(len(early), len(arrivals))

    wo_late = range(len(wo_early), len(wo_early) + len(wo_last))
    grad_keep, grad_send = call(
        functools.partial(grad_kernel, line, wo_late, 2),
        place,
        (live_flat, *live_pieces, *grad_parts, *wo_last),
        [shape((rows, half_cols), BF16)] * 2,
        [pltpu.VMEM((rows, half_cols), F32)] * 2,
        rows * width * local_cols,
    )
    text_flat, live_mine, grad_keep, grad_send = gate(
        (text_flat, live_mine, grad_keep, grad_send)
    )
    grad_come = line.swap(grad_send)
    queries, attended = call(
        functools.partial(forward_kernel, line, relayed, late, image_own),
        place,
        (text_flat, kv_all, query_part, *arrivals[len(early) :], *wq_others[len(early) :]),
        [shape((rows, local_cols), BF16)] * 2,
        [pltpu.VMEM((rows, local_cols), F32)],
        rows * width * local_cols,
    )
    wq_blocks = [*arrivals, *wq_others]

    att_next = [line.shift(attended, m) for m in (1, line.n_z - 1)]
    attended, grad_come = gate((attended, grad_come))
    att_swapped = line.swap(attended)

    query_grad, kv_part = call(
        functools.partial(backward_kernel, image_own),
        place,
        (queries, kv_all, grad_keep, grad_come),
        [shape((rows, local_cols), BF16), shape((images, 2 * local_cols), F32)],
        (),
        10 * images * rows * local_cols,
    )
    chunk = n_dp // n_tensor
    term = call(
        functools.partial(term_kernel, line, relayed),
        place,
        (query_grad, *wq_blocks),
        [shape((n_tensor, chunk, rows, own_width), BF16)],
        (),
        2 * rows * width * local_cols,
    )
    live_pair = jnp.stack([live_mine, tensor_swap(live_mine, 2)])
    kv_part, term, live_pair, attended, att_swapped, *att_next = gate(
        (kv_part, term, live_pair, attended, att_swapped, *att_next)
    )

    kv_part = kv_part.reshape(n_dp, image_rows, 2 * local_cols)
    kv_grad = jnp.sum(lax.all_to_all(kv_part, "dp", split_axis=0, concat_axis=0), axis=0)
    kv_grad_all = everywhere(kv_grad.astype(BF16)).reshape(images, 2 * local_cols)
    text_parts = lax.all_to_all(term, "tensor", split_axis=0, concat_axis=0).reshape(term.shape)
    live_core = tensor_swap(live_pair, 1)
    att_far = [line.shift(attended, m) for m in range(2, line.n_z - 1)]
    att_other_next = [line.swap(block) for block in att_next]
    text_parts, *att_far = gate((text_parts, *att_far))
    text_grad = call(
        sum_kernel, place, (text_parts,), [shape((rows, width // n_tensor), BF16)]
    )
    next_at, far_at = (0, 1, line.n_z - 1), range(2, line.n_z - 1)
    weight_part = call(
        functools.partial(weight_grad_kernel, line, next_at, 0),
        place,
        (live_pair, live_core, attended, *att_next, att_swapped, *att_other_next),
        [shape((local_cols, own_width), F32)],
        (),
        6 * 2 * rows * local_cols * own_width,
    )
    kv_grad_all, text_grad = gate((kv_grad_all, text_grad))

    att_other_far = [line.swap(block) for block in att_far]
    image_term = matmul(kv_grad_all[:, :local_cols], key_weight, BACK)
    image_term = image_term + matmul(kv_grad_all[:, local_cols:], value_weight, BACK)
    image_grad, weight_part, *att_other_far = to_owner(
        line, image_term.astype(BF16), weight_part, *att_other_far
    )
    image_grad = image_grad.reshape(samples, image_own, width // n_tensor)
    text_grad = text_grad.reshape(samples, tok_rows, width // n_tensor)

    weight_grad = call(
        functools.partial(weight_grad_kernel, line, far_at, 1),
        place,
        (live_pair, live_core, weight_part, *att_far, *att_other_far),
        [shape((local_cols, own_width), BF16)],
        [pltpu.VMEM((local_cols, own_width), F32)],
        2 * 2 * rows * local_cols * own_width,
    )
    return text_grad, image_grad, weight_grad


def solution(mesh):
    return jax.shard_map(
        shards,
        mesh=mesh,
        in_specs=(
            P(None, "dp", None),
            P(None, "dp", None),
            P(None, "dp", None),
            P(),
            P("dp", "tensor"),
            P("dp", "tensor"),
            P("dp", "tensor"),
            P("tensor", "dp"),
        ),
        out_specs=(P(None, "dp", "tensor"), P(None, "dp", "tensor"), P("tensor", "dp")),
        check_vma=False,
    )
```

```python
import functools

import jax
import jax.numpy as jnp
from jax import lax
from jax.experimental import pallas as pl
from jax.experimental.pallas import tpu as pltpu
from jax.sharding import PartitionSpec as P

HEAD_DIM = 128
F32 = jnp.float32
BF16 = jnp.bfloat16
BACK = (((1,), (1,)), ((), ()))
FIRST = (((0,), (0,)), ((), ()))
VMEM_LIMIT = 24 * 1024 * 1024


def matmul(a, b, dims=None):
    if dims is None:
        return jnp.dot(a, b, preferred_element_type=F32)
    return lax.dot_general(a, b, dims, preferred_element_type=F32)


class Line:
    def __init__(self):
        self.n_dp = lax.axis_size("dp")
        self.n_z = self.n_dp // 2

    def move(self, block, moves):
        pairs = [(2 * a + e, 2 * b + e) for a, b in moves for e in range(2)]
        return lax.ppermute(block, "dp", pairs)

    def swap(self, block, planes=None):
        planes = range(self.n_z) if planes is None else planes
        pairs = [(2 * a + e, 2 * a + 1 - e) for a in planes for e in range(2)]
        return lax.ppermute(block, "dp", pairs)

    def shift(self, block, distance):
        n = self.n_z
        return self.move(block, [((a + distance) % n, a) for a in range(n)])

    def first(self, block):
        if self.n_z != 4:
            return [self.shift(block, m) for m in range(1, self.n_z)]
        above = self.move(block, [(1, 0), (2, 1), (3, 2)])
        below = self.move(block, [(0, 1), (1, 2), (2, 3)])
        return [above, below]

    def second(self, moved):
        if self.n_z != 4:
            return []
        return [self.move(moved[0], [(1, 0), (2, 1)]), self.move(moved[1], [(1, 2), (2, 3)])]

    def third(self, forwarded):
        if self.n_z != 4:
            return []
        across = jnp.where(lax.axis_index("dp") < 4, forwarded[0], forwarded[1])
        return [across, self.move(across, [(1, 0), (2, 3)])]

    def slots(self, z, relayed):
        if not relayed:
            return [(m, None) for m in range(self.n_z)]
        return [
            (0, None),
            (1, z < 3),
            (3, z > 0),
            (2, None),
            (jnp.where(z == 3, 1, 3), (z == 3) | (z == 0)),
        ]


def each_block(line, place, relayed, which, body):
    z, x = place[0], place[1]
    slots = line.slots(z, relayed)
    for j, at in enumerate(which):
        m, came = slots[at]
        plane = lax.rem(z + m, line.n_z)
        for e in range(2):
            index = 2 * plane + (x if e == 0 else 1 - x)
            if came is None:
                body(j, e, index)
            else:
                pl.when(came)(functools.partial(body, j, e, index))


def columns(index, size):
    return pl.ds(pl.multiple_of(index * size, size), size)


def probabilities(query, key, image_own):
    scores = matmul(key, query, BACK) * HEAD_DIM ** (-0.5)
    image = lax.broadcasted_iota(jnp.int32, scores.shape, 0)
    token = lax.broadcasted_iota(jnp.int32, scores.shape, 1)
    image_sample = lax.rem(lax.div(image, image_own), 2)
    same = image_sample == lax.div(token, scores.shape[1] // 2)
    scores = jnp.where(same, scores, -1e30)
    peak = jnp.max(scores, axis=0, keepdims=True)
    expo = jnp.where(same, jnp.exp(scores - peak), 0.0)
    return expo / jnp.sum(expo, axis=0, keepdims=True)


def query_kernel(line, relayed, which, place, text, *refs):
    n = len(which)
    weights, total = (refs[:n], refs[n : 2 * n]), refs[-1]
    own_width = weights[0][0].shape[0]
    total[...] = jnp.zeros_like(total)

    def add(j, e, index):
        total[...] += matmul(text[:, columns(index, own_width)], weights[e][j][...])

    each_block(line, place, relayed, which, add)


def forward_kernel(line, relayed, which, image_own, place, text, kv, part, *refs):
    n = len(which)
    weights, (query_out, attended_out, total) = (refs[:n], refs[n : 2 * n]), refs[2 * n :]
    rows, cols = total.shape
    total[...] = part[...]

    def add(j, e, index):
        weight = weights[e][j]
        total[...] += matmul(text[:, columns(index, weight.shape[0])], weight[...])

    each_block(line, place, relayed, which, add)
    query_out[...] = total[...].astype(BF16)
    part_rows = rows // 4
    quarter = place[2]
    for h in range(cols // HEAD_DIM):
        at = slice(h * HEAD_DIM, (h + 1) * HEAD_DIM)
        value = kv[:, cols + h * HEAD_DIM : cols + (h + 1) * HEAD_DIM]
        prob = probabilities(query_out[:, at], kv[:, at], image_own)
        attended = matmul(prob.astype(BF16), value, FIRST).astype(BF16)
        for r in range(4):
            low_bit = (quarter + r) % 2
            high_bit = (quarter // 2 + r // 2) % 2
            start = pl.multiple_of((2 * low_bit + high_bit) * part_rows, part_rows)
            attended_out[pl.ds(start, part_rows), at] = attended[
                r * part_rows : (r + 1) * part_rows
            ]


def grad_kernel(line, which, parts, place, live, mine, by_core, by_y, by_both, *refs):
    before, refs = refs[:parts], refs[parts:]
    weights, outs = refs[: len(which)], refs[len(which) :]
    cut = line.n_dp // 4
    keep, send = outs[-2:]
    keep[...] = before[0][...] if parts else jnp.zeros_like(keep)
    send[...] = before[1][...] if parts else jnp.zeros_like(send)

    def add(j, e, index):
        own_width = weights[j].shape[1] // 2
        weight = weights[j][:, e * own_width : (e + 1) * own_width]
        keep[...] += matmul(live[:, columns(index, own_width)], weight, BACK)
        inner = columns(lax.rem(index, cut), own_width)
        member = lax.bitwise_xor(lax.div(index, cut), place[2])
        other = mine[:, inner]
        for at, piece in ((1, by_core), (2, by_y), (3, by_both)):
            other = jnp.where(member == at, piece[:, inner], other)
        send[...] += matmul(other, weight, BACK)

    each_block(line, place, line.n_z == 4, which, add)
    if parts:
        outs[0][...] = keep[...].astype(BF16)
        outs[1][...] = send[...].astype(BF16)


def backward_kernel(image_own, place, query, kv, keep, come, query_grad, kv_grad):
    cols = query.shape[1]
    half = cols // 2
    x = place[1]
    for h in range(cols // HEAD_DIM):
        at = slice(h * HEAD_DIM, (h + 1) * HEAD_DIM)
        value_at = slice(cols + h * HEAD_DIM, cols + (h + 1) * HEAD_DIM)
        side = h * HEAD_DIM // half
        inner = slice(h * HEAD_DIM - side * half, (h + 1) * HEAD_DIM - side * half)
        grad = jnp.where(x == side, keep[:, inner], come[:, inner])
        prob = probabilities(query[:, at], kv[:, at], image_own)
        kv_grad[:, value_at] = matmul(prob.astype(BF16), grad)
        prob_grad = matmul(kv[:, value_at], grad, BACK)
        delta = jnp.sum(prob * prob_grad, axis=0, keepdims=True)
        score_grad = (prob * (prob_grad - delta) * HEAD_DIM ** (-0.5)).astype(BF16)
        kv_grad[:, at] = matmul(score_grad, query[:, at])
        query_grad[:, at] = matmul(score_grad, kv[:, at], FIRST).astype(BF16)


def term_kernel(line, relayed, place, query_grad, *refs):
    out = refs[-1]
    n = (len(refs) - 1) // 2
    weights = (refs[:n], refs[n : 2 * n])
    chunk = out.shape[1]

    def write(i, e, index):
        term = matmul(query_grad[...], weights[e][i][...], BACK)
        member = lax.bitwise_xor(lax.div(index, chunk), place[3])
        out[member, lax.rem(index, chunk)] = term.astype(BF16)

    each_block(line, place, relayed, range(n), write)


def weight_grad_kernel(line, place, *refs):
    live, refs = refs[:2], refs[2:]
    n = (len(refs) - 2) // 2
    attended, (out, total) = (refs[:n], refs[n : 2 * n]), refs[2 * n :]
    total[...] = jnp.zeros_like(total)

    def add(i, e, index):
        block = jnp.concatenate([part[i, index] for part in live for i in range(2)], axis=0)
        term = matmul(attended[e][i][...], block, FIRST)
        total[...] += term.astype(BF16).astype(F32)

    each_block(line, place, False, range(n), add)
    out[...] = total[...].astype(BF16)


def sum_kernel(place, term, *refs):
    parts, out = refs[:-1], refs[-1]
    width = term.shape[3]
    for c in range(term.shape[1]):
        total = term[0, c].astype(F32)
        for part in parts:
            total = total + part[c].astype(F32)
        out[:, c * width : (c + 1) * width] = total.astype(BF16)


def call(kernel, place, operands, outs, scratch=(), flops=0):
    moved = sum(a.size * a.dtype.itemsize for a in (*operands, *outs))
    single = len(outs) == 1
    return pl.pallas_call(
        kernel,
        out_shape=outs[0] if single else outs,
        in_specs=[pl.BlockSpec(memory_space=pltpu.SMEM)]
        + [pl.BlockSpec(memory_space=pltpu.VMEM)] * len(operands),
        out_specs=pl.BlockSpec(memory_space=pltpu.VMEM)
        if single
        else [pl.BlockSpec(memory_space=pltpu.VMEM)] * len(outs),
        scratch_shapes=list(scratch),
        compiler_params=pltpu.CompilerParams(vmem_limit_bytes=VMEM_LIMIT),
        cost_estimate=pl.CostEstimate(flops=flops, bytes_accessed=moved, transcendentals=0),
    )(place, *operands)


def to_owner(line, terms, *others):
    n_dp, n_tensor = line.n_dp, lax.axis_size("tensor")
    images, cols = terms.shape
    if line.n_z != n_tensor:
        terms = lax.all_to_all(terms, "dp", split_axis=0, concat_axis=1, tiled=True)
        terms = terms.reshape(images // n_dp, n_tensor, n_dp * cols // n_tensor)
        parts = lax.all_to_all(terms, "tensor", split_axis=1, concat_axis=0)
        return (jnp.sum(parts.astype(F32), axis=0).astype(BF16), *others)
    parts = lax.all_to_all(
        terms.reshape(n_tensor, images // n_tensor, cols), "tensor", split_axis=0, concat_axis=0
    )
    total = jnp.sum(parts.astype(F32), axis=0).astype(BF16)
    total, *others = lax.optimization_barrier((total, *others))
    total = total.reshape(2, images // n_dp, cols)
    x = lax.axis_index("dp") % 2
    come = []
    for other in range(2):
        block = jnp.where(x == other, total[0], total[1])
        pairs = [
            ((2 * z + e) * n_tensor + t, (2 * t + (e ^ other)) * n_tensor + z)
            for z in range(line.n_z)
            for e in range(2)
            for t in range(n_tensor)
        ]
        come.append(lax.ppermute(block, ("dp", "tensor"), pairs))
    rows = jnp.where(
        x == 0, jnp.concatenate(come, axis=1), jnp.concatenate(come[::-1], axis=1)
    )
    return (rows, *others)


def shards(
    text_states,
    image_states,
    out_grad,
    text_lengths,
    query_weight,
    key_weight,
    value_weight,
    out_weight,
):
    samples, tok_rows, width = text_states.shape
    image_own = image_states.shape[1]
    line = Line()
    n_dp = line.n_dp
    n_tensor = lax.axis_size("tensor")
    dp_at, tensor_at = lax.axis_index("dp"), lax.axis_index("tensor")
    x, quarter = dp_at % 2, tensor_at % 4
    place = jnp.stack([dp_at // 2, x, quarter, tensor_at]).astype(jnp.int32)
    rows = samples * tok_rows
    image_rows = samples * image_own
    images = n_dp * image_rows
    local_cols = query_weight.shape[1]
    own_width = query_weight.shape[0]
    half_cols = local_cols // 2
    shape = jax.ShapeDtypeStruct

    def tensor_swap(block, bit):
        return lax.ppermute(block, "tensor", [(t, t ^ bit) for t in range(n_tensor)])

    positions = dp_at * tok_rows + lax.iota(jnp.int32, tok_rows)
    live_rows = positions[None, :] < text_lengths[:, None]
    grad_live = jnp.where(live_rows[..., None], out_grad, jnp.zeros_like(out_grad))
    text_flat = text_states.reshape(rows, width)
    live_flat = grad_live.reshape(rows, width)
    image_flat = image_states.reshape(image_rows, width)

    gate = lax.optimization_barrier

    relayed = line.n_z == 4
    wq_moved = line.first(query_weight)
    image_cols = lax.all_to_all(image_flat, "dp", split_axis=1, concat_axis=0, tiled=True)
    wo_keep = lax.dynamic_slice_in_dim(out_weight, x * half_cols, half_cols, 0)
    wo_send = lax.dynamic_slice_in_dim(out_weight, (1 - x) * half_cols, half_cols, 0)
    wo_pair = jnp.concatenate([wo_keep, line.swap(wo_send)], axis=1)
    quarter_cols = width // 4
    live_part = lax.dynamic_slice_in_dim(live_flat, quarter * quarter_cols, quarter_cols, 1)
    live_here = line.swap(live_part)
    image_cols, wo_pair, live_here, query_weight, *wq_moved = gate(
        (image_cols, wo_pair, live_here, query_weight, *wq_moved)
    )

    n_moved = len(wq_moved)
    planes = [(0, 1, 2), (1, 2, 3)] if relayed else [None] * n_moved
    wq_two = line.second(wq_moved)
    wo_moved = line.first(wo_pair)
    above, wq_other = gate((wq_moved[0], line.swap(query_weight)))
    wq_others = [wq_other, line.swap(above, planes[0])]
    part_kv = jnp.concatenate(
        [matmul(image_cols, key_weight), matmul(image_cols, value_weight)], axis=1
    )
    part_kv = part_kv.reshape(n_dp, image_rows, 2 * local_cols)
    kv_own = jnp.sum(lax.all_to_all(part_kv, "dp", split_axis=0, concat_axis=0), axis=0)
    kv_own, live_here, *staged = gate(
        (kv_own.astype(BF16), live_here, *wq_others, *wq_moved, *wq_two, *wo_moved)
    )
    wq_others, staged = staged[:2], staged[2:]
    wq_moved, wq_two, wo_moved = staged[:n_moved], staged[n_moved:-n_moved], staged[-n_moved:]

    def everywhere(values):
        copies = jnp.broadcast_to(values[None], (n_dp, *values.shape))
        return lax.all_to_all(copies, "dp", split_axis=0, concat_axis=0)

    wq_last = line.third(wq_two)
    wo_two = line.second(wo_moved)
    wq_others += [line.swap(block, at) for block, at in zip(wq_moved[1:], planes[1:])]
    wq_others += [line.swap(block) for block in wq_last[:1]]
    kv_all = everywhere(kv_own).reshape(images, 2 * local_cols)
    kv_all, live_here, wo_pair, live_flat, *staged = gate(
        (kv_all, live_here, wo_pair, live_flat, *wo_two, *wq_last, *wq_others)
    )
    wo_two, staged = staged[: len(wo_two)], staged[len(wo_two) :]
    wq_last, wq_others = staged[: len(wq_last)], staged[len(wq_last) :]

    wo_last = line.third(wo_two)
    quarter_rows = rows // 4
    live_rows = lax.dynamic_slice_in_dim(live_flat, quarter * quarter_rows, quarter_rows, 0)
    live_mine = lax.all_to_all(
        live_rows.reshape(quarter_rows, n_dp, own_width), "dp", split_axis=1, concat_axis=0
    )
    live_mine = live_mine.reshape(n_dp, quarter_rows, own_width)
    by_y = tensor_swap(live_here, 2)
    live_pieces = [live_here, tensor_swap(live_here, 1), by_y, tensor_swap(by_y, 1)]
    wq_others += [line.swap(block, (0, 3)) for block in wq_last[1:]]
    arrivals = [query_weight, *wq_moved, *wq_last]
    early = range(4 if relayed else len(arrivals))
    late = range(len(early), len(arrivals))
    query_part = call(
        functools.partial(query_kernel, line, relayed, early),
        place,
        (text_flat, *arrivals[: len(early)], *wq_others[: len(early)]),
        [shape((rows, local_cols), F32)],
        (),
        2 * rows * width * local_cols,
    )

    half = shape((rows, half_cols), F32)
    wo_early = [wo_pair, *wo_moved]
    grad_parts = call(
        functools.partial(grad_kernel, line, range(len(wo_early)), 0),
        place,
        (live_flat, *live_pieces, *wo_early),
        [half] * 2,
        (),
        rows * width * local_cols,
    )

    query_part, *grad_parts = gate((query_part, *grad_parts))

    wo_late = range(len(wo_early), len(wo_early) + len(wo_last))
    grad_keep, grad_send = call(
        functools.partial(grad_kernel, line, wo_late, 2),
        place,
        (live_flat, *live_pieces, *grad_parts, *wo_last),
        [shape((rows, half_cols), BF16)] * 2,
        [pltpu.VMEM((rows, half_cols), F32)] * 2,
        rows * width * local_cols,
    )
    text_flat, live_mine, grad_keep, grad_send = gate(
        (text_flat, live_mine, grad_keep, grad_send)
    )
    grad_come = line.swap(grad_send)
    queries, attended = call(
        functools.partial(forward_kernel, line, relayed, late, image_own),
        place,
        (text_flat, kv_all, query_part, *arrivals[len(early) :], *wq_others[len(early) :]),
        [shape((rows, local_cols), BF16)] * 2,
        [pltpu.VMEM((rows, local_cols), F32)],
        rows * width * local_cols,
    )
    wq_blocks = [*arrivals, *wq_others]

    att_next = [line.shift(attended, m) for m in (1, line.n_z - 1)]
    attended, grad_come = gate((attended, grad_come))
    att_swapped = line.swap(attended)
    live_y = tensor_swap(live_mine, 2)

    query_grad, kv_part = call(
        functools.partial(backward_kernel, image_own),
        place,
        (queries, kv_all, grad_keep, grad_come),
        [shape((rows, local_cols), BF16), shape((images, 2 * local_cols), F32)],
        (),
        10 * images * rows * local_cols,
    )
    chunk = n_dp // n_tensor
    term = call(
        functools.partial(term_kernel, line, relayed),
        place,
        (query_grad, *wq_blocks),
        [shape((n_tensor, chunk, rows, own_width), BF16)],
        (),
        2 * rows * width * local_cols,
    )
    kv_part, term, live_y, attended, att_swapped, *att_next = gate(
        (kv_part, term, live_y, attended, att_swapped, *att_next)
    )

    kv_part = kv_part.reshape(n_dp, image_rows, 2 * local_cols)
    kv_grad = jnp.sum(lax.all_to_all(kv_part, "dp", split_axis=0, concat_axis=0), axis=0)
    kv_grad_all = everywhere(kv_grad.astype(BF16)).reshape(images, 2 * local_cols)
    text_parts = [tensor_swap(term[k], k) for k in range(2, n_tensor)]
    att_far = [line.shift(attended, m) for m in range(2, line.n_z - 1)]
    att_other_next = [line.swap(block) for block in att_next]
    live_pair = jnp.stack([live_mine, live_y])
    kv_grad_all, term, live_pair, *staged = gate(
        (kv_grad_all, term, live_pair, *att_other_next, *text_parts, *att_far)
    )
    att_other_next, staged = staged[:2], staged[2:]
    text_parts, att_far = staged[: n_tensor - 2], staged[n_tensor - 2 :]

    att_other_far = [line.swap(block) for block in att_far]
    live_core = tensor_swap(live_pair, 1)
    text_parts.append(tensor_swap(term[1], 1))
    image_term = matmul(kv_grad_all[:, :local_cols], key_weight, BACK)
    image_term = image_term + matmul(kv_grad_all[:, local_cols:], value_weight, BACK)
    text_grad = call(
        sum_kernel, place, (term, *text_parts), [shape((rows, width // n_tensor), BF16)]
    )
    image_grad, live_core, text_grad, *att_other_far = to_owner(
        line, image_term.astype(BF16), live_core, text_grad, *att_other_far
    )
    image_grad = image_grad.reshape(samples, image_own, width // n_tensor)
    text_grad = text_grad.reshape(samples, tok_rows, width // n_tensor)

    att_blocks = [attended, att_next[0], *att_far, att_next[1]]
    att_others = [att_swapped, att_other_next[0], *att_other_far, att_other_next[1]]
    weight_grad = call(
        functools.partial(weight_grad_kernel, line),
        place,
        (live_pair, live_core, *att_blocks, *att_others),
        [shape((local_cols, own_width), BF16)],
        [pltpu.VMEM((local_cols, own_width), F32)],
        2 * n_dp * rows * local_cols * own_width,
    )
    return text_grad, image_grad, weight_grad


def solution(mesh):
    return jax.shard_map(
        shards,
        mesh=mesh,
        in_specs=(
            P(None, "dp", None),
            P(None, "dp", None),
            P(None, "dp", None),
            P(),
            P("dp", "tensor"),
            P("dp", "tensor"),
            P("dp", "tensor"),
            P("tensor", "dp"),
        ),
        out_specs=(P(None, "dp", "tensor"), P(None, "dp", "tensor"), P("tensor", "dp")),
        check_vma=False,
    )
```

```python
import functools

import jax
import jax.numpy as jnp
from jax import lax
from jax.experimental import pallas as pl
from jax.experimental.pallas import tpu as pltpu
from jax.sharding import PartitionSpec as P

HEAD_DIM = 128
F32 = jnp.float32
BF16 = jnp.bfloat16
BACK = (((1,), (1,)), ((), ()))
FIRST = (((0,), (0,)), ((), ()))
VMEM_LIMIT = 24 * 1024 * 1024


def matmul(a, b, dims=None):
    if dims is None:
        return jnp.dot(a, b, preferred_element_type=F32)
    return lax.dot_general(a, b, dims, preferred_element_type=F32)


class Line:
    def __init__(self):
        self.n_dp = lax.axis_size("dp")
        self.n_z = self.n_dp // 2

    def move(self, block, moves):
        pairs = [(2 * a + e, 2 * b + e) for a, b in moves for e in range(2)]
        return lax.ppermute(block, "dp", pairs)

    def swap(self, block, planes=None):
        planes = range(self.n_z) if planes is None else planes
        pairs = [(2 * a + e, 2 * a + 1 - e) for a in planes for e in range(2)]
        return lax.ppermute(block, "dp", pairs)

    def shift(self, block, distance):
        n = self.n_z
        return self.move(block, [((a + distance) % n, a) for a in range(n)])

    def first(self, block):
        if self.n_z != 4:
            return [self.shift(block, m) for m in range(1, self.n_z)]
        above = self.move(block, [(1, 0), (2, 1), (3, 2)])
        below = self.move(block, [(0, 1), (1, 2), (2, 3)])
        return [above, below]

    def second(self, moved):
        if self.n_z != 4:
            return []
        return [self.move(moved[0], [(1, 0), (2, 1)]), self.move(moved[1], [(1, 2), (2, 3)])]

    def third(self, forwarded):
        if self.n_z != 4:
            return []
        across = jnp.where(lax.axis_index("dp") < 4, forwarded[0], forwarded[1])
        return [across, self.move(across, [(1, 0), (2, 3)])]

    def slots(self, z, relayed):
        if not relayed:
            return [(m, None) for m in range(self.n_z)]
        return [
            (0, None),
            (1, z < 3),
            (3, z > 0),
            (2, None),
            (jnp.where(z == 3, 1, 3), (z == 3) | (z == 0)),
        ]


def each_block(line, place, relayed, which, body):
    z, x = place[0], place[1]
    slots = line.slots(z, relayed)
    for j, at in enumerate(which):
        m, came = slots[at]
        plane = lax.rem(z + m, line.n_z)
        for e in range(2):
            index = 2 * plane + (x if e == 0 else 1 - x)
            if came is None:
                body(j, e, index)
            else:
                pl.when(came)(functools.partial(body, j, e, index))


def columns(index, size):
    return pl.ds(pl.multiple_of(index * size, size), size)


def probabilities(query, key, image_own):
    scores = matmul(key, query, BACK) * HEAD_DIM ** (-0.5)
    image = lax.broadcasted_iota(jnp.int32, scores.shape, 0)
    token = lax.broadcasted_iota(jnp.int32, scores.shape, 1)
    image_sample = lax.rem(lax.div(image, image_own), 2)
    same = image_sample == lax.div(token, scores.shape[1] // 2)
    scores = jnp.where(same, scores, -1e30)
    peak = jnp.max(scores, axis=0, keepdims=True)
    expo = jnp.where(same, jnp.exp(scores - peak), 0.0)
    return expo / jnp.sum(expo, axis=0, keepdims=True)


def query_kernel(line, relayed, which, place, text, *refs):
    n = len(which)
    weights, total = (refs[:n], refs[n : 2 * n]), refs[-1]
    own_width = weights[0][0].shape[0]
    total[...] = jnp.zeros_like(total)

    def add(j, e, index):
        total[...] += matmul(text[:, columns(index, own_width)], weights[e][j][...])

    each_block(line, place, relayed, which, add)


def forward_kernel(line, relayed, which, image_own, place, text, kv, part, *refs):
    n = len(which)
    weights, (query_out, attended_out, total) = (refs[:n], refs[n : 2 * n]), refs[2 * n :]
    rows, cols = total.shape
    total[...] = part[...]

    def add(j, e, index):
        weight = weights[e][j]
        total[...] += matmul(text[:, columns(index, weight.shape[0])], weight[...])

    each_block(line, place, relayed, which, add)
    query_out[...] = total[...].astype(BF16)
    part_rows = rows // 4
    quarter = place[2]
    for h in range(cols // HEAD_DIM):
        at = slice(h * HEAD_DIM, (h + 1) * HEAD_DIM)
        value = kv[:, cols + h * HEAD_DIM : cols + (h + 1) * HEAD_DIM]
        prob = probabilities(query_out[:, at], kv[:, at], image_own)
        attended = matmul(prob.astype(BF16), value, FIRST).astype(BF16)
        for r in range(4):
            low_bit = (quarter + r) % 2
            high_bit = (quarter // 2 + r // 2) % 2
            start = pl.multiple_of((2 * low_bit + high_bit) * part_rows, part_rows)
            attended_out[pl.ds(start, part_rows), at] = attended[
                r * part_rows : (r + 1) * part_rows
            ]


def grad_kernel(line, which, parts, place, live, mine, by_core, by_y, by_both, *refs):
    before, refs = refs[:parts], refs[parts:]
    weights, outs = refs[: len(which)], refs[len(which) :]
    cut = line.n_dp // 4
    keep, send = outs[-2:]
    keep[...] = before[0][...] if parts else jnp.zeros_like(keep)
    send[...] = before[1][...] if parts else jnp.zeros_like(send)

    def add(j, e, index):
        own_width = weights[j].shape[1] // 2
        weight = weights[j][:, e * own_width : (e + 1) * own_width]
        keep[...] += matmul(live[:, columns(index, own_width)], weight, BACK)
        inner = columns(lax.rem(index, cut), own_width)
        member = lax.bitwise_xor(lax.div(index, cut), place[2])
        other = mine[:, inner]
        for at, piece in ((1, by_core), (2, by_y), (3, by_both)):
            other = jnp.where(member == at, piece[:, inner], other)
        send[...] += matmul(other, weight, BACK)

    each_block(line, place, line.n_z == 4, which, add)
    if parts:
        outs[0][...] = keep[...].astype(BF16)
        outs[1][...] = send[...].astype(BF16)


def backward_kernel(image_own, place, query, kv, keep, come, query_grad, kv_grad):
    cols = query.shape[1]
    half = cols // 2
    x = place[1]
    for h in range(cols // HEAD_DIM):
        at = slice(h * HEAD_DIM, (h + 1) * HEAD_DIM)
        value_at = slice(cols + h * HEAD_DIM, cols + (h + 1) * HEAD_DIM)
        side = h * HEAD_DIM // half
        inner = slice(h * HEAD_DIM - side * half, (h + 1) * HEAD_DIM - side * half)
        grad = jnp.where(x == side, keep[:, inner], come[:, inner])
        prob = probabilities(query[:, at], kv[:, at], image_own)
        kv_grad[:, value_at] = matmul(prob.astype(BF16), grad)
        prob_grad = matmul(kv[:, value_at], grad, BACK)
        delta = jnp.sum(prob * prob_grad, axis=0, keepdims=True)
        score_grad = (prob * (prob_grad - delta) * HEAD_DIM ** (-0.5)).astype(BF16)
        kv_grad[:, at] = matmul(score_grad, query[:, at])
        query_grad[:, at] = matmul(score_grad, kv[:, at], FIRST).astype(BF16)


def term_kernel(line, relayed, place, query_grad, *refs):
    out = refs[-1]
    n = (len(refs) - 1) // 2
    weights = (refs[:n], refs[n : 2 * n])
    chunk = out.shape[1]

    def write(i, e, index):
        term = matmul(query_grad[...], weights[e][i][...], BACK)
        member = lax.bitwise_xor(lax.div(index, chunk), place[3])
        out[member, lax.rem(index, chunk)] = term.astype(BF16)

    each_block(line, place, relayed, range(n), write)


def weight_grad_kernel(line, place, *refs):
    live, refs = refs[:2], refs[2:]
    n = (len(refs) - 2) // 2
    attended, (out, total) = (refs[:n], refs[n : 2 * n]), refs[2 * n :]
    total[...] = jnp.zeros_like(total)

    def add(i, e, index):
        block = jnp.concatenate([part[i, index] for part in live for i in range(2)], axis=0)
        term = matmul(attended[e][i][...], block, FIRST)
        total[...] += term.astype(BF16).astype(F32)

    each_block(line, place, False, range(n), add)
    out[...] = total[...].astype(BF16)


def sum_kernel(place, term, *refs):
    parts, out = refs[:-1], refs[-1]
    width = term.shape[3]
    for c in range(term.shape[1]):
        total = term[0, c].astype(F32)
        for part in parts:
            total = total + part[c].astype(F32)
        out[:, c * width : (c + 1) * width] = total.astype(BF16)


def call(kernel, place, operands, outs, scratch=(), flops=0):
    moved = sum(a.size * a.dtype.itemsize for a in (*operands, *outs))
    single = len(outs) == 1
    return pl.pallas_call(
        kernel,
        out_shape=outs[0] if single else outs,
        in_specs=[pl.BlockSpec(memory_space=pltpu.SMEM)]
        + [pl.BlockSpec(memory_space=pltpu.VMEM)] * len(operands),
        out_specs=pl.BlockSpec(memory_space=pltpu.VMEM)
        if single
        else [pl.BlockSpec(memory_space=pltpu.VMEM)] * len(outs),
        scratch_shapes=list(scratch),
        compiler_params=pltpu.CompilerParams(vmem_limit_bytes=VMEM_LIMIT),
        cost_estimate=pl.CostEstimate(flops=flops, bytes_accessed=moved, transcendentals=0),
    )(place, *operands)


def to_owner(line, terms, *others):
    n_dp, n_tensor = line.n_dp, lax.axis_size("tensor")
    images, cols = terms.shape
    if line.n_z != n_tensor:
        terms = lax.all_to_all(terms, "dp", split_axis=0, concat_axis=1, tiled=True)
        terms = terms.reshape(images // n_dp, n_tensor, n_dp * cols // n_tensor)
        parts = lax.all_to_all(terms, "tensor", split_axis=1, concat_axis=0)
        return (jnp.sum(parts.astype(F32), axis=0).astype(BF16), *others)
    parts = lax.all_to_all(
        terms.reshape(n_tensor, images // n_tensor, cols), "tensor", split_axis=0, concat_axis=0
    )
    total = jnp.sum(parts.astype(F32), axis=0).astype(BF16)
    total, *others = lax.optimization_barrier((total, *others))
    total = total.reshape(2, images // n_dp, cols)
    x = lax.axis_index("dp") % 2
    come = []
    for other in range(2):
        block = jnp.where(x == other, total[0], total[1])
        pairs = [
            ((2 * z + e) * n_tensor + t, (2 * t + (e ^ other)) * n_tensor + z)
            for z in range(line.n_z)
            for e in range(2)
            for t in range(n_tensor)
        ]
        come.append(lax.ppermute(block, ("dp", "tensor"), pairs))
    rows = jnp.where(
        x == 0, jnp.concatenate(come, axis=1), jnp.concatenate(come[::-1], axis=1)
    )
    return (rows, *others)


def shards(
    text_states,
    image_states,
    out_grad,
    text_lengths,
    query_weight,
    key_weight,
    value_weight,
    out_weight,
):
    samples, tok_rows, width = text_states.shape
    image_own = image_states.shape[1]
    line = Line()
    n_dp = line.n_dp
    n_tensor = lax.axis_size("tensor")
    dp_at, tensor_at = lax.axis_index("dp"), lax.axis_index("tensor")
    x, quarter = dp_at % 2, tensor_at % 4
    place = jnp.stack([dp_at // 2, x, quarter, tensor_at]).astype(jnp.int32)
    rows = samples * tok_rows
    image_rows = samples * image_own
    images = n_dp * image_rows
    local_cols = query_weight.shape[1]
    own_width = query_weight.shape[0]
    half_cols = local_cols // 2
    shape = jax.ShapeDtypeStruct

    def tensor_swap(block, bit):
        return lax.ppermute(block, "tensor", [(t, t ^ bit) for t in range(n_tensor)])

    positions = dp_at * tok_rows + lax.iota(jnp.int32, tok_rows)
    live_rows = positions[None, :] < text_lengths[:, None]
    grad_live = jnp.where(live_rows[..., None], out_grad, jnp.zeros_like(out_grad))
    text_flat = text_states.reshape(rows, width)
    live_flat = grad_live.reshape(rows, width)
    image_flat = image_states.reshape(image_rows, width)

    gate = lax.optimization_barrier

    relayed = line.n_z == 4
    wq_moved = line.first(query_weight)
    image_cols = lax.all_to_all(image_flat, "dp", split_axis=1, concat_axis=0, tiled=True)
    wo_keep = lax.dynamic_slice_in_dim(out_weight, x * half_cols, half_cols, 0)
    wo_send = lax.dynamic_slice_in_dim(out_weight, (1 - x) * half_cols, half_cols, 0)
    wo_pair = jnp.concatenate([wo_keep, line.swap(wo_send)], axis=1)
    quarter_cols = width // 4
    live_part = lax.dynamic_slice_in_dim(live_flat, quarter * quarter_cols, quarter_cols, 1)
    live_here = line.swap(live_part)
    image_cols, wo_pair, live_here, query_weight, *wq_moved = gate(
        (image_cols, wo_pair, live_here, query_weight, *wq_moved)
    )

    n_moved = len(wq_moved)
    planes = [(0, 1, 2), (1, 2, 3)] if relayed else [None] * n_moved
    wq_two = line.second(wq_moved)
    wo_moved = line.first(wo_pair)
    above, wq_other = gate((wq_moved[0], line.swap(query_weight)))
    wq_others = [wq_other, line.swap(above, planes[0])]
    part_kv = jnp.concatenate(
        [matmul(image_cols, key_weight), matmul(image_cols, value_weight)], axis=1
    )
    part_kv = part_kv.reshape(n_dp, image_rows, 2 * local_cols)
    kv_own = jnp.sum(lax.all_to_all(part_kv, "dp", split_axis=0, concat_axis=0), axis=0)
    kv_own, live_here, *staged = gate(
        (kv_own.astype(BF16), live_here, *wq_others, *wq_moved, *wq_two, *wo_moved)
    )
    wq_others, staged = staged[:2], staged[2:]
    wq_moved, wq_two, wo_moved = staged[:n_moved], staged[n_moved:-n_moved], staged[-n_moved:]

    def everywhere(values):
        copies = jnp.broadcast_to(values[None], (n_dp, *values.shape))
        return lax.all_to_all(copies, "dp", split_axis=0, concat_axis=0)

    wq_last = line.third(wq_two)
    wo_two = line.second(wo_moved)
    wq_others += [line.swap(block, at) for block, at in zip(wq_moved[1:], planes[1:])]
    wq_others += [line.swap(block) for block in wq_last[:1]]
    kv_all = everywhere(kv_own).reshape(images, 2 * local_cols)
    kv_all, live_here, wo_pair, live_flat, *staged = gate(
        (kv_all, live_here, wo_pair, live_flat, *wo_two, *wq_last, *wq_others)
    )
    wo_two, staged = staged[: len(wo_two)], staged[len(wo_two) :]
    wq_last, wq_others = staged[: len(wq_last)], staged[len(wq_last) :]

    wo_last = line.third(wo_two)
    quarter_rows = rows // 4
    live_rows = lax.dynamic_slice_in_dim(live_flat, quarter * quarter_rows, quarter_rows, 0)
    live_mine = lax.all_to_all(
        live_rows.reshape(quarter_rows, n_dp, own_width), "dp", split_axis=1, concat_axis=0
    )
    live_mine = live_mine.reshape(n_dp, quarter_rows, own_width)
    by_y = tensor_swap(live_here, 2)
    live_pieces = [live_here, tensor_swap(live_here, 1), by_y, tensor_swap(by_y, 1)]
    wq_others += [line.swap(block, (0, 3)) for block in wq_last[1:]]
    arrivals = [query_weight, *wq_moved, *wq_last]
    early = range(4 if relayed else len(arrivals))
    late = range(len(early), len(arrivals))
    query_part = call(
        functools.partial(query_kernel, line, relayed, early),
        place,
        (text_flat, *arrivals[: len(early)], *wq_others[: len(early)]),
        [shape((rows, local_cols), F32)],
        (),
        2 * rows * width * local_cols,
    )

    half = shape((rows, half_cols), F32)
    wo_early = [wo_pair, *wo_moved]
    grad_parts = call(
        functools.partial(grad_kernel, line, range(len(wo_early)), 0),
        place,
        (live_flat, *live_pieces, *wo_early),
        [half] * 2,
        (),
        rows * width * local_cols,
    )

    query_part, *grad_parts = gate((query_part, *grad_parts))

    wo_late = range(len(wo_early), len(wo_early) + len(wo_last))
    grad_keep, grad_send = call(
        functools.partial(grad_kernel, line, wo_late, 2),
        place,
        (live_flat, *live_pieces, *grad_parts, *wo_last),
        [shape((rows, half_cols), BF16)] * 2,
        [pltpu.VMEM((rows, half_cols), F32)] * 2,
        rows * width * local_cols,
    )
    text_flat, live_mine, grad_keep, grad_send = gate(
        (text_flat, live_mine, grad_keep, grad_send)
    )
    grad_come = line.swap(grad_send)
    queries, attended = call(
        functools.partial(forward_kernel, line, relayed, late, image_own),
        place,
        (text_flat, kv_all, query_part, *arrivals[len(early) :], *wq_others[len(early) :]),
        [shape((rows, local_cols), BF16)] * 2,
        [pltpu.VMEM((rows, local_cols), F32)],
        rows * width * local_cols,
    )
    wq_blocks = [*arrivals, *wq_others]

    att_next = [line.shift(attended, m) for m in (1, line.n_z - 1)]
    attended, grad_come = gate((attended, grad_come))
    att_swapped = line.swap(attended)
    live_y = tensor_swap(live_mine, 2)

    query_grad, kv_part = call(
        functools.partial(backward_kernel, image_own),
        place,
        (queries, kv_all, grad_keep, grad_come),
        [shape((rows, local_cols), BF16), shape((images, 2 * local_cols), F32)],
        (),
        10 * images * rows * local_cols,
    )
    chunk = n_dp // n_tensor
    term = call(
        functools.partial(term_kernel, line, relayed),
        place,
        (query_grad, *wq_blocks),
        [shape((n_tensor, chunk, rows, own_width), BF16)],
        (),
        2 * rows * width * local_cols,
    )
    kv_part, term, live_y, attended, att_swapped, *att_next = gate(
        (kv_part, term, live_y, attended, att_swapped, *att_next)
    )

    kv_part = kv_part.reshape(n_dp, image_rows, 2 * local_cols)
    kv_grad = jnp.sum(lax.all_to_all(kv_part, "dp", split_axis=0, concat_axis=0), axis=0)
    kv_grad_all = everywhere(kv_grad.astype(BF16)).reshape(images, 2 * local_cols)
    text_parts = [tensor_swap(term[k], k) for k in range(2, n_tensor)]
    att_far = [line.shift(attended, m) for m in range(2, line.n_z - 1)]
    att_other_next = [line.swap(block) for block in att_next]
    live_pair = jnp.stack([live_mine, live_y])
    att_other_far = [line.swap(block) for block in att_far]
    live_core = tensor_swap(live_pair, 1)

    att_blocks = [attended, att_next[0], *att_far, att_next[1]]
    att_others = [att_swapped, att_other_next[0], *att_other_far, att_other_next[1]]
    weight_grad = call(
        functools.partial(weight_grad_kernel, line),
        place,
        (live_pair, live_core, *att_blocks, *att_others),
        [shape((local_cols, own_width), BF16)],
        [pltpu.VMEM((local_cols, own_width), F32)],
        2 * n_dp * rows * local_cols * own_width,
    )
    kv_grad_all, term, weight_grad, *text_parts = gate(
        (kv_grad_all, term, weight_grad, *text_parts)
    )

    text_parts.append(tensor_swap(term[1], 1))
    image_term = matmul(kv_grad_all[:, :local_cols], key_weight, BACK)
    image_term = image_term + matmul(kv_grad_all[:, local_cols:], value_weight, BACK)
    text_grad = call(
        sum_kernel, place, (term, *text_parts), [shape((rows, width // n_tensor), BF16)]
    )
    image_grad, text_grad = to_owner(line, image_term.astype(BF16), text_grad)
    image_grad = image_grad.reshape(samples, image_own, width // n_tensor)
    text_grad = text_grad.reshape(samples, tok_rows, width // n_tensor)

    return text_grad, image_grad, weight_grad


def solution(mesh):
    return jax.shard_map(
        shards,
        mesh=mesh,
        in_specs=(
            P(None, "dp", None),
            P(None, "dp", None),
            P(None, "dp", None),
            P(),
            P("dp", "tensor"),
            P("dp", "tensor"),
            P("dp", "tensor"),
            P("tensor", "dp"),
        ),
        out_specs=(P(None, "dp", "tensor"), P(None, "dp", "tensor"), P("tensor", "dp")),
        check_vma=False,
    )
```

```python
import functools

import jax
import jax.numpy as jnp
from jax import lax
from jax.experimental import pallas as pl
from jax.experimental.pallas import tpu as pltpu
from jax.sharding import PartitionSpec as P

HEAD_DIM = 128
F32 = jnp.float32
BF16 = jnp.bfloat16
BACK = (((1,), (1,)), ((), ()))
FIRST = (((0,), (0,)), ((), ()))
VMEM_LIMIT = 24 * 1024 * 1024


def matmul(a, b, dims=None):
    if dims is None:
        return jnp.dot(a, b, preferred_element_type=F32)
    return lax.dot_general(a, b, dims, preferred_element_type=F32)


class Line:
    def __init__(self):
        self.n_dp = lax.axis_size("dp")
        self.n_z = self.n_dp // 2

    def move(self, block, moves):
        pairs = [(2 * a + e, 2 * b + e) for a, b in moves for e in range(2)]
        return lax.ppermute(block, "dp", pairs)

    def swap(self, block, planes=None):
        planes = range(self.n_z) if planes is None else planes
        pairs = [(2 * a + e, 2 * a + 1 - e) for a in planes for e in range(2)]
        return lax.ppermute(block, "dp", pairs)

    def shift(self, block, distance):
        n = self.n_z
        return self.move(block, [((a + distance) % n, a) for a in range(n)])

    def first(self, block):
        if self.n_z != 4:
            return [self.shift(block, m) for m in range(1, self.n_z)]
        above = self.move(block, [(1, 0), (2, 1), (3, 2)])
        below = self.move(block, [(0, 1), (1, 2), (2, 3)])
        return [above, below]

    def second(self, moved):
        if self.n_z != 4:
            return []
        return [self.move(moved[0], [(1, 0), (2, 1)]), self.move(moved[1], [(1, 2), (2, 3)])]

    def third(self, forwarded):
        if self.n_z != 4:
            return []
        across = jnp.where(lax.axis_index("dp") < 4, forwarded[0], forwarded[1])
        return [across, self.move(across, [(1, 0), (2, 3)])]

    def slots(self, z, relayed):
        if not relayed:
            return [(m, None) for m in range(self.n_z)]
        return [
            (0, None),
            (1, z < 3),
            (3, z > 0),
            (2, None),
            (jnp.where(z == 3, 1, 3), (z == 3) | (z == 0)),
        ]


def each_block(line, place, relayed, which, body):
    z, x = place[0], place[1]
    slots = line.slots(z, relayed)
    for j, at in enumerate(which):
        m, came = slots[at]
        plane = lax.rem(z + m, line.n_z)
        for e in range(2):
            index = 2 * plane + (x if e == 0 else 1 - x)
            if came is None:
                body(j, e, index)
            else:
                pl.when(came)(functools.partial(body, j, e, index))


def columns(index, size):
    return pl.ds(pl.multiple_of(index * size, size), size)


def probabilities(query, key, image_own):
    scores = matmul(key, query, BACK) * HEAD_DIM ** (-0.5)
    image = lax.broadcasted_iota(jnp.int32, scores.shape, 0)
    token = lax.broadcasted_iota(jnp.int32, scores.shape, 1)
    image_sample = lax.rem(lax.div(image, image_own), 2)
    same = image_sample == lax.div(token, scores.shape[1] // 2)
    scores = jnp.where(same, scores, -1e30)
    peak = jnp.max(scores, axis=0, keepdims=True)
    expo = jnp.where(same, jnp.exp(scores - peak), 0.0)
    return expo / jnp.sum(expo, axis=0, keepdims=True)


def query_kernel(line, relayed, which, place, text, *refs):
    n = len(which)
    weights, total = (refs[:n], refs[n : 2 * n]), refs[-1]
    own_width = weights[0][0].shape[0]
    total[...] = jnp.zeros_like(total)

    def add(j, e, index):
        total[...] += matmul(text[:, columns(index, own_width)], weights[e][j][...])

    each_block(line, place, relayed, which, add)


def forward_kernel(line, relayed, which, image_own, place, text, kv, part, *refs):
    n = len(which)
    weights, (query_out, attended_out, total) = (refs[:n], refs[n : 2 * n]), refs[2 * n :]
    rows, cols = total.shape
    total[...] = part[...]

    def add(j, e, index):
        weight = weights[e][j]
        total[...] += matmul(text[:, columns(index, weight.shape[0])], weight[...])

    each_block(line, place, relayed, which, add)
    query_out[...] = total[...].astype(BF16)
    part_rows = rows // 4
    quarter = place[2]
    for h in range(cols // HEAD_DIM):
        at = slice(h * HEAD_DIM, (h + 1) * HEAD_DIM)
        value = kv[:, cols + h * HEAD_DIM : cols + (h + 1) * HEAD_DIM]
        prob = probabilities(query_out[:, at], kv[:, at], image_own)
        attended = matmul(prob.astype(BF16), value, FIRST).astype(BF16)
        for r in range(4):
            low_bit = (quarter + r) % 2
            high_bit = (quarter // 2 + r // 2) % 2
            start = pl.multiple_of((2 * low_bit + high_bit) * part_rows, part_rows)
            attended_out[pl.ds(start, part_rows), at] = attended[
                r * part_rows : (r + 1) * part_rows
            ]


def grad_kernel(line, which, parts, place, live, mine, by_core, by_y, by_both, *refs):
    before, refs = refs[:parts], refs[parts:]
    weights, outs = refs[: len(which)], refs[len(which) :]
    cut = line.n_dp // 4
    keep, send = outs[-2:]
    keep[...] = before[0][...] if parts else jnp.zeros_like(keep)
    send[...] = before[1][...] if parts else jnp.zeros_like(send)

    def add(j, e, index):
        own_width = weights[j].shape[1] // 2
        weight = weights[j][:, e * own_width : (e + 1) * own_width]
        keep[...] += matmul(live[:, columns(index, own_width)], weight, BACK)
        inner = columns(lax.rem(index, cut), own_width)
        member = lax.bitwise_xor(lax.div(index, cut), place[2])
        other = mine[:, inner]
        for at, piece in ((1, by_core), (2, by_y), (3, by_both)):
            other = jnp.where(member == at, piece[:, inner], other)
        send[...] += matmul(other, weight, BACK)

    each_block(line, place, line.n_z == 4, which, add)
    if parts:
        outs[0][...] = keep[...].astype(BF16)
        outs[1][...] = send[...].astype(BF16)


def backward_kernel(image_own, place, query, kv, keep, come, query_grad, kv_grad):
    cols = query.shape[1]
    half = cols // 2
    x = place[1]
    for h in range(cols // HEAD_DIM):
        at = slice(h * HEAD_DIM, (h + 1) * HEAD_DIM)
        value_at = slice(cols + h * HEAD_DIM, cols + (h + 1) * HEAD_DIM)
        side = h * HEAD_DIM // half
        inner = slice(h * HEAD_DIM - side * half, (h + 1) * HEAD_DIM - side * half)
        grad = jnp.where(x == side, keep[:, inner], come[:, inner])
        prob = probabilities(query[:, at], kv[:, at], image_own)
        kv_grad[:, value_at] = matmul(prob.astype(BF16), grad)
        prob_grad = matmul(kv[:, value_at], grad, BACK)
        delta = jnp.sum(prob * prob_grad, axis=0, keepdims=True)
        score_grad = (prob * (prob_grad - delta) * HEAD_DIM ** (-0.5)).astype(BF16)
        kv_grad[:, at] = matmul(score_grad, query[:, at])
        query_grad[:, at] = matmul(score_grad, kv[:, at], FIRST).astype(BF16)


def term_kernel(line, relayed, place, query_grad, *refs):
    out = refs[-1]
    n = (len(refs) - 1) // 2
    weights = (refs[:n], refs[n : 2 * n])
    chunk = out.shape[1]

    def write(i, e, index):
        term = matmul(query_grad[...], weights[e][i][...], BACK)
        member = lax.bitwise_xor(lax.div(index, chunk), place[3])
        out[member, lax.rem(index, chunk)] = term.astype(BF16)

    each_block(line, place, relayed, range(n), write)


def weight_grad_kernel(line, place, *refs):
    live, refs = refs[:2], refs[2:]
    n = (len(refs) - 2) // 2
    attended, (out, total) = (refs[:n], refs[n : 2 * n]), refs[2 * n :]
    total[...] = jnp.zeros_like(total)

    def add(i, e, index):
        block = jnp.concatenate([part[i, index] for part in live for i in range(2)], axis=0)
        term = matmul(attended[e][i][...], block, FIRST)
        total[...] += term.astype(BF16).astype(F32)

    each_block(line, place, False, range(n), add)
    out[...] = total[...].astype(BF16)


def sum_kernel(place, term, *refs):
    parts, out = refs[:-1], refs[-1]
    width = term.shape[3]
    for c in range(term.shape[1]):
        total = term[0, c].astype(F32)
        for part in parts:
            total = total + part[c].astype(F32)
        out[:, c * width : (c + 1) * width] = total.astype(BF16)


def call(kernel, place, operands, outs, scratch=(), flops=0):
    moved = sum(a.size * a.dtype.itemsize for a in (*operands, *outs))
    single = len(outs) == 1
    return pl.pallas_call(
        kernel,
        out_shape=outs[0] if single else outs,
        in_specs=[pl.BlockSpec(memory_space=pltpu.SMEM)]
        + [pl.BlockSpec(memory_space=pltpu.VMEM)] * len(operands),
        out_specs=pl.BlockSpec(memory_space=pltpu.VMEM)
        if single
        else [pl.BlockSpec(memory_space=pltpu.VMEM)] * len(outs),
        scratch_shapes=list(scratch),
        compiler_params=pltpu.CompilerParams(vmem_limit_bytes=VMEM_LIMIT),
        cost_estimate=pl.CostEstimate(flops=flops, bytes_accessed=moved, transcendentals=0),
    )(place, *operands)


def to_owner(line, terms, *others):
    n_dp, n_tensor = line.n_dp, lax.axis_size("tensor")
    images, cols = terms.shape
    if line.n_z != n_tensor:
        terms = lax.all_to_all(terms, "dp", split_axis=0, concat_axis=1, tiled=True)
        terms = terms.reshape(images // n_dp, n_tensor, n_dp * cols // n_tensor)
        parts = lax.all_to_all(terms, "tensor", split_axis=1, concat_axis=0)
        return (jnp.sum(parts.astype(F32), axis=0).astype(BF16), *others)
    parts = lax.all_to_all(
        terms.reshape(n_tensor, images // n_tensor, cols), "tensor", split_axis=0, concat_axis=0
    )
    total = jnp.sum(parts.astype(F32), axis=0).astype(BF16)
    total, *others = lax.optimization_barrier((total, *others))
    total = total.reshape(2, images // n_dp, cols)
    x = lax.axis_index("dp") % 2
    come = []
    for other in range(2):
        block = jnp.where(x == other, total[0], total[1])
        pairs = [
            ((2 * z + e) * n_tensor + t, (2 * t + (e ^ other)) * n_tensor + z)
            for z in range(line.n_z)
            for e in range(2)
            for t in range(n_tensor)
        ]
        come.append(lax.ppermute(block, ("dp", "tensor"), pairs))
    rows = jnp.where(
        x == 0, jnp.concatenate(come, axis=1), jnp.concatenate(come[::-1], axis=1)
    )
    return (rows, *others)


def shards(
    text_states,
    image_states,
    out_grad,
    text_lengths,
    query_weight,
    key_weight,
    value_weight,
    out_weight,
):
    samples, tok_rows, width = text_states.shape
    image_own = image_states.shape[1]
    line = Line()
    n_dp = line.n_dp
    n_tensor = lax.axis_size("tensor")
    dp_at, tensor_at = lax.axis_index("dp"), lax.axis_index("tensor")
    x, quarter = dp_at % 2, tensor_at % 4
    place = jnp.stack([dp_at // 2, x, quarter, tensor_at]).astype(jnp.int32)
    rows = samples * tok_rows
    image_rows = samples * image_own
    images = n_dp * image_rows
    local_cols = query_weight.shape[1]
    own_width = query_weight.shape[0]
    half_cols = local_cols // 2
    shape = jax.ShapeDtypeStruct

    def tensor_swap(block, bit):
        return lax.ppermute(block, "tensor", [(t, t ^ bit) for t in range(n_tensor)])

    positions = dp_at * tok_rows + lax.iota(jnp.int32, tok_rows)
    live_rows = positions[None, :] < text_lengths[:, None]
    grad_live = jnp.where(live_rows[..., None], out_grad, jnp.zeros_like(out_grad))
    text_flat = text_states.reshape(rows, width)
    live_flat = grad_live.reshape(rows, width)
    image_flat = image_states.reshape(image_rows, width)

    gate = lax.optimization_barrier

    relayed = line.n_z == 4
    wq_moved = line.first(query_weight)
    image_cols = lax.all_to_all(image_flat, "dp", split_axis=1, concat_axis=0, tiled=True)
    wo_keep = lax.dynamic_slice_in_dim(out_weight, x * half_cols, half_cols, 0)
    wo_send = lax.dynamic_slice_in_dim(out_weight, (1 - x) * half_cols, half_cols, 0)
    wo_pair = jnp.concatenate([wo_keep, line.swap(wo_send)], axis=1)
    quarter_cols = width // 4
    live_part = lax.dynamic_slice_in_dim(live_flat, quarter * quarter_cols, quarter_cols, 1)
    live_here = line.swap(live_part)
    image_cols, wo_pair, live_here, query_weight, *wq_moved = gate(
        (image_cols, wo_pair, live_here, query_weight, *wq_moved)
    )

    n_moved = len(wq_moved)
    planes = [(0, 1, 2), (1, 2, 3)] if relayed else [None] * n_moved
    wq_two = line.second(wq_moved)
    wo_moved = line.first(wo_pair)
    above, wq_other = gate((wq_moved[0], line.swap(query_weight)))
    wq_others = [wq_other, line.swap(above, planes[0])]
    part_kv = jnp.concatenate(
        [matmul(image_cols, key_weight), matmul(image_cols, value_weight)], axis=1
    )
    part_kv = part_kv.reshape(n_dp, image_rows, 2 * local_cols)
    kv_own = jnp.sum(lax.all_to_all(part_kv, "dp", split_axis=0, concat_axis=0), axis=0)
    kv_own, live_here, *staged = gate(
        (kv_own.astype(BF16), live_here, *wq_others, *wq_moved, *wq_two, *wo_moved)
    )
    wq_others, staged = staged[:2], staged[2:]
    wq_moved, wq_two, wo_moved = staged[:n_moved], staged[n_moved:-n_moved], staged[-n_moved:]

    def everywhere(values):
        copies = jnp.broadcast_to(values[None], (n_dp, *values.shape))
        return lax.all_to_all(copies, "dp", split_axis=0, concat_axis=0)

    wq_last = line.third(wq_two)
    wo_two = line.second(wo_moved)
    wq_others += [line.swap(block, at) for block, at in zip(wq_moved[1:], planes[1:])]
    wq_others += [line.swap(block) for block in wq_last[:1]]
    kv_all = everywhere(kv_own).reshape(images, 2 * local_cols)
    early = range(2 if relayed else 1 + n_moved)
    query_part = call(
        functools.partial(query_kernel, line, relayed, early),
        place,
        (text_flat, query_weight, *wq_moved[: len(early) - 1], *wq_others[: len(early)]),
        [shape((rows, local_cols), F32)],
        (),
        rows * width * local_cols,
    )
    kv_all, query_part, live_here, wo_pair, live_flat, *staged = gate(
        (kv_all, query_part, live_here, wo_pair, live_flat, *wo_two, *wq_last, *wq_others)
    )
    wo_two, staged = staged[: len(wo_two)], staged[len(wo_two) :]
    wq_last, wq_others = staged[: len(wq_last)], staged[len(wq_last) :]

    wo_last = line.third(wo_two)
    quarter_rows = rows // 4
    live_rows = lax.dynamic_slice_in_dim(live_flat, quarter * quarter_rows, quarter_rows, 0)
    live_mine = lax.all_to_all(
        live_rows.reshape(quarter_rows, n_dp, own_width), "dp", split_axis=1, concat_axis=0
    )
    live_mine = live_mine.reshape(n_dp, quarter_rows, own_width)
    by_y = tensor_swap(live_here, 2)
    live_pieces = [live_here, tensor_swap(live_here, 1), by_y, tensor_swap(by_y, 1)]
    wq_others += [line.swap(block, (0, 3)) for block in wq_last[1:]]
    half = shape((rows, half_cols), F32)
    wo_early = [wo_pair, *wo_moved]
    grad_parts = call(
        functools.partial(grad_kernel, line, range(len(wo_early)), 0),
        place,
        (live_flat, *live_pieces, *wo_early),
        [half] * 2,
        (),
        rows * width * local_cols,
    )

    arrivals = [query_weight, *wq_moved, *wq_last]
    late = range(len(early), len(arrivals))

    wo_late = range(len(wo_early), len(wo_early) + len(wo_last))
    grad_keep, grad_send = call(
        functools.partial(grad_kernel, line, wo_late, 2),
        place,
        (live_flat, *live_pieces, *grad_parts, *wo_last),
        [shape((rows, half_cols), BF16)] * 2,
        [pltpu.VMEM((rows, half_cols), F32)] * 2,
        rows * width * local_cols,
    )
    text_flat, grad_keep, grad_send = gate((text_flat, grad_keep, grad_send))
    grad_come = line.swap(grad_send)
    queries, attended = call(
        functools.partial(forward_kernel, line, relayed, late, image_own),
        place,
        (text_flat, kv_all, query_part, *arrivals[len(early) :], *wq_others[len(early) :]),
        [shape((rows, local_cols), BF16)] * 2,
        [pltpu.VMEM((rows, local_cols), F32)],
        rows * width * local_cols,
    )
    wq_blocks = [*arrivals, *wq_others]

    att_next = [line.shift(attended, m) for m in (1, line.n_z - 1)]
    attended, grad_come = gate((attended, grad_come))
    att_swapped = line.swap(attended)

    query_grad, kv_part = call(
        functools.partial(backward_kernel, image_own),
        place,
        (queries, kv_all, grad_keep, grad_come),
        [shape((rows, local_cols), BF16), shape((images, 2 * local_cols), F32)],
        (),
        10 * images * rows * local_cols,
    )
    chunk = n_dp // n_tensor
    term = call(
        functools.partial(term_kernel, line, relayed),
        place,
        (query_grad, *wq_blocks),
        [shape((n_tensor, chunk, rows, own_width), BF16)],
        (),
        2 * rows * width * local_cols,
    )
    kv_part, term, live_y, attended, att_swapped, *att_next = gate(
        (kv_part, term, tensor_swap(live_mine, 2), attended, att_swapped, *att_next)
    )

    kv_part = kv_part.reshape(n_dp, image_rows, 2 * local_cols)
    kv_grad = jnp.sum(lax.all_to_all(kv_part, "dp", split_axis=0, concat_axis=0), axis=0)
    kv_grad_all = everywhere(kv_grad.astype(BF16)).reshape(images, 2 * local_cols)
    text_parts = [tensor_swap(term[k], k) for k in range(2, n_tensor)]
    att_far = [line.shift(attended, m) for m in range(2, line.n_z - 1)]
    att_other_next = [line.swap(block) for block in att_next]
    live_pair = jnp.stack([live_mine, live_y])
    kv_grad_all, term, live_pair, *staged = gate(
        (kv_grad_all, term, live_pair, *att_other_next, *text_parts, *att_far)
    )
    att_other_next, staged = staged[:2], staged[2:]
    text_parts, att_far = staged[: n_tensor - 2], staged[n_tensor - 2 :]

    att_other_far = [line.swap(block) for block in att_far]
    live_core = tensor_swap(live_pair, 1)
    text_parts.append(tensor_swap(term[1], 1))
    image_term = matmul(kv_grad_all[:, :local_cols], key_weight, BACK)
    image_term = image_term + matmul(kv_grad_all[:, local_cols:], value_weight, BACK)
    text_grad = call(
        sum_kernel, place, (term, *text_parts), [shape((rows, width // n_tensor), BF16)]
    )
    image_grad, live_core, text_grad, *att_other_far = to_owner(
        line, image_term.astype(BF16), live_core, text_grad, *att_other_far
    )
    image_grad = image_grad.reshape(samples, image_own, width // n_tensor)
    text_grad = text_grad.reshape(samples, tok_rows, width // n_tensor)

    att_blocks = [attended, att_next[0], *att_far, att_next[1]]
    att_others = [att_swapped, att_other_next[0], *att_other_far, att_other_next[1]]
    weight_grad = call(
        functools.partial(weight_grad_kernel, line),
        place,
        (live_pair, live_core, *att_blocks, *att_others),
        [shape((local_cols, own_width), BF16)],
        [pltpu.VMEM((local_cols, own_width), F32)],
        2 * n_dp * rows * local_cols * own_width,
    )
    return text_grad, image_grad, weight_grad


def solution(mesh):
    return jax.shard_map(
        shards,
        mesh=mesh,
        in_specs=(
            P(None, "dp", None),
            P(None, "dp", None),
            P(None, "dp", None),
            P(),
            P("dp", "tensor"),
            P("dp", "tensor"),
            P("dp", "tensor"),
            P("tensor", "dp"),
        ),
        out_specs=(P(None, "dp", "tensor"), P(None, "dp", "tensor"), P("tensor", "dp")),
        check_vma=False,
    )
```

```python
import functools

import jax
import jax.numpy as jnp
from jax import lax
from jax.experimental import pallas as pl
from jax.experimental.pallas import tpu as pltpu
from jax.sharding import PartitionSpec as P

HEAD_DIM = 128
F32 = jnp.float32
BF16 = jnp.bfloat16
BACK = (((1,), (1,)), ((), ()))
FIRST = (((0,), (0,)), ((), ()))
VMEM_LIMIT = 24 * 1024 * 1024


def matmul(a, b, dims=None):
    if dims is None:
        return jnp.dot(a, b, preferred_element_type=F32)
    return lax.dot_general(a, b, dims, preferred_element_type=F32)


class Line:
    def __init__(self):
        self.n_dp = lax.axis_size("dp")
        self.n_z = self.n_dp // 2

    def move(self, block, moves):
        pairs = [(2 * a + e, 2 * b + e) for a, b in moves for e in range(2)]
        return lax.ppermute(block, "dp", pairs)

    def swap(self, block, planes=None):
        planes = range(self.n_z) if planes is None else planes
        pairs = [(2 * a + e, 2 * a + 1 - e) for a in planes for e in range(2)]
        return lax.ppermute(block, "dp", pairs)

    def shift(self, block, distance):
        n = self.n_z
        return self.move(block, [((a + distance) % n, a) for a in range(n)])

    def first(self, block):
        if self.n_z != 4:
            return [self.shift(block, m) for m in range(1, self.n_z)]
        above = self.move(block, [(1, 0), (2, 1), (3, 2)])
        below = self.move(block, [(0, 1), (1, 2), (2, 3)])
        return [above, below]

    def second(self, moved):
        if self.n_z != 4:
            return []
        return [self.move(moved[0], [(1, 0), (2, 1)]), self.move(moved[1], [(1, 2), (2, 3)])]

    def third(self, forwarded):
        if self.n_z != 4:
            return []
        across = jnp.where(lax.axis_index("dp") < 4, forwarded[0], forwarded[1])
        return [across, self.move(across, [(1, 0), (2, 3)])]

    def slots(self, z, relayed):
        if not relayed:
            return [(m, None) for m in range(self.n_z)]
        return [
            (0, None),
            (1, z < 3),
            (3, z > 0),
            (2, None),
            (jnp.where(z == 3, 1, 3), (z == 3) | (z == 0)),
        ]


def each_block(line, place, relayed, which, body):
    z, x = place[0], place[1]
    slots = line.slots(z, relayed)
    for j, at in enumerate(which):
        m, came = slots[at]
        plane = lax.rem(z + m, line.n_z)
        for e in range(2):
            index = 2 * plane + (x if e == 0 else 1 - x)
            if came is None:
                body(j, e, index)
            else:
                pl.when(came)(functools.partial(body, j, e, index))


def columns(index, size):
    return pl.ds(pl.multiple_of(index * size, size), size)


def probabilities(query, key, image_own):
    scores = matmul(key, query, BACK) * HEAD_DIM ** (-0.5)
    image = lax.broadcasted_iota(jnp.int32, scores.shape, 0)
    token = lax.broadcasted_iota(jnp.int32, scores.shape, 1)
    image_sample = lax.rem(lax.div(image, image_own), 2)
    same = image_sample == lax.div(token, scores.shape[1] // 2)
    scores = jnp.where(same, scores, -1e30)
    peak = jnp.max(scores, axis=0, keepdims=True)
    expo = jnp.where(same, jnp.exp(scores - peak), 0.0)
    return expo / jnp.sum(expo, axis=0, keepdims=True)


def query_kernel(line, relayed, which, place, text, *refs):
    n = len(which)
    weights, total = (refs[:n], refs[n : 2 * n]), refs[-1]
    own_width = weights[0][0].shape[0]
    total[...] = jnp.zeros_like(total)

    def add(j, e, index):
        total[...] += matmul(text[:, columns(index, own_width)], weights[e][j][...])

    each_block(line, place, relayed, which, add)


def forward_kernel(line, relayed, which, image_own, place, text, kv, part, *refs):
    n = len(which)
    weights, (query_out, attended_out, total) = (refs[:n], refs[n : 2 * n]), refs[2 * n :]
    rows, cols = total.shape
    total[...] = part[...]

    def add(j, e, index):
        weight = weights[e][j]
        total[...] += matmul(text[:, columns(index, weight.shape[0])], weight[...])

    each_block(line, place, relayed, which, add)
    query_out[...] = total[...].astype(BF16)
    part_rows = rows // 4
    quarter = place[2]
    for h in range(cols // HEAD_DIM):
        at = slice(h * HEAD_DIM, (h + 1) * HEAD_DIM)
        value = kv[:, cols + h * HEAD_DIM : cols + (h + 1) * HEAD_DIM]
        prob = probabilities(query_out[:, at], kv[:, at], image_own)
        attended = matmul(prob.astype(BF16), value, FIRST).astype(BF16)
        for r in range(4):
            low_bit = (quarter + r) % 2
            high_bit = (quarter // 2 + r // 2) % 2
            start = pl.multiple_of((2 * low_bit + high_bit) * part_rows, part_rows)
            attended_out[pl.ds(start, part_rows), at] = attended[
                r * part_rows : (r + 1) * part_rows
            ]


def grad_kernel(line, which, parts, place, live, mine, by_core, by_y, by_both, *refs):
    before, refs = refs[:parts], refs[parts:]
    weights, outs = refs[: len(which)], refs[len(which) :]
    cut = line.n_dp // 4
    keep, send = outs[-2:]
    keep[...] = before[0][...] if parts else jnp.zeros_like(keep)
    send[...] = before[1][...] if parts else jnp.zeros_like(send)

    def add(j, e, index):
        own_width = weights[j].shape[1] // 2
        weight = weights[j][:, e * own_width : (e + 1) * own_width]
        keep[...] += matmul(live[:, columns(index, own_width)], weight, BACK)
        inner = columns(lax.rem(index, cut), own_width)
        member = lax.bitwise_xor(lax.div(index, cut), place[2])
        other = mine[:, inner]
        for at, piece in ((1, by_core), (2, by_y), (3, by_both)):
            other = jnp.where(member == at, piece[:, inner], other)
        send[...] += matmul(other, weight, BACK)

    each_block(line, place, line.n_z == 4, which, add)
    if parts:
        outs[0][...] = keep[...].astype(BF16)
        outs[1][...] = send[...].astype(BF16)


def backward_kernel(image_own, place, query, kv, keep, come, query_grad, kv_grad):
    cols = query.shape[1]
    half = cols // 2
    x = place[1]
    for h in range(cols // HEAD_DIM):
        at = slice(h * HEAD_DIM, (h + 1) * HEAD_DIM)
        value_at = slice(cols + h * HEAD_DIM, cols + (h + 1) * HEAD_DIM)
        side = h * HEAD_DIM // half
        inner = slice(h * HEAD_DIM - side * half, (h + 1) * HEAD_DIM - side * half)
        grad = jnp.where(x == side, keep[:, inner], come[:, inner])
        prob = probabilities(query[:, at], kv[:, at], image_own)
        kv_grad[:, value_at] = matmul(prob.astype(BF16), grad)
        prob_grad = matmul(kv[:, value_at], grad, BACK)
        delta = jnp.sum(prob * prob_grad, axis=0, keepdims=True)
        score_grad = (prob * (prob_grad - delta) * HEAD_DIM ** (-0.5)).astype(BF16)
        kv_grad[:, at] = matmul(score_grad, query[:, at])
        query_grad[:, at] = matmul(score_grad, kv[:, at], FIRST).astype(BF16)


def term_kernel(line, relayed, place, query_grad, *refs):
    out = refs[-1]
    n = (len(refs) - 1) // 2
    weights = (refs[:n], refs[n : 2 * n])
    chunk = out.shape[1]

    def write(i, e, index):
        term = matmul(query_grad[...], weights[e][i][...], BACK)
        member = lax.bitwise_xor(lax.div(index, chunk), place[3])
        out[member, lax.rem(index, chunk)] = term.astype(BF16)

    each_block(line, place, relayed, range(n), write)


def weight_grad_kernel(line, place, *refs):
    live, refs = refs[:2], refs[2:]
    n = (len(refs) - 2) // 2
    attended, (out, total) = (refs[:n], refs[n : 2 * n]), refs[2 * n :]
    total[...] = jnp.zeros_like(total)

    def add(i, e, index):
        block = jnp.concatenate([part[i, index] for part in live for i in range(2)], axis=0)
        term = matmul(attended[e][i][...], block, FIRST)
        total[...] += term.astype(BF16).astype(F32)

    each_block(line, place, False, range(n), add)
    out[...] = total[...].astype(BF16)


def sum_kernel(place, term, *refs):
    parts, out = refs[:-1], refs[-1]
    width = term.shape[3]
    for c in range(term.shape[1]):
        total = term[0, c].astype(F32)
        for part in parts:
            total = total + part[c].astype(F32)
        out[:, c * width : (c + 1) * width] = total.astype(BF16)


def call(kernel, place, operands, outs, scratch=(), flops=0):
    moved = sum(a.size * a.dtype.itemsize for a in (*operands, *outs))
    single = len(outs) == 1
    return pl.pallas_call(
        kernel,
        out_shape=outs[0] if single else outs,
        in_specs=[pl.BlockSpec(memory_space=pltpu.SMEM)]
        + [pl.BlockSpec(memory_space=pltpu.VMEM)] * len(operands),
        out_specs=pl.BlockSpec(memory_space=pltpu.VMEM)
        if single
        else [pl.BlockSpec(memory_space=pltpu.VMEM)] * len(outs),
        scratch_shapes=list(scratch),
        compiler_params=pltpu.CompilerParams(vmem_limit_bytes=VMEM_LIMIT),
        cost_estimate=pl.CostEstimate(flops=flops, bytes_accessed=moved, transcendentals=0),
    )(place, *operands)


def to_owner(line, terms, *others):
    n_dp, n_tensor = line.n_dp, lax.axis_size("tensor")
    images, cols = terms.shape
    if line.n_z != n_tensor:
        terms = lax.all_to_all(terms, "dp", split_axis=0, concat_axis=1, tiled=True)
        terms = terms.reshape(images // n_dp, n_tensor, n_dp * cols // n_tensor)
        parts = lax.all_to_all(terms, "tensor", split_axis=1, concat_axis=0)
        return (jnp.sum(parts.astype(F32), axis=0).astype(BF16), *others)
    parts = lax.all_to_all(
        terms.reshape(n_tensor, images // n_tensor, cols), "tensor", split_axis=0, concat_axis=0
    )
    total = jnp.sum(parts.astype(F32), axis=0).astype(BF16)
    total, *others = lax.optimization_barrier((total, *others))
    total = total.reshape(2, images // n_dp, cols)
    x = lax.axis_index("dp") % 2
    come = []
    for other in range(2):
        block = jnp.where(x == other, total[0], total[1])
        pairs = [
            ((2 * z + e) * n_tensor + t, (2 * t + (e ^ other)) * n_tensor + z)
            for z in range(line.n_z)
            for e in range(2)
            for t in range(n_tensor)
        ]
        come.append(lax.ppermute(block, ("dp", "tensor"), pairs))
    rows = jnp.where(
        x == 0, jnp.concatenate(come, axis=1), jnp.concatenate(come[::-1], axis=1)
    )
    return (rows, *others)


def shards(
    text_states,
    image_states,
    out_grad,
    text_lengths,
    query_weight,
    key_weight,
    value_weight,
    out_weight,
):
    samples, tok_rows, width = text_states.shape
    image_own = image_states.shape[1]
    line = Line()
    n_dp = line.n_dp
    n_tensor = lax.axis_size("tensor")
    dp_at, tensor_at = lax.axis_index("dp"), lax.axis_index("tensor")
    x, quarter = dp_at % 2, tensor_at % 4
    place = jnp.stack([dp_at // 2, x, quarter, tensor_at]).astype(jnp.int32)
    rows = samples * tok_rows
    image_rows = samples * image_own
    images = n_dp * image_rows
    local_cols = query_weight.shape[1]
    own_width = query_weight.shape[0]
    half_cols = local_cols // 2
    shape = jax.ShapeDtypeStruct

    def tensor_swap(block, bit):
        return lax.ppermute(block, "tensor", [(t, t ^ bit) for t in range(n_tensor)])

    positions = dp_at * tok_rows + lax.iota(jnp.int32, tok_rows)
    live_rows = positions[None, :] < text_lengths[:, None]
    grad_live = jnp.where(live_rows[..., None], out_grad, jnp.zeros_like(out_grad))
    text_flat = text_states.reshape(rows, width)
    live_flat = grad_live.reshape(rows, width)
    image_flat = image_states.reshape(image_rows, width)

    gate = lax.optimization_barrier

    relayed = line.n_z == 4
    wq_moved = line.first(query_weight)
    image_cols = lax.all_to_all(image_flat, "dp", split_axis=1, concat_axis=0, tiled=True)
    wo_keep = lax.dynamic_slice_in_dim(out_weight, x * half_cols, half_cols, 0)
    wo_send = lax.dynamic_slice_in_dim(out_weight, (1 - x) * half_cols, half_cols, 0)
    wo_pair = jnp.concatenate([wo_keep, line.swap(wo_send)], axis=1)
    quarter_cols = width // 4
    live_part = lax.dynamic_slice_in_dim(live_flat, quarter * quarter_cols, quarter_cols, 1)
    live_here = line.swap(live_part)
    image_cols, wo_pair, live_here, query_weight, *wq_moved = gate(
        (image_cols, wo_pair, live_here, query_weight, *wq_moved)
    )

    n_moved = len(wq_moved)
    planes = [(0, 1, 2), (1, 2, 3)] if relayed else [None] * n_moved
    wq_two = line.second(wq_moved)
    wo_moved = line.first(wo_pair)
    above, wq_other = gate((wq_moved[0], line.swap(query_weight)))
    wq_others = [wq_other, line.swap(above, planes[0])]
    part_kv = jnp.concatenate(
        [matmul(image_cols, key_weight), matmul(image_cols, value_weight)], axis=1
    )
    part_kv = part_kv.reshape(n_dp, image_rows, 2 * local_cols)
    kv_own = jnp.sum(lax.all_to_all(part_kv, "dp", split_axis=0, concat_axis=0), axis=0)
    kv_own, live_here, *staged = gate(
        (kv_own.astype(BF16), live_here, *wq_others, *wq_moved, *wq_two, *wo_moved)
    )
    wq_others, staged = staged[:2], staged[2:]
    wq_moved, wq_two, wo_moved = staged[:n_moved], staged[n_moved:-n_moved], staged[-n_moved:]

    def everywhere(values):
        copies = jnp.broadcast_to(values[None], (n_dp, *values.shape))
        return lax.all_to_all(copies, "dp", split_axis=0, concat_axis=0)

    wq_last = line.third(wq_two)
    wo_two = line.second(wo_moved)
    wq_others += [line.swap(block, at) for block, at in zip(wq_moved[1:], planes[1:])]
    wq_others += [line.swap(block) for block in wq_last[:1]]
    kv_all = everywhere(kv_own).reshape(images, 2 * local_cols)
    early = range(2 if relayed else 1 + n_moved)
    query_part = call(
        functools.partial(query_kernel, line, relayed, early),
        place,
        (text_flat, query_weight, *wq_moved[: len(early) - 1], *wq_others[: len(early)]),
        [shape((rows, local_cols), F32)],
        (),
        rows * width * local_cols,
    )
    kv_all, query_part, live_here, wo_pair, live_flat, *staged = gate(
        (kv_all, query_part, live_here, wo_pair, live_flat, *wo_two, *wq_last, *wq_others)
    )
    wo_two, staged = staged[: len(wo_two)], staged[len(wo_two) :]
    wq_last, wq_others = staged[: len(wq_last)], staged[len(wq_last) :]

    wo_last = line.third(wo_two)
    quarter_rows = rows // 4
    live_rows = lax.dynamic_slice_in_dim(live_flat, quarter * quarter_rows, quarter_rows, 0)
    live_mine = lax.all_to_all(
        live_rows.reshape(quarter_rows, n_dp, own_width), "dp", split_axis=1, concat_axis=0
    )
    live_mine = live_mine.reshape(n_dp, quarter_rows, own_width)
    by_y = tensor_swap(live_here, 2)
    live_pieces = [live_here, tensor_swap(live_here, 1), by_y, tensor_swap(by_y, 1)]
    wq_others += [line.swap(block, (0, 3)) for block in wq_last[1:]]
    half = shape((rows, half_cols), F32)
    wo_early = [wo_pair, *wo_moved]
    grad_parts = call(
        functools.partial(grad_kernel, line, range(len(wo_early)), 0),
        place,
        (live_flat, *live_pieces, *wo_early),
        [half] * 2,
        (),
        rows * width * local_cols,
    )

    arrivals = [query_weight, *wq_moved, *wq_last]
    late = range(len(early), len(arrivals))

    wo_late = range(len(wo_early), len(wo_early) + len(wo_last))
    grad_keep, grad_send = call(
        functools.partial(grad_kernel, line, wo_late, 2),
        place,
        (live_flat, *live_pieces, *grad_parts, *wo_last),
        [shape((rows, half_cols), BF16)] * 2,
        [pltpu.VMEM((rows, half_cols), F32)] * 2,
        rows * width * local_cols,
    )
    text_flat, grad_keep, grad_send = gate((text_flat, grad_keep, grad_send))
    grad_come = line.swap(grad_send)
    queries, attended = call(
        functools.partial(forward_kernel, line, relayed, late, image_own),
        place,
        (text_flat, kv_all, query_part, *arrivals[len(early) :], *wq_others[len(early) :]),
        [shape((rows, local_cols), BF16)] * 2,
        [pltpu.VMEM((rows, local_cols), F32)],
        rows * width * local_cols,
    )
    wq_blocks = [*arrivals, *wq_others]

    att_next = [line.shift(attended, m) for m in (1, line.n_z - 1)]
    attended, grad_come = gate((attended, grad_come))
    att_swapped = line.swap(attended)

    query_grad, kv_part = call(
        functools.partial(backward_kernel, image_own),
        place,
        (queries, kv_all, grad_keep, grad_come),
        [shape((rows, local_cols), BF16), shape((images, 2 * local_cols), F32)],
        (),
        10 * images * rows * local_cols,
    )
    chunk = n_dp // n_tensor
    term = call(
        functools.partial(term_kernel, line, relayed),
        place,
        (query_grad, *wq_blocks),
        [shape((n_tensor, chunk, rows, own_width), BF16)],
        (),
        2 * rows * width * local_cols,
    )
    kv_part, term, live_y, attended, att_swapped, *att_next = gate(
        (kv_part, term, tensor_swap(live_mine, 2), attended, att_swapped, *att_next)
    )

    kv_part = kv_part.reshape(n_dp, image_rows, 2 * local_cols)
    kv_grad = jnp.sum(lax.all_to_all(kv_part, "dp", split_axis=0, concat_axis=0), axis=0)
    text_parts = [tensor_swap(term[k], k) for k in range(n_tensor - 1, 0, -1)]
    live_pair = jnp.stack([live_mine, live_y])
    live_core = tensor_swap(live_pair, 1)
    kv_grad, live_core, text_parts[-1], attended, *att_next = gate(
        (kv_grad.astype(BF16), live_core, text_parts[-1], attended, *att_next)
    )
    kv_grad_all = everywhere(kv_grad).reshape(images, 2 * local_cols)
    att_far = [line.shift(attended, m) for m in range(2, line.n_z - 1)]
    att_other_next = [line.swap(block) for block in att_next]
    att_other_far = [line.swap(block) for block in att_far]
    text_grad = call(
        sum_kernel, place, (term, *text_parts), [shape((rows, width // n_tensor), BF16)]
    )
    kv_grad_all, text_grad, *att_other_next = gate((kv_grad_all, text_grad, *att_other_next))

    image_term = matmul(kv_grad_all[:, :local_cols], key_weight, BACK)
    image_term = image_term + matmul(kv_grad_all[:, local_cols:], value_weight, BACK)
    image_grad, *att_other_far = to_owner(line, image_term.astype(BF16), *att_other_far)
    image_grad = image_grad.reshape(samples, image_own, width // n_tensor)
    text_grad = text_grad.reshape(samples, tok_rows, width // n_tensor)

    att_blocks = [attended, att_next[0], *att_far, att_next[1]]
    att_others = [att_swapped, att_other_next[0], *att_other_far, att_other_next[1]]
    weight_grad = call(
        functools.partial(weight_grad_kernel, line),
        place,
        (live_pair, live_core, *att_blocks, *att_others),
        [shape((local_cols, own_width), BF16)],
        [pltpu.VMEM((local_cols, own_width), F32)],
        2 * n_dp * rows * local_cols * own_width,
    )
    return text_grad, image_grad, weight_grad


def solution(mesh):
    return jax.shard_map(
        shards,
        mesh=mesh,
        in_specs=(
            P(None, "dp", None),
            P(None, "dp", None),
            P(None, "dp", None),
            P(),
            P("dp", "tensor"),
            P("dp", "tensor"),
            P("dp", "tensor"),
            P("tensor", "dp"),
        ),
        out_specs=(P(None, "dp", "tensor"), P(None, "dp", "tensor"), P("tensor", "dp")),
        check_vma=False,
    )
```
